32 devices in a mesh: lon: 8 (over z, x), lat: 4 (over y, core).
Axes of the slice: x: 2, y: 2, z: 4, core: 2. Of those that a mesh axis runs over, the one named last changes fastest.
Arguments:
- state_field: float32 [2, 137, 128, 1024], P(None, None, 'lat', 'lon'), may hold values from -6 to 6
- jacobian: bfloat16 [4, 512, 2, 137, 128], P('lat', 'lon'), may hold values from -0.375 to 0.375
- observed: bfloat16 [4, 512, 128], P('lat', 'lon'), may hold values from -6 to 6
- inverse_var: bfloat16 [4, 512, 128], P('lat', 'lon'), may hold values from 0.25 to 4
- valid_count: int32 [4, 512], P('lat', 'lon'), may hold values from 32 to 128
- destination: int32 [4, 512, 1], P('lat', 'lon'), may hold values from 0 to 7; in each aligned block of 64 rows (0 to 63, 64 to 127, ..., all dimensions but the last counted through in order) at most 16 rows name the same one
- column: int32 [4, 512], P('lat', 'lon'), may hold values from 0 to 4095
- vertical: bfloat16 [2, 137, 137], replicated, may hold values from -0.5 to 0.5
- lon_taps: float32 [2, 137, 9], replicated, may hold values from 0.05 to 0.3
- lat_taps: float32 [2, 137, 9], replicated, may hold values from 0.05 to 0.3
Outputs:
- gradient: float32 [2, 137, 128, 1024], P(None, None, 'lat', 'lon')
The draws below stay inside these ranges and needn't reach their ends.
Inputs may be any that keep to these rules, and one draw needn't show every extreme that they name: `destination`: among the 64 records of one device no longitude tile is named more than 16 times, a bound that some block reaches.
All inputs are finite; a program needn't handle non-finite values.
Results may differ from the reference program's by a relative error of at most 0.0045.
Values may be sent and summed in bfloat16 or wider, within the bound.
No kernel may reach another device: no remote copies, remote signals or barrier semaphores. Data moves between devices by JAX's collectives and lax.ppermute only.
A program may use at most 128 MiB of HBM per device.

```python
import math
import jax
import jax.numpy as jnp
import numpy as np
from jax import lax

VARS = 2
LEVELS = 137
CH = 128
TAPS = 9
CLON = 128
CLAT = 32
REC_DEV = 64
BANDS = 4
NLAT = 128
NLON = 1024
RECS = 512
CAP = 16
N_LON = 8


def touch_ends(drawn, own_key, least, high):
    index_at = [jax.random.randint(jax.random.fold_in(own_key, axis), (), 0, length) for axis, length in enumerate(drawn.shape)]
    main_axis = drawn.shape.index(max(drawn.shape))
    neighbour = index_at[:main_axis] + [(index_at[main_axis] + 1) % drawn.shape[main_axis]] + index_at[main_axis + 1:]
    return drawn.at[tuple(index_at)].set(least).at[tuple(neighbour)].set(high)


def steps_of(key, extent, split, low, largest):
    factor_of, own = 1.0, jax.random.fold_in(key, 6)
    for dim, shards_of in split:
        steps = jnp.exp(jax.random.uniform(jax.random.fold_in(own, dim), (shards_of,), jnp.float32, low / len(split), largest / len(split)))
        factor_of = factor_of * jnp.repeat(steps, extent[dim] // shards_of).reshape([-1 if axis == dim else 1 for axis in range(len(extent))])
    return factor_of


def shared_out(rng, own, number, rows, number_of, top, limit, lean):
    order = jax.random.permutation(rng, number_of)
    crowded, ordinary = portions_of(number_of, rows * top, limit, lean, True), portions_of(number_of, rows * top, limit, lean, False)
    places = jnp.arange(number_of)

    def named(tallies, turn):
        used = int((tallies > 0).sum())
        fixed = max(1, used // 4)
        moved = fixed + (places - fixed + turn * (used - fixed)) % max(1, number_of - fixed)
        return jnp.zeros((number_of,), jnp.int32).at[order[jnp.where(places < fixed, places, moved)]].set(jnp.asarray(tallies, jnp.int32))

    tallies = jnp.where(number % 4 == 0, named(crowded, number // 4), named(ordinary, number - number // 4 - 1))
    mixed = jax.random.permutation(jax.random.fold_in(own, 3), number_of)
    giver, receiver = mixed[0:number_of // 2 * 2:2], mixed[1:number_of // 2 * 2:2]
    room = jnp.minimum(tallies[giver] - 1, limit - tallies[receiver]) // 2
    room = jnp.where((giver == order[0]) | (receiver == order[0]) | (tallies[receiver] == 0), 0, jnp.maximum(room, 0))
    moved = jax.random.randint(jax.random.fold_in(own, 4), (number_of // 2,), 0, 1 << 20) % (room + 1)
    tallies = tallies.at[giver].add(-moved).at[receiver].add(moved)
    labels = jnp.searchsorted(jnp.cumsum(tallies), jnp.arange(rows * top), side="right").astype(jnp.int32)
    grid = labels.reshape(top, rows).T
    grid = grid[jax.random.permutation(jax.random.fold_in(own, 1), rows)]
    turn = jax.random.randint(jax.random.fold_in(own, 2), (rows, 1), 0, top)
    return jnp.take_along_axis(grid, (jnp.arange(top)[None, :] + turn) % top, axis=1)


def portions_of(count, total, bound, lean, full):
    loads = [(1 << 20) // math.isqrt(standing ** lean) + 1 for standing in range(1, count + 1)]
    largest = bound if full else min(bound, max(-(-total // count), total * loads[0] // sum(loads)))
    least = 1 if total - largest >= count - 1 else 0
    counts, spare = [largest] + [least] * (count - 1), total - largest - least * (count - 1)
    while spare > 0:
        candidates = [i for i in range(1, count) if counts[i] < largest] or [i for i in range(1, count) if counts[i] < bound]
        pool, budget = sum([loads[i] for i in candidates]), spare
        for i in candidates:
            addition = min(bound - counts[i], max(1, budget * loads[i] // pool), spare)
            counts[i] = counts[i] + addition
            spare = spare - addition
    return np.array(counts)


def normal_values(key, extent, deviation, limit, shards=(), kind=jnp.bfloat16):
    values = jax.random.normal(key, extent, jnp.float32) * deviation
    if len(shards) > 0:
        values = steps_of(key, extent, shards, -0.22, 0.18) * values
    return jnp.clip(values, min=-limit, max=limit).astype(kind)


def setup_inputs(seed: int = 0) -> dict:
    splits = jax.random.split(jax.random.key(seed), 11)
    state_field = normal_values(splits[0], (VARS, LEVELS, NLAT, NLON), 1.0, 6.0, ((2, 4), (3, 8)), jnp.float32)
    jacobian = normal_values(splits[1], (BANDS, RECS, VARS, LEVELS, CH), (VARS * LEVELS) ** -0.5, 0.375, ((0, 4), (1, 8)))
    observed = normal_values(splits[2], (BANDS, RECS, CH), 1.0, 6.0, ((0, 4), (1, 8)))
    inverse_var = jnp.clip(jnp.exp(math.log(4.0) - 2.7725887 * jax.random.uniform(splits[3], (BANDS, RECS, CH), jnp.float32) ** steps_of(splits[3], (BANDS, RECS, CH), ((0, 4), (1, 8)), -0.2, 0.2)), 0.25, 4.0).astype(jnp.bfloat16)
    valid_count = touch_ends(jax.random.randint(splits[4], (BANDS, RECS), CH // 4, CH + 1), jax.random.fold_in(splits[4], 1), CH // 4, CH).astype(jnp.int32)
    destination_keys = jax.random.split(jax.random.fold_in(splits[5], 1), BANDS * RECS // REC_DEV)
    destination_turns = jax.random.permutation(jax.random.fold_in(splits[5], 3), BANDS * RECS // REC_DEV)
    destination = jax.vmap(lambda own, number: shared_out(jax.random.fold_in(splits[5], 2), own, number, REC_DEV, N_LON, 1, CAP, 2))(destination_keys, destination_turns).reshape((BANDS, RECS, 1))
    column = touch_ends(jax.random.randint(splits[6], (BANDS, RECS), 0, CLAT * CLON), jax.random.fold_in(splits[6], 1), 0, (CLAT * CLON) - 1).astype(jnp.int32)
    vertical = normal_values(splits[7], (VARS, LEVELS, LEVELS), LEVELS ** -0.5, 0.5)
    lon_taps = jnp.clip(jax.random.uniform(splits[8], (VARS, LEVELS, TAPS), jnp.float32, 0.05, 0.3), 0.05, 0.3)
    lat_taps = jnp.clip(jax.random.uniform(splits[9], (VARS, LEVELS, TAPS), jnp.float32, 0.05, 0.3), 0.05, 0.3)
    return dict(state_field=state_field, jacobian=jacobian, observed=observed, inverse_var=inverse_var, valid_count=valid_count, destination=destination, column=column, vertical=vertical, lon_taps=lon_taps, lat_taps=lat_taps)


def reference(state_field, jacobian, observed, inverse_var, valid_count, destination, column, vertical, lon_taps, lat_taps):
    features = VARS * LEVELS
    highest = lax.Precision.HIGHEST
    rounded = lax.optimization_barrier(state_field.astype(jnp.bfloat16)).astype(jnp.float32)
    rounded = rounded.reshape(features, NLAT * NLON)
    band_start = (jnp.arange(BANDS, dtype=jnp.int32) * CLAT)[:, None]
    lat_index = band_start + column // CLON
    lon_index = destination[..., 0] * CLON + column % CLON
    flat_index = (lat_index * NLON + lon_index).astype(jnp.int32)
    alive_mask = jnp.arange(CH, dtype=jnp.int32)[None, None, :] < valid_count[..., None]

    def one_band(pieces):
        jac_band, obs_band, inv_band, alive_band, index_band = pieces
        jac_full = jac_band.astype(jnp.float32).reshape(RECS, features, CH)
        state_cols = jnp.take(rounded, index_band, axis=1).T
        model = jnp.einsum('rfc,rf->rc', jac_full, state_cols, precision=highest)
        misfit = jnp.where(alive_band, inv_band.astype(jnp.float32), jnp.float32(0.0)) * (model - obs_band.astype(jnp.float32))
        scaled = lax.optimization_barrier(misfit.astype(jnp.bfloat16)).astype(jnp.float32)
        return jnp.einsum('rfc,rc->rf', jac_full, scaled, precision=highest)

    products = lax.map(one_band, (jacobian, observed, inverse_var, alive_mask, flat_index))
    impact = jnp.zeros((features, NLAT * NLON), jnp.float32)
    impact = impact.at[:, flat_index.reshape(-1)].add(products.reshape(-1, features).T)
    impact = impact.reshape(VARS, LEVELS, NLAT, NLON)
    reach = TAPS // 2

    def one_variable(pieces):
        impact_var, vert_var, lon_var, lat_var = pieces
        impact_low = lax.optimization_barrier(impact_var.astype(jnp.bfloat16)).astype(jnp.float32)
        mixed = jnp.einsum('lm,lij->mij', vert_var.astype(jnp.float32), impact_low, precision=highest)
        along = jnp.zeros_like(mixed)
        for offset in range(TAPS):
            along = along + lon_var[:, offset][:, None, None] * jnp.roll(mixed, reach - offset, axis=2)
        padded = jnp.pad(along, ((0, 0), (reach, reach), (0, 0)))
        result = jnp.zeros_like(mixed)
        for offset in range(TAPS):
            result = result + lat_var[:, offset][:, None, None] * padded[:, offset:offset + NLAT, :]
        return result

    return lax.map(one_variable, (impact, vertical, lon_taps, lat_taps))
```

```python
import functools

import jax
import jax.numpy as jnp
from jax import lax
from jax.experimental import pallas as pl
from jax.experimental.pallas import tpu as pltpu
from jax.sharding import PartitionSpec as P

LANES = 128
F32 = jnp.float32
BF16 = jnp.bfloat16
VMEM_LIMIT = 56 * 1024 * 1024


def lane_iota(shape):
    return lax.broadcasted_iota(jnp.int32, shape, 1)


def row_iota(shape):
    return lax.broadcasted_iota(jnp.int32, shape, 0)


def earlier_rows(size):
    return (lane_iota((size, size)) < row_iota((size, size))).astype(F32).astype(BF16)


def split_codes(codes_ref, records, points):
    flipped = jnp.transpose(codes_ref[...].astype(F32))[:records].astype(jnp.int32)
    tile = lax.div(flipped, points)
    return tile, flipped - tile * points


def gather_kernel(records, capacity, rows, features, codes_ref, state_ref, out_ref, held, pick, row_mask):
    step = pl.program_id(0)
    count = codes_ref.shape[0]
    slots = out_ref.shape[0]
    planes = state_ref.shape[0] // rows

    @pl.when(step == 0)
    def _():
        me = lax.axis_index("lon")
        tile, column = split_codes(codes_ref, records, rows * LANES)
        mine = (tile == me).astype(F32)
        rank = jnp.dot(earlier_rows(records), mine.astype(BF16), preferred_element_type=F32)
        slot = lane_iota(mine.shape) * capacity + rank.astype(jnp.int32)
        slot = jnp.where(tile == me, slot, -1)
        row_of = jnp.zeros((1, slots), F32)
        lon_of = jnp.zeros((1, slots), F32)
        for d in range(count):
            hit = slot[:, d : d + 1] == lane_iota((records, slots))
            row = lax.div(column[:, d : d + 1], LANES)
            lon = column[:, d : d + 1] - row * LANES
            row_of += jnp.sum(jnp.where(hit, (row + 1).astype(F32), 0.0), axis=0, keepdims=True)
            lon_of += jnp.sum(jnp.where(hit, lon.astype(F32), 0.0), axis=0, keepdims=True)
        pick[...] = (row_iota((LANES, slots)) == lon_of.astype(jnp.int32)).astype(F32).astype(BF16)
        row_mask[...] = (row_iota((rows, slots)) == row_of.astype(jnp.int32) - 1).astype(F32)

    found = jnp.dot(state_ref[...].astype(BF16), pick[...], preferred_element_type=F32)
    found = found.reshape(planes, rows, slots) * row_mask[...][None]
    held[pl.ds(pl.multiple_of(step * planes, planes), planes), :] = jnp.sum(found, axis=1)

    @pl.when(step == pl.num_programs(0) - 1)
    def _():
        for t in range(out_ref.shape[1] // LANES):
            out_ref[:, t * LANES : (t + 1) * LANES] = jnp.transpose(
                held[t * LANES : (t + 1) * LANES, :]
            ).astype(BF16)


def gather_state(codes, state, records, capacity):
    variables, levels, rows, cols = state.shape
    features = variables * levels
    wide = pl.cdiv(features, LANES) * LANES
    slots = codes.shape[0] * capacity
    planes = 32
    steps = pl.cdiv(features, planes)
    return pl.pallas_call(
        functools.partial(gather_kernel, records, capacity, rows, features),
        grid=(steps,),
        in_specs=[
            pl.BlockSpec(codes.shape, lambda s: (0, 0)),
            pl.BlockSpec((planes * rows, cols), lambda s: (s, 0)),
        ],
        out_specs=pl.BlockSpec((slots, wide), lambda s: (0, 0)),
        out_shape=jax.ShapeDtypeStruct((slots, wide), BF16),
        scratch_shapes=[
            pltpu.VMEM((wide, slots), F32),
            pltpu.VMEM((cols, slots), BF16),
            pltpu.VMEM((rows, slots), F32),
        ],
        compiler_params=pltpu.CompilerParams(vmem_limit_bytes=VMEM_LIMIT),
        cost_estimate=pl.CostEstimate(
            flops=2 * features * rows * cols * slots, bytes_accessed=features * rows * cols * 4, transcendentals=0
        ),
        name="gather_state",
    )(codes, state.reshape(features * rows, cols))


def departure_kernel(capacity, dest_ref, valid_ref, states_ref, obs_ref, inv_ref, jac_ref, out_ref, state, scaled_rows, total):
    step = pl.program_id(0)
    group, variables, levels, channels = jac_ref.shape
    records = dest_ref.shape[0]
    slots = states_ref.shape[0]

    @pl.when(step == 0)
    def _():
        dest = dest_ref[...]
        named = (dest == lane_iota((records, LANES))).astype(F32)
        before = jnp.dot(earlier_rows(records), named.astype(BF16), preferred_element_type=F32)
        rank = jnp.sum(before * named, axis=1, keepdims=True).astype(jnp.int32)
        chosen = (dest * capacity + rank == lane_iota((records, slots))).astype(F32).astype(BF16)
        columns = jnp.dot(chosen, states_ref[...], preferred_element_type=F32)
        for v in range(variables):
            state[v] = columns[:, v * levels : (v + 1) * levels].astype(BF16)
        scaled_rows[...] = jnp.zeros_like(scaled_rows)
        total[...] = jnp.zeros_like(total)

    first = pl.multiple_of(step * group, group)
    mine = [state[v, pl.ds(first, group), :] for v in range(variables)]
    model = jnp.zeros((group, channels), F32)
    for r in range(group):
        one = jnp.dot(mine[0], jac_ref[r, 0], preferred_element_type=F32)
        for v in range(1, variables):
            one += jnp.dot(mine[v], jac_ref[r, v], preferred_element_type=F32)
        model = jnp.where(row_iota(model.shape) == r, one, model)
    alive = lane_iota(model.shape) < valid_ref[pl.ds(first, group), :]
    weight = jnp.where(alive, inv_ref[pl.ds(first, group), :].astype(F32), 0.0)
    scaled = (weight * (model - obs_ref[pl.ds(first, group), :].astype(F32))).astype(BF16)
    for v in range(variables):
        scaled_rows[pl.ds(pl.multiple_of(v * records + first, group), group), :] = scaled
    against = scaled_rows[...]
    sums = total[...]
    lane = lane_iota(sums.shape)
    for r in range(group):
        for v in range(variables):
            one = lax.dot_general(
                jac_ref[r, v], against, (((1,), (1,)), ((), ())), preferred_element_type=F32
            )
            sums = jnp.where(lane == v * records + first + r, one, sums)
    total[...] = sums

    @pl.when(step == pl.num_programs(0) - 1)
    def _():
        low = sums.astype(BF16)
        for t in range(out_ref.shape[0]):
            out_ref[t] = low


def departures(dest, valid, states, obs, inv, jac, capacity, devices):
    records, variables, levels, channels = jac.shape
    group = 16

    def whole(shape):
        return pl.BlockSpec(shape, lambda s: (0,) * len(shape))

    return pl.pallas_call(
        functools.partial(departure_kernel, capacity),
        grid=(records // group,),
        in_specs=[
            whole(dest.shape),
            whole(valid.shape),
            whole(states.shape),
            whole(obs.shape),
            whole(inv.shape),
            pl.BlockSpec((group, variables, levels, channels), lambda s: (s, 0, 0, 0)),
        ],
        out_specs=whole((devices, levels, variables * records)),
        out_shape=jax.ShapeDtypeStruct((devices, levels, variables * records), BF16),
        scratch_shapes=[
            pltpu.VMEM((variables, records, levels), BF16),
            pltpu.VMEM((variables * records, channels), BF16),
            pltpu.VMEM((levels, variables * records), F32),
        ],
        compiler_params=pltpu.CompilerParams(vmem_limit_bytes=VMEM_LIMIT),
        cost_estimate=pl.CostEstimate(
            flops=4 * jac.size, bytes_accessed=jac.size * 2, transcendentals=0
        ),
        name="departures",
    )(dest, valid, states, obs, inv, jac)


def place_records(records, rows, reach, codes_ref, main, halo, wrap):
    me = lax.axis_index("lon")
    count = codes_ref.shape[0]
    right, left = lax.rem(me + 1, count), lax.rem(me + count - 1, count)
    tile, column = split_codes(codes_ref, records, rows * LANES)
    row = lax.div(column, LANES)
    lon = column - row * LANES
    far = LANES - reach
    edge = row * (2 * reach) + jnp.where(lon < reach, lon, lon - far + reach)
    near_right, near_left = lon < reach, lon >= far
    on_main = jnp.where(tile == me, column, -1)
    on_halo = jnp.where(((tile == right) & near_right) | ((tile == left) & near_left), edge, -1)
    on_wrap = jnp.where((tile == me) & (near_right | near_left), edge, -1)
    for where_to, what in ((main, on_main), (halo, on_halo), (wrap, on_wrap)):
        if where_to is None:
            continue
        for d in range(count):
            where_to[d * records : (d + 1) * records, :] = jnp.broadcast_to(
                what[:, d : d + 1], (records, LANES)
            )


def order_products(records, products_ref, terms):
    count, levels, width = products_ref.shape
    tall = terms.shape[0] * records // width
    terms[...] = jnp.zeros_like(terms)
    lane = lane_iota((levels, width))
    for pair in range(count // 2):
        one = products_ref[2 * pair].astype(F32)
        two = products_ref[2 * pair + 1].astype(F32)
        first = jnp.where(lane < records, one, pltpu.roll(two, records, 1))
        second = jnp.where(lane < records, pltpu.roll(one, records, 1), two)
        terms[0:levels, pair * width : (pair + 1) * width] = first.astype(BF16)
        terms[tall : tall + levels, pair * width : (pair + 1) * width] = second.astype(BF16)


def mix_columns(levels, place, base, width, terms, vertical_ref, mixed, at):
    tall = vertical_ref.shape[1]
    spots = [place[...] == lane_iota(place.shape) + (base + n * LANES) for n in range(width // LANES)]
    onehot = jnp.concatenate([s.astype(F32).astype(BF16) for s in spots], axis=1)
    impact = jnp.dot(terms[...], onehot, preferred_element_type=F32).astype(BF16)
    for v in range(vertical_ref.shape[0]):
        mixed[v * levels : v * levels + tall, at : at + width] = jnp.dot(
            vertical_ref[v], impact[v * tall : (v + 1) * tall], preferred_element_type=F32
        )


def edge_fix(reach, outer, inner, taps):
    gap = outer - inner
    lane = lane_iota(gap.shape) % (2 * reach)
    width = gap.shape[1]
    fix = jnp.zeros_like(gap)
    for s in range(reach):
        right = pltpu.roll(gap, s, 1) if s else gap
        left = pltpu.roll(gap, width - s, 1) if s else gap
        on_right = (lane >= s) & (lane < reach)
        on_left = (lane >= reach) & (lane < 2 * reach - s)
        fix += jnp.where(on_right, taps[2 * reach - s] * right, 0.0)
        fix += jnp.where(on_left, taps[s] * left, 0.0)
    return fix


def lon_row(reach, row, x, fix, taps, ends):
    before, after = pltpu.roll(x, 1, 1), pltpu.roll(x, LANES - 1, 1)
    parts = [taps[3 * a] * before + taps[3 * a + 1] * x + taps[3 * a + 2] * after for a in range(3)]
    total = pltpu.roll(parts[0], 3, 1) + parts[1] + pltpu.roll(parts[2], LANES - 3, 1)
    span = 2 * reach
    block, spot = divmod(row * span, LANES)
    shift = (LANES - reach - spot) % LANES
    piece = fix[:, block * LANES : (block + 1) * LANES]
    piece = pltpu.roll(piece, shift, 1) if shift else piece
    return total + jnp.where(ends, piece, 0.0)


def spread_taps(block, height):
    return [jnp.broadcast_to(block[:, k : k + 1], (height, LANES)) for k in range(block.shape[1])]


def edges_kernel(records, rows, reach, levels, codes_ref, products_ref, vertical_ref, lon_ref, out_ref, main, halo, wrap, terms, mixed):
    place_records(records, rows, reach, codes_ref, main, halo, wrap)
    order_products(records, products_ref, terms)
    span = 2 * reach
    half = reach * LANES
    mix_columns(levels, main, 0, half, terms, vertical_ref, mixed, 0)
    mix_columns(levels, main, (rows - reach) * LANES, half, terms, vertical_ref, mixed, half)
    ends = rows * span
    mix_columns(levels, halo, 0, ends, terms, vertical_ref, mixed, 2 * half)
    mix_columns(levels, wrap, 0, ends, terms, vertical_ref, mixed, 2 * half + ends)
    height = 16
    lane = lane_iota((height, LANES))
    at_ends = (lane < reach) | (lane >= LANES - reach)

    @pl.loop(0, out_ref.shape[2] // height)
    def _(g):
        here = pl.ds(pl.multiple_of(g * height, height), height)
        taps = spread_taps(lon_ref[here, :], height)
        wide_taps = [jnp.concatenate([t] * (ends // LANES), axis=1) for t in taps]
        fix = edge_fix(
            reach, mixed[here, 2 * half : 2 * half + ends], mixed[here, 2 * half + ends :], wide_taps
        )
        for side in range(2):
            for n in range(reach):
                row = n if side == 0 else rows - reach + n
                at = (side * reach + n) * LANES
                out_ref[side, n, here, :] = lon_row(
                    reach, row, mixed[here, at : at + LANES], fix, taps, at_ends
                ).astype(BF16)


def mix_kernel(records, rows, reach, levels, codes_ref, products_ref, vertical_ref, out_ref, main, halo, wrap, terms):
    place_records(records, rows, reach, codes_ref, main, halo, wrap)
    order_products(records, products_ref, terms)
    points = rows * LANES
    ends = rows * 2 * reach
    width = 2 * LANES
    for at in range(0, points, width):
        mix_columns(levels, main, at, width, terms, vertical_ref, out_ref, at)
    mix_columns(levels, halo, 0, ends, terms, vertical_ref, out_ref, points)
    mix_columns(levels, wrap, 0, ends, terms, vertical_ref, out_ref, points + ends)


def filter_kernel(rows, reach, features, mixed_ref, lon_ref, lat_ref, above_ref, below_ref, out_ref, outer):
    height = 8
    block = mixed_ref.shape[0]
    points = rows * LANES
    ends = rows * 2 * reach
    outer[0] = above_ref[...].astype(F32)
    outer[1] = below_ref[...].astype(F32)
    lane = lane_iota((height, LANES))
    at_ends = (lane < reach) | (lane >= LANES - reach)
    left = features - pl.program_id(0) * block
    groups = jnp.minimum(block // height, lax.div(left + height - 1, height))

    def one_group(g, carry):
        first = pl.multiple_of(g * height, height)
        here = pl.ds(first, height)
        lon = spread_taps(lon_ref[here, :], height)
        lat = spread_taps(lat_ref[here, :], height)
        wide = [jnp.concatenate([t] * (ends // LANES), axis=1) for t in lon]
        fix = edge_fix(reach, mixed_ref[here, points : points + ends], mixed_ref[here, points + ends :], wide)
        pending = {}
        for row in range(-reach, rows + reach):
            if row < 0:
                along = outer[0, row + reach, here, :]
            elif row >= rows:
                along = outer[1, row - rows, here, :]
            else:
                along = lon_row(reach, row, mixed_ref[here, row * LANES : (row + 1) * LANES], fix, lon, at_ends)
            for k in range(2 * reach + 1):
                target = row - k + reach
                if 0 <= target < rows:
                    term = lat[k] * along
                    pending[target] = pending[target] + term if target in pending else term
            done = row - reach
            if done >= 0:
                out_ref[pl.ds(first * rows + done, height, stride=rows), :] = pending.pop(done)
        return carry

    lax.fori_loop(0, groups, one_group, 0)


def solution(mesh):
    lon_devices, lat_devices = mesh.shape["lon"], mesh.shape["lat"]

    def body(state_field, jacobian, observed, inverse_var, valid_count, destination, column, vertical, lon_taps, lat_taps):
        variables, levels, rows, cols = state_field.shape
        features = variables * levels
        records, channels = jacobian.shape[1], jacobian.shape[-1]
        capacity = max(2, 2 * records // lon_devices)
        reach = lon_taps.shape[-1] // 2
        points = rows * cols
        span = records * lon_devices
        tall = pl.cdiv(levels, 16) * 16
        height = pl.cdiv((variables - 1) * levels + tall, 48) * 48
        ends = rows * 2 * reach

        dest = destination.reshape(records, 1)
        codes = destination.reshape(1, records) * points + column.reshape(1, records)
        codes = jnp.broadcast_to(jnp.pad(codes, ((0, 0), (0, LANES - records))), (lon_devices, LANES))
        codes = lax.all_to_all(codes, "lon", split_axis=0, concat_axis=0, tiled=True)

        found = gather_state(codes, state_field, records, capacity)
        found = found.reshape(lon_devices, capacity, found.shape[-1])
        found = lax.all_to_all(found, "lon", split_axis=0, concat_axis=0, tiled=True)
        found = found.reshape(lon_devices * capacity, found.shape[-1])

        products = departures(
            dest,
            valid_count.reshape(records, 1),
            found,
            observed.reshape(records, channels),
            inverse_var.reshape(records, channels),
            jacobian.reshape(records, variables, levels, channels),
            capacity,
            lon_devices,
        )
        products = lax.all_to_all(products, "lon", split_axis=0, concat_axis=0, tiled=True)

        mixing = jnp.pad(jnp.swapaxes(vertical, 1, 2), ((0, 0), (0, tall - levels), (0, tall - levels)))
        lon_flat = jnp.pad(lon_taps.reshape(features, -1), ((0, height - features), (0, 0)))
        lat_flat = jnp.pad(lat_taps.reshape(features, -1), ((0, height - features), (0, 0)))

        params = pltpu.CompilerParams(vmem_limit_bytes=VMEM_LIMIT)
        placing = [
            pltpu.VMEM((span, LANES), jnp.int32),
            pltpu.VMEM((span, LANES), jnp.int32),
            pltpu.VMEM((span, LANES), jnp.int32),
            pltpu.VMEM((variables * tall, span), BF16),
        ]
        edges = pl.pallas_call(
            functools.partial(edges_kernel, records, rows, reach, levels),
            out_shape=jax.ShapeDtypeStruct((2, reach, height, cols), BF16),
            scratch_shapes=placing + [pltpu.VMEM((height, 2 * reach * cols + 2 * ends), F32)],
            compiler_params=params,
            name="edge_rows",
        )(codes, products, mixing, lon_flat)
        below = lax.ppermute(edges[0], "lat", [(i + 1, i) for i in range(lat_devices - 1)])
        above = lax.ppermute(edges[1], "lat", [(i, i + 1) for i in range(lat_devices - 1)])
        mixed = pl.pallas_call(
            functools.partial(mix_kernel, records, rows, reach, levels),
            out_shape=jax.ShapeDtypeStruct((height, points + 2 * ends), F32),
            scratch_shapes=placing,
            compiler_params=params,
            cost_estimate=pl.CostEstimate(
                flops=2 * features * span * points, bytes_accessed=height * points * 4, transcendentals=0
            ),
            name="mix_levels",
        )(codes, products, mixing)

        block = 48
        result = pl.pallas_call(
            functools.partial(filter_kernel, rows, reach, features),
            grid=(pl.cdiv(features, block),),
            in_specs=[
                pl.BlockSpec((block, mixed.shape[1]), lambda s: (s, 0)),
                pl.BlockSpec((block, lon_flat.shape[1]), lambda s: (s, 0)),
                pl.BlockSpec((block, lat_flat.shape[1]), lambda s: (s, 0)),
                pl.BlockSpec((reach, block, cols), lambda s: (0, s, 0)),
                pl.BlockSpec((reach, block, cols), lambda s: (0, s, 0)),
            ],
            out_specs=pl.BlockSpec((block * rows, cols), lambda s: (s, 0)),
            out_shape=jax.ShapeDtypeStruct((features * rows, cols), F32),
            scratch_shapes=[pltpu.VMEM((2, reach, block, cols), F32)],
            compiler_params=params,
            name="filters",
        )(mixed, lon_flat, lat_flat, above, below)
        return result.reshape(variables, levels, rows, cols)

    placed = (
        P(None, None, "lat", "lon"),
        P("lat", "lon", None, None, None),
        P("lat", "lon", None),
        P("lat", "lon", None),
        P("lat", "lon"),
        P("lat", "lon", None),
        P("lat", "lon"),
        P(),
        P(),
        P(),
    )
    return jax.shard_map(
        body, mesh=mesh, in_specs=placed, out_specs=P(None, None, "lat", "lon"), check_vma=False
    )
```

```python
import functools

import jax
import jax.numpy as jnp
from jax import lax
from jax.experimental import pallas as pl
from jax.experimental.pallas import tpu as pltpu
from jax.sharding import PartitionSpec as P

LANES = 128
F32 = jnp.float32
BF16 = jnp.bfloat16
VMEM_LIMIT = 56 * 1024 * 1024


def lane_iota(shape):
    return lax.broadcasted_iota(jnp.int32, shape, 1)


def row_iota(shape):
    return lax.broadcasted_iota(jnp.int32, shape, 0)


def earlier_rows(size):
    return (lane_iota((size, size)) < row_iota((size, size))).astype(F32).astype(BF16)


def split_codes(codes_ref, records, points):
    flipped = jnp.transpose(codes_ref[...].astype(F32))[:records].astype(jnp.int32)
    tile = lax.div(flipped, points)
    return tile, flipped - tile * points


def gather_kernel(records, capacity, rows, features, codes_ref, state_ref, out_ref, held, pick, row_mask):
    step = pl.program_id(0)
    count = codes_ref.shape[0]
    slots = out_ref.shape[0]
    planes = state_ref.shape[0] // rows

    @pl.when(step == 0)
    def _():
        me = lax.axis_index("lon")
        tile, column = split_codes(codes_ref, records, rows * LANES)
        mine = (tile == me).astype(F32)
        rank = jnp.dot(earlier_rows(records), mine.astype(BF16), preferred_element_type=F32)
        slot = lane_iota(mine.shape) * capacity + rank.astype(jnp.int32)
        slot = jnp.where(tile == me, slot, -1)
        row_of = jnp.zeros((1, slots), F32)
        lon_of = jnp.zeros((1, slots), F32)
        for d in range(count):
            hit = slot[:, d : d + 1] == lane_iota((records, slots))
            row = lax.div(column[:, d : d + 1], LANES)
            lon = column[:, d : d + 1] - row * LANES
            row_of += jnp.sum(jnp.where(hit, (row + 1).astype(F32), 0.0), axis=0, keepdims=True)
            lon_of += jnp.sum(jnp.where(hit, lon.astype(F32), 0.0), axis=0, keepdims=True)
        pick[...] = (row_iota((LANES, slots)) == lon_of.astype(jnp.int32)).astype(F32).astype(BF16)
        row_mask[...] = (row_iota((rows, slots)) == row_of.astype(jnp.int32) - 1).astype(F32)

    found = jnp.dot(state_ref[...].astype(BF16), pick[...], preferred_element_type=F32)
    found = found.reshape(planes, rows, slots) * row_mask[...][None]
    held[pl.ds(pl.multiple_of(step * planes, planes), planes), :] = jnp.sum(found, axis=1)

    @pl.when(step == pl.num_programs(0) - 1)
    def _():
        for t in range(out_ref.shape[1] // LANES):
            out_ref[:, t * LANES : (t + 1) * LANES] = jnp.transpose(
                held[t * LANES : (t + 1) * LANES, :]
            ).astype(BF16)


def gather_state(codes, state, records, capacity):
    variables, levels, rows, cols = state.shape
    features = variables * levels
    wide = pl.cdiv(features, LANES) * LANES
    slots = codes.shape[0] * capacity
    planes = 32
    steps = pl.cdiv(features, planes)
    return pl.pallas_call(
        functools.partial(gather_kernel, records, capacity, rows, features),
        grid=(steps,),
        in_specs=[
            pl.BlockSpec(codes.shape, lambda s: (0, 0)),
            pl.BlockSpec((planes * rows, cols), lambda s: (s, 0)),
        ],
        out_specs=pl.BlockSpec((slots, wide), lambda s: (0, 0)),
        out_shape=jax.ShapeDtypeStruct((slots, wide), BF16),
        scratch_shapes=[
            pltpu.VMEM((wide, slots), F32),
            pltpu.VMEM((cols, slots), BF16),
            pltpu.VMEM((rows, slots), F32),
        ],
        compiler_params=pltpu.CompilerParams(vmem_limit_bytes=VMEM_LIMIT),
        cost_estimate=pl.CostEstimate(
            flops=2 * features * rows * cols * slots, bytes_accessed=features * rows * cols * 4, transcendentals=0
        ),
        name="gather_state",
    )(codes, state.reshape(features * rows, cols))


def departure_kernel(capacity, dest_ref, valid_ref, states_ref, obs_ref, inv_ref, jac_ref, out_ref, state, scaled_rows, total):
    step = pl.program_id(0)
    group, variables, levels, channels = jac_ref.shape
    records = dest_ref.shape[0]
    slots = states_ref.shape[0]

    @pl.when(step == 0)
    def _():
        dest = dest_ref[...]
        named = (dest == lane_iota((records, LANES))).astype(F32)
        before = jnp.dot(earlier_rows(records), named.astype(BF16), preferred_element_type=F32)
        rank = jnp.sum(before * named, axis=1, keepdims=True).astype(jnp.int32)
        chosen = (dest * capacity + rank == lane_iota((records, slots))).astype(F32).astype(BF16)
        columns = jnp.dot(chosen, states_ref[...], preferred_element_type=F32)
        for v in range(variables):
            state[v] = columns[:, v * levels : (v + 1) * levels].astype(BF16)
        scaled_rows[...] = jnp.zeros_like(scaled_rows)
        total[...] = jnp.zeros_like(total)

    first = pl.multiple_of(step * group, group)
    mine = [state[v, pl.ds(first, group), :] for v in range(variables)]
    model = jnp.zeros((group, channels), F32)
    for r in range(group):
        one = jnp.dot(mine[0], jac_ref[r, 0], preferred_element_type=F32)
        for v in range(1, variables):
            one += jnp.dot(mine[v], jac_ref[r, v], preferred_element_type=F32)
        model = jnp.where(row_iota(model.shape) == r, one, model)
    alive = lane_iota(model.shape) < valid_ref[pl.ds(first, group), :]
    weight = jnp.where(alive, inv_ref[pl.ds(first, group), :].astype(F32), 0.0)
    scaled = (weight * (model - obs_ref[pl.ds(first, group), :].astype(F32))).astype(BF16)
    for v in range(variables):
        scaled_rows[pl.ds(pl.multiple_of(v * records + first, group), group), :] = scaled
    against = scaled_rows[...]
    sums = total[...]
    lane = lane_iota(sums.shape)
    for r in range(group):
        for v in range(variables):
            one = lax.dot_general(
                jac_ref[r, v], against, (((1,), (1,)), ((), ())), preferred_element_type=F32
            )
            sums = jnp.where(lane == v * records + first + r, one, sums)
    total[...] = sums

    @pl.when(step == pl.num_programs(0) - 1)
    def _():
        low = sums.astype(BF16)
        for t in range(out_ref.shape[0]):
            out_ref[t] = low


def departures(dest, valid, states, obs, inv, jac, capacity, devices):
    records, variables, levels, channels = jac.shape
    group = 16

    def whole(shape):
        return pl.BlockSpec(shape, lambda s: (0,) * len(shape))

    return pl.pallas_call(
        functools.partial(departure_kernel, capacity),
        grid=(records // group,),
        in_specs=[
            whole(dest.shape),
            whole(valid.shape),
            whole(states.shape),
            whole(obs.shape),
            whole(inv.shape),
            pl.BlockSpec((group, variables, levels, channels), lambda s: (s, 0, 0, 0)),
        ],
        out_specs=whole((devices, levels, variables * records)),
        out_shape=jax.ShapeDtypeStruct((devices, levels, variables * records), BF16),
        scratch_shapes=[
            pltpu.VMEM((variables, records, levels), BF16),
            pltpu.VMEM((variables * records, channels), BF16),
            pltpu.VMEM((levels, variables * records), F32),
        ],
        compiler_params=pltpu.CompilerParams(vmem_limit_bytes=VMEM_LIMIT),
        cost_estimate=pl.CostEstimate(
            flops=4 * jac.size, bytes_accessed=jac.size * 2, transcendentals=0
        ),
        name="departures",
    )(dest, valid, states, obs, inv, jac)


STRIDE = 256
NOWHERE = 1 << 20


def point_key(tile, column, count, reach):
    me = lax.axis_index("lon")
    right, left = lax.rem(me + 1, count), lax.rem(me + count - 1, count)
    row = lax.div(column, LANES)
    lon = column - row * LANES
    key = jnp.where(tile == me, lon + reach, NOWHERE)
    key = jnp.where((tile == right) & (lon < reach), lon + LANES + reach, key)
    key = jnp.where((tile == left) & (lon >= LANES - reach), lon - LANES + reach, key)
    return jnp.where(key == NOWHERE, NOWHERE, key + row * STRIDE)


def plan_kernel(records, points, reach, codes_ref, same_ref, info_ref, down, first):
    count = codes_ref.shape[0]
    span, listed = count * records, same_ref.shape[0]
    tile, column = split_codes(codes_ref, records, points)
    key = point_key(tile, column, count, reach)
    for d in range(count):
        down[d * records : (d + 1) * records, :] = jnp.broadcast_to(key[:, d : d + 1], (records, LANES))
    codes = codes_ref[...]
    tile = lax.div(codes, points)
    key = point_key(tile, codes - tile * points, count, reach)
    per = LANES // records
    across = []
    for t in range(span // LANES):
        lane = lane_iota((1, LANES))
        one = key[per * t : per * t + 1, :]
        for h in range(1, per):
            one = jnp.where(
                lane < h * records, one, pltpu.roll(key[per * t + h : per * t + h + 1, :], h * records, 1)
            )
        across.append(one)
    repeats = jnp.zeros((span, LANES), F32)
    for t, one in enumerate(across):
        before = lane_iota((span, LANES)) + t * LANES < row_iota((span, LANES))
        repeats += ((down[...] == one) & before).astype(F32)
    fresh = jnp.sum(repeats, axis=1, keepdims=True) == 0.0
    first[...] = (fresh & (down[...] < NOWHERE)).astype(F32)
    found = jnp.zeros((listed, LANES), jnp.int32)
    for t, one in enumerate(across):
        rank = jnp.sum(jnp.where(down[...] < one, first[...], 0.0), axis=0, keepdims=True)
        rank = jnp.where(one < NOWHERE, rank.astype(jnp.int32), -1)
        same = rank == row_iota((listed, LANES))
        same_ref[:, t * LANES : (t + 1) * LANES] = same.astype(F32).astype(BF16)
        found = jnp.maximum(found, jnp.where(same, one, 0))
    found = jnp.max(found, axis=1, keepdims=True).astype(F32)
    for b in range(listed // LANES):
        wide = jnp.broadcast_to(found[b * LANES : (b + 1) * LANES], (LANES, LANES))
        info_ref[0:1, b * LANES : (b + 1) * LANES] = jnp.transpose(wide)[0:1].astype(jnp.int32)
    starts = jnp.where(down[...] < lane_iota((span, LANES)) * STRIDE, first[...], 0.0)
    info_ref[0:1, listed:] = jnp.sum(starts, axis=0, keepdims=True).astype(jnp.int32)


def impact_kernel(records, products_ref, same_ref, out_ref, terms):
    count, levels, width = products_ref.shape
    listed = same_ref.shape[0]
    tall = out_ref.shape[0]
    variables = out_ref.shape[1] // listed
    terms[...] = jnp.zeros_like(terms)
    lane = lane_iota((levels, width))
    for pair in range(count // variables):
        one = products_ref[2 * pair].astype(F32)
        two = products_ref[2 * pair + 1].astype(F32)
        first = jnp.where(lane < records, one, pltpu.roll(two, records, 1))
        second = jnp.where(lane < records, pltpu.roll(one, records, 1), two)
        terms[0, 0:levels, pair * width : (pair + 1) * width] = first.astype(BF16)
        terms[1, 0:levels, pair * width : (pair + 1) * width] = second.astype(BF16)
    for v in range(variables):
        out_ref[:, v * listed : (v + 1) * listed] = lax.dot_general(
            terms[v], same_ref[...], (((1,), (1,)), ((), ())), preferred_element_type=F32
        ).astype(BF16)


def filter_kernel(block_of, reach, rows, *refs):
    (*lists, vertical_ref, lon_ref, lat_ref, out_ref, mixed, along, mean) = refs
    lists = [(lists[n], lists[n + 1]) for n in range(0, len(lists) // 2 * 2, 2)]
    listed = lists[0][1].shape[1] // vertical_ref.shape[0]
    features = out_ref.shape[0]
    wide = vertical_ref.shape[2]
    height = out_ref.shape[1]
    window = height + 2 * reach
    pitch = along.shape[0] // window
    step = pl.program_id(0)
    base = block_of(step) * height - reach

    @pl.when(step == 0)
    def _():
        for n, (_, impact) in enumerate(lists):
            total = 0.0
            for v in range(vertical_ref.shape[0]):
                total += lax.dot_general(
                    impact[:, v * listed : (v + 1) * listed],
                    vertical_ref[v],
                    (((0,), (0,)), ((), ())),
                    preferred_element_type=F32,
                )
            mixed[n * listed : (n + 1) * listed, :] = total

    along[...] = jnp.zeros_like(along)
    for n, (info, _) in enumerate(lists):
        offset = (0, -rows, rows)[n] - base
        low = jnp.clip(-offset, 0, rows)
        high = jnp.clip(window - offset, 0, rows)

        def add(s, carry, info=info, n=n, offset=offset):
            key = info[0, s]
            row = lax.shift_right_logical(key, 8) + offset
            place = jnp.bitwise_and(key, STRIDE - 1)
            spot = jnp.bitwise_and(place, 7)
            at = pl.ds(pl.multiple_of(row * pitch + place - spot, 8), 16)
            taps = lon_ref[pl.ds(pl.multiple_of(spot * 16, 16), 16), :]
            along[at, :] += taps * mixed[pl.ds(n * listed + s, 1), :]
            return carry

        lax.fori_loop(info[0, listed + low], info[0, listed + high], add, 0)

    flat = out_ref.reshape(features * height, LANES)
    for t in range(wide // LANES):
        here = slice(t * LANES, (t + 1) * LANES)
        lat = [jnp.broadcast_to(lat_ref[k : k + 1, here], (8, LANES)) for k in range(2 * reach + 1)]

        @pl.loop(0, LANES // 8, unroll=2)
        def _(j):
            sums = [None] * height
            for w in range(window):
                part = along[pl.ds(pl.multiple_of(w * pitch + 8 + j * 8, 8), 8), here]
                for row in range(max(0, w - 2 * reach), min(height, w + 1)):
                    term = lat[w - row] * part
                    sums[row] = term if sums[row] is None else sums[row] + term
            for row in range(height):
                mean[row, pl.ds(pl.multiple_of(j * 8, 8), 8), :] = sums[row]

        kept = min(LANES, features - t * LANES)
        for row in range(height):
            turned = jnp.transpose(mean[row])
            flat[pl.ds(t * LANES * height + row, kept, stride=height), :] = turned[0:kept]


def solution(mesh):
    lon_devices, lat_devices = mesh.shape["lon"], mesh.shape["lat"]

    def body(state_field, jacobian, observed, inverse_var, valid_count, destination, column, vertical, lon_taps, lat_taps):
        variables, levels, rows, cols = state_field.shape
        features = variables * levels
        records, channels = jacobian.shape[1], jacobian.shape[-1]
        capacity = max(2, 2 * records // lon_devices)
        reach = lon_taps.shape[-1] // 2
        points = rows * cols
        span = records * lon_devices
        tall = pl.cdiv(levels, 16) * 16

        dest = destination.reshape(records, 1)
        codes = destination.reshape(1, records) * points + column.reshape(1, records)
        codes = jnp.broadcast_to(jnp.pad(codes, ((0, 0), (0, LANES - records))), (lon_devices, LANES))
        codes = lax.all_to_all(codes, "lon", split_axis=0, concat_axis=0, tiled=True)

        found = gather_state(codes, state_field, records, capacity)
        found = found.reshape(lon_devices, capacity, found.shape[-1])
        found = lax.all_to_all(found, "lon", split_axis=0, concat_axis=0, tiled=True)
        found = found.reshape(lon_devices * capacity, found.shape[-1])

        products = departures(
            dest,
            valid_count.reshape(records, 1),
            found,
            observed.reshape(records, channels),
            inverse_var.reshape(records, channels),
            jacobian.reshape(records, variables, levels, channels),
            capacity,
            lon_devices,
        )
        products = lax.all_to_all(products, "lon", split_axis=0, concat_axis=0, tiled=True)

        listed = 3 * lon_devices * capacity
        wide = pl.cdiv(features, LANES) * LANES
        plan = pl.pallas_call(
            functools.partial(plan_kernel, records, points, reach),
            out_shape=(
                jax.ShapeDtypeStruct((listed, span), BF16),
                jax.ShapeDtypeStruct((1, listed + LANES), jnp.int32),
            ),
            scratch_shapes=[pltpu.VMEM((span, LANES), jnp.int32), pltpu.VMEM((span, LANES), F32)],
            compiler_params=pltpu.CompilerParams(vmem_limit_bytes=16 * 1024 * 1024),
            cost_estimate=pl.CostEstimate(flops=8 * span * span, bytes_accessed=span * listed * 2, transcendentals=0),
            name="plan_points",
        )
        same, info = plan(codes)
        down = [(i, i + 1) for i in range(lat_devices - 1)]
        up = [(i + 1, i) for i in range(lat_devices - 1)]
        info_above, info_below = lax.ppermute(info, "lat", down), lax.ppermute(info, "lat", up)

        impact = pl.pallas_call(
            functools.partial(impact_kernel, records),
            out_shape=jax.ShapeDtypeStruct((tall, variables * listed), BF16),
            scratch_shapes=[pltpu.VMEM((variables, tall, span), BF16)],
            compiler_params=pltpu.CompilerParams(vmem_limit_bytes=16 * 1024 * 1024),
            name="impact_columns",
        )(products, same)
        above, below = lax.ppermute(impact, "lat", down), lax.ppermute(impact, "lat", up)

        mixing = jnp.stack(
            [
                jnp.pad(vertical[v], ((0, tall - levels), (v * levels, wide - (v + 1) * levels)))
                for v in range(variables)
            ]
        )
        lon_flat = jnp.pad(lon_taps.reshape(features, -1).T[::-1], ((0, 0), (0, wide - features)))
        taps = lon_flat.shape[0]
        lon_table = jnp.concatenate([jnp.pad(lon_flat, ((b, 16 - taps - b), (0, 0))) for b in range(8)])
        lat_flat = jnp.pad(lat_taps.reshape(features, -1).T, ((0, 0), (0, wide - features)))

        height = 8
        blocks = rows // height
        pitch = LANES + 16

        def filtered(lists, steps, block_of, before, name):
            held = [pl.BlockSpec(memory_space=pltpu.SMEM), pl.BlockSpec(memory_space=pltpu.VMEM)] * (len(lists) // 2)
            held += [pl.BlockSpec(memory_space=pltpu.VMEM)] * 3
            given = list(lists) + [mixing, lon_table, lat_flat]
            kernel = functools.partial(filter_kernel, block_of, reach, rows)
            if before is not None:
                given.append(before)
                held.append(pl.BlockSpec(memory_space=pl.ANY))
                at = len(lists) + 3
                inner = kernel
                kernel = lambda *refs: inner(*refs[:at], *refs[at + 1 :])
            return pl.pallas_call(
                kernel,
                grid=(steps,),
                in_specs=held,
                out_specs=pl.BlockSpec((features, height, cols), lambda s: (0, block_of(s), 0)),
                out_shape=jax.ShapeDtypeStruct((features, rows, cols), F32),
                scratch_shapes=[
                    pltpu.VMEM((len(lists) // 2 * listed, wide), F32),
                    pltpu.VMEM(((height + 2 * reach) * pitch, wide), F32),
                    pltpu.VMEM((height, cols, LANES), F32),
                ],
                input_output_aliases={} if before is None else {len(given) - 1: 0},
                compiler_params=pltpu.CompilerParams(vmem_limit_bytes=24 * 1024 * 1024),
                cost_estimate=pl.CostEstimate(
                    flops=40 * features * rows * cols, bytes_accessed=features * rows * cols * 2, transcendentals=0
                ),
                name=name,
            )(*given)

        inner = filtered([info, impact], blocks - 2, lambda s: s + 1, None, "inner_rows")
        result = filtered(
            [info, impact, info_above, above, info_below, below],
            2,
            lambda s: s * (blocks - 1),
            inner,
            "outer_rows",
        )
        return result.reshape(variables, levels, rows, cols)

    placed = (
        P(None, None, "lat", "lon"),
        P("lat", "lon", None, None, None),
        P("lat", "lon", None),
        P("lat", "lon", None),
        P("lat", "lon"),
        P("lat", "lon", None),
        P("lat", "lon"),
        P(),
        P(),
        P(),
    )
    return jax.shard_map(
        body, mesh=mesh, in_specs=placed, out_specs=P(None, None, "lat", "lon"), check_vma=False
    )
```

```python
import functools

import jax
import jax.numpy as jnp
from jax import lax
from jax.experimental import pallas as pl
from jax.experimental.pallas import tpu as pltpu
from jax.sharding import PartitionSpec as P

LANES = 128
F32 = jnp.float32
BF16 = jnp.bfloat16
VMEM_LIMIT = 56 * 1024 * 1024


def lane_iota(shape):
    return lax.broadcasted_iota(jnp.int32, shape, 1)


def row_iota(shape):
    return lax.broadcasted_iota(jnp.int32, shape, 0)


def earlier_rows(size):
    return (lane_iota((size, size)) < row_iota((size, size))).astype(F32).astype(BF16)


def split_codes(codes_ref, records, points):
    flipped = jnp.transpose(codes_ref[...].astype(F32))[:records].astype(jnp.int32)
    tile = lax.div(flipped, points)
    return tile, flipped - tile * points


def gather_kernel(records, capacity, rows, levels, chunk, codes_ref, state_ref, out_ref, state, held, arrived):
    count = codes_ref.shape[0]
    slots = out_ref.shape[0]
    variables = state_ref.shape[0] // (rows * levels)
    parts = []
    for first in range(0, levels, chunk):
        size = min(chunk, levels - first)
        for v in range(variables):
            here = pl.ds((v * levels + first) * rows, size * rows)
            copy = pltpu.make_async_copy(state_ref.at[here], state.at[here], arrived.at[len(parts)])
            copy.start()
            parts.append((v, first, size, here, copy))

    held[...] = jnp.zeros_like(held)
    me = lax.axis_index("lon")
    tile, column = split_codes(codes_ref, records, rows * LANES)
    mine = (tile == me).astype(F32)
    rank = jnp.dot(earlier_rows(records), mine.astype(BF16), preferred_element_type=F32)
    slot = lane_iota(mine.shape) * capacity + rank.astype(jnp.int32)
    slot = jnp.where(tile == me, slot, -1)
    row_of = jnp.zeros((1, slots), F32)
    lon_of = jnp.zeros((1, slots), F32)
    for d in range(count):
        hit = slot[:, d : d + 1] == lane_iota((records, slots))
        row = lax.div(column[:, d : d + 1], LANES)
        lon = column[:, d : d + 1] - row * LANES
        row_of += jnp.sum(jnp.where(hit, (row + 1).astype(F32), 0.0), axis=0, keepdims=True)
        lon_of += jnp.sum(jnp.where(hit, lon.astype(F32), 0.0), axis=0, keepdims=True)
    pick = (row_iota((LANES, slots)) == lon_of.astype(jnp.int32)).astype(F32).astype(BF16)
    row_mask = (row_iota((rows, slots)) == row_of.astype(jnp.int32) - 1).astype(F32)

    for v, first, size, here, copy in parts:
        copy.wait()
        found = jnp.dot(state[here, :].astype(BF16), pick, preferred_element_type=F32)
        found = found.reshape(size, rows, slots) * row_mask[None]
        held[pl.ds(variables * first + v, size, stride=variables), :] = jnp.sum(found, axis=1)
    for t in range(out_ref.shape[1] // LANES):
        out_ref[:, t * LANES : (t + 1) * LANES] = jnp.transpose(
            held[t * LANES : (t + 1) * LANES, :]
        ).astype(BF16)


def gather_state(codes, state, records, capacity):
    variables, levels, rows, cols = state.shape
    features = variables * levels
    wide = pl.cdiv(features, LANES) * LANES
    slots = codes.shape[0] * capacity
    chunk = 32
    return pl.pallas_call(
        functools.partial(gather_kernel, records, capacity, rows, levels, chunk),
        in_specs=[pl.BlockSpec(memory_space=pltpu.VMEM), pl.BlockSpec(memory_space=pl.ANY)],
        out_shape=jax.ShapeDtypeStruct((slots, wide), BF16),
        scratch_shapes=[
            pltpu.VMEM((features * rows, cols), F32),
            pltpu.VMEM((wide, slots), F32),
            pltpu.SemaphoreType.DMA((variables * pl.cdiv(levels, chunk),)),
        ],
        compiler_params=pltpu.CompilerParams(vmem_limit_bytes=20 * 1024 * 1024),
        cost_estimate=pl.CostEstimate(
            flops=2 * features * rows * cols * slots, bytes_accessed=features * rows * cols * 4, transcendentals=0
        ),
        name="gather_state",
    )(codes, state.reshape(features * rows, cols))


def departure_kernel(capacity, group, dest_ref, valid_ref, states_ref, obs_ref, inv_ref, jac_ref, out_ref, jac, scaled_rows, sums, total, arrived):
    records = dest_ref.shape[0]
    slots = states_ref.shape[0]
    channels = jac_ref.shape[1]
    features = jac_ref.shape[0] // records
    span = group * features
    copies = []
    for g in range(records // group):
        here = pl.ds(g * span, span)
        copies.append(pltpu.make_async_copy(jac_ref.at[here], jac.at[here], arrived.at[g]))
        copies[g].start()

    dest = dest_ref[...]
    named = (dest == lane_iota((records, LANES))).astype(F32)
    before = jnp.dot(earlier_rows(records), named.astype(BF16), preferred_element_type=F32)
    rank = jnp.sum(before * named, axis=1, keepdims=True).astype(jnp.int32)
    chosen = (dest * capacity + rank == lane_iota((records, slots))).astype(F32).astype(BF16)
    columns = jnp.dot(chosen, states_ref[...], preferred_element_type=F32)
    alive = lane_iota((records, channels)) < valid_ref[...]
    weight = jnp.where(alive, inv_ref[...].astype(F32), 0.0)
    scaled_rows[...] = jnp.zeros_like(scaled_rows)
    total[...] = jnp.zeros_like(total)

    tiles, skip = divmod(features, LANES)
    wide = columns.shape[1]
    reach = pl.cdiv(skip * (group - 1) + features, LANES)
    row = row_iota((group, LANES))
    half = total.shape[0] // 2
    for g in range(records // group):
        mine = columns[g * group : (g + 1) * group]
        mine = jnp.concatenate([mine, jnp.zeros((group, reach * LANES - wide), F32)], axis=1)
        bit = 1
        while bit < group:
            moved = pltpu.roll(mine, skip * bit, 1)
            mine = jnp.where(jnp.bitwise_and(row_iota(mine.shape), bit) > 0, moved, mine)
            bit *= 2
        spread = []
        for t in range(pl.cdiv(span, LANES)):
            piece = jnp.zeros((group, LANES), F32)
            for r in range(group):
                at = t - tiles * r
                if 0 <= at < reach:
                    piece = jnp.where(row == r, mine[:, at * LANES : (at + 1) * LANES], piece)
            spread.append(piece.astype(BF16))
        spread = jnp.concatenate(spread, axis=1)[:, :span]
        copies[g].wait()
        here = slice(g * span, (g + 1) * span)
        model = jnp.dot(spread, jac[here, :], preferred_element_type=F32)
        own = slice(g * group, (g + 1) * group)
        misfit = weight[own] * (model - obs_ref[own, :].astype(F32))
        scaled_rows[own, :] = misfit.astype(BF16)
        against = scaled_rows[...]
        for h in range(2):
            part = span // 2
            sums[...] = lax.dot_general(
                jac[g * span + h * part : g * span + (h + 1) * part, :],
                against,
                (((1,), (1,)), ((), ())),
                preferred_element_type=F32,
            )
            kept = total[0:features, :]
            lane = lane_iota(kept.shape)
            for r in range(group // 2):
                kept = jnp.where(
                    lane == g * group + h * (group // 2) + r, sums[r * features : (r + 1) * features, :], kept
                )
            total[0:features, :] = kept
    lane = lane_iota((half, LANES))
    low = jnp.where(lane < records, total[0:half, :], pltpu.roll(total[half:, :], records, 1)).astype(BF16)
    for t in range(out_ref.shape[0]):
        out_ref[t] = low


def departures(dest, valid, states, obs, inv, jac, capacity, devices, tall):
    records = dest.shape[0]
    channels = jac.shape[1]
    features = jac.shape[0] // records
    group = 16
    vmem = pl.BlockSpec(memory_space=pltpu.VMEM)
    return pl.pallas_call(
        functools.partial(departure_kernel, capacity, group),
        in_specs=[vmem] * 5 + [pl.BlockSpec(memory_space=pl.ANY)],
        out_shape=jax.ShapeDtypeStruct((devices, tall, 2 * records), BF16),
        scratch_shapes=[
            pltpu.VMEM(jac.shape, BF16),
            pltpu.VMEM((2 * records, channels), BF16),
            pltpu.VMEM((group // 2 * features, 2 * records), F32),
            pltpu.VMEM((2 * tall, 2 * records), F32),
            pltpu.SemaphoreType.DMA((records // group,)),
        ],
        compiler_params=pltpu.CompilerParams(vmem_limit_bytes=20 * 1024 * 1024),
        cost_estimate=pl.CostEstimate(
            flops=4 * jac.size, bytes_accessed=jac.size * 2, transcendentals=0
        ),
        name="departures",
    )(dest, valid, states, obs, inv, jac)


STRIDE = 256
NOWHERE = 1 << 20


def point_key(tile, column, count, reach):
    me = lax.axis_index("lon")
    right, left = lax.rem(me + 1, count), lax.rem(me + count - 1, count)
    row = lax.div(column, LANES)
    lon = column - row * LANES
    key = jnp.where(tile == me, lon + reach, NOWHERE)
    key = jnp.where((tile == right) & (lon < reach), lon + LANES + reach, key)
    key = jnp.where((tile == left) & (lon >= LANES - reach), lon - LANES + reach, key)
    return jnp.where(key == NOWHERE, NOWHERE, key + row * STRIDE)


def plan_kernel(records, points, reach, codes_ref, same_ref, info_ref, down, first):
    count = codes_ref.shape[0]
    span, listed = count * records, same_ref.shape[0]
    tile, column = split_codes(codes_ref, records, points)
    key = point_key(tile, column, count, reach)
    for d in range(count):
        down[d * records : (d + 1) * records, :] = jnp.broadcast_to(key[:, d : d + 1], (records, LANES))
    codes = codes_ref[...]
    tile = lax.div(codes, points)
    key = point_key(tile, codes - tile * points, count, reach)
    per = LANES // records
    across = []
    for t in range(span // LANES):
        lane = lane_iota((1, LANES))
        one = key[per * t : per * t + 1, :]
        for h in range(1, per):
            one = jnp.where(
                lane < h * records, one, pltpu.roll(key[per * t + h : per * t + h + 1, :], h * records, 1)
            )
        across.append(one)
    repeats = jnp.zeros((span, LANES), F32)
    for t, one in enumerate(across):
        before = lane_iota((span, LANES)) + t * LANES < row_iota((span, LANES))
        repeats += ((down[...] == one) & before).astype(F32)
    fresh = jnp.sum(repeats, axis=1, keepdims=True) == 0.0
    first[...] = (fresh & (down[...] < NOWHERE)).astype(F32)
    found = jnp.zeros((listed, LANES), jnp.int32)
    for t, one in enumerate(across):
        rank = jnp.sum(jnp.where(down[...] < one, first[...], 0.0), axis=0, keepdims=True)
        rank = jnp.where(one < NOWHERE, rank.astype(jnp.int32), -1)
        same = rank == row_iota((listed, LANES))
        same_ref[:, t * LANES : (t + 1) * LANES] = same.astype(F32).astype(BF16)
        found = jnp.maximum(found, jnp.where(same, one, 0))
    found = jnp.max(found, axis=1, keepdims=True).astype(F32)
    for b in range(listed // LANES):
        wide = jnp.broadcast_to(found[b * LANES : (b + 1) * LANES], (LANES, LANES))
        info_ref[0:1, b * LANES : (b + 1) * LANES] = jnp.transpose(wide)[0:1].astype(jnp.int32)
    starts = jnp.where(down[...] < lane_iota((span, LANES)) * STRIDE, first[...], 0.0)
    info_ref[0:1, listed:] = jnp.sum(starts, axis=0, keepdims=True).astype(jnp.int32)


def impact_kernel(records, products_ref, same_ref, out_ref, terms):
    count, tall, width = products_ref.shape
    listed = same_ref.shape[0]
    lane = lane_iota((tall, width))
    for pair in range(count // 2):
        one = products_ref[2 * pair].astype(F32)
        two = products_ref[2 * pair + 1].astype(F32)
        first = jnp.where(lane < records, one, pltpu.roll(two, records, 1))
        second = jnp.where(lane < records, pltpu.roll(one, records, 1), two)
        terms[0, :, pair * width : (pair + 1) * width] = first.astype(BF16)
        terms[1, :, pair * width : (pair + 1) * width] = second.astype(BF16)
    for h in range(2):
        out_ref[:, h * listed : (h + 1) * listed] = lax.dot_general(
            terms[h], same_ref[...], (((1,), (1,)), ((), ())), preferred_element_type=F32
        ).astype(BF16)


def filter_kernel(block_of, reach, rows, *refs):
    (*lists, vertical_ref, lon_ref, lat_ref, out_ref, mixed, along, mean) = refs
    lists = [(lists[n], lists[n + 1]) for n in range(0, len(lists) // 2 * 2, 2)]
    listed = lists[0][1].shape[1] // vertical_ref.shape[0]
    features = out_ref.shape[0]
    wide = vertical_ref.shape[2]
    height = out_ref.shape[1]
    window = height + 2 * reach
    pitch = along.shape[0] // window
    step = pl.program_id(0)
    base = block_of(step) * height - reach

    @pl.when(step == 0)
    def _():
        for n, (_, impact) in enumerate(lists):
            total = 0.0
            for v in range(vertical_ref.shape[0]):
                total += lax.dot_general(
                    impact[:, v * listed : (v + 1) * listed],
                    vertical_ref[v],
                    (((0,), (0,)), ((), ())),
                    preferred_element_type=F32,
                )
            mixed[n * listed : (n + 1) * listed, :] = total

    along[...] = jnp.zeros_like(along)
    for n, (info, _) in enumerate(lists):
        offset = (0, -rows, rows)[n] - base
        low = jnp.clip(-offset, 0, rows)
        high = jnp.clip(window - offset, 0, rows)

        def add(s, carry, info=info, n=n, offset=offset):
            key = info[0, s]
            row = lax.shift_right_logical(key, 8) + offset
            place = jnp.bitwise_and(key, STRIDE - 1)
            spot = jnp.bitwise_and(place, 7)
            at = pl.ds(pl.multiple_of(row * pitch + place - spot, 8), 16)
            taps = lon_ref[pl.ds(pl.multiple_of(spot * 16, 16), 16), :]
            along[at, :] += taps * mixed[pl.ds(n * listed + s, 1), :]
            return carry

        lax.fori_loop(info[0, listed + low], info[0, listed + high], add, 0)

    flat = out_ref.reshape(features * height, LANES)
    for t in range(wide // LANES):
        here = slice(t * LANES, (t + 1) * LANES)
        lat = [jnp.broadcast_to(lat_ref[k : k + 1, here], (8, LANES)) for k in range(2 * reach + 1)]

        @pl.loop(0, LANES // 8, unroll=2)
        def _(j):
            sums = [None] * height
            for w in range(window):
                part = along[pl.ds(pl.multiple_of(w * pitch + 8 + j * 8, 8), 8), here]
                for row in range(max(0, w - 2 * reach), min(height, w + 1)):
                    term = lat[w - row] * part
                    sums[row] = term if sums[row] is None else sums[row] + term
            for row in range(height):
                mean[row, pl.ds(pl.multiple_of(j * 8, 8), 8), :] = sums[row]

        kept = min(LANES, features - t * LANES)
        for row in range(height):
            turned = jnp.transpose(mean[row])
            flat[pl.ds(t * LANES * height + row, kept, stride=height), :] = turned[0:kept]


def solution(mesh):
    lon_devices, lat_devices = mesh.shape["lon"], mesh.shape["lat"]

    def body(state_field, jacobian, observed, inverse_var, valid_count, destination, column, vertical, lon_taps, lat_taps):
        variables, levels, rows, cols = state_field.shape
        features = variables * levels
        records, channels = jacobian.shape[1], jacobian.shape[-1]
        capacity = max(2, 2 * records // lon_devices)
        reach = lon_taps.shape[-1] // 2
        points = rows * cols
        span = records * lon_devices
        tall = pl.cdiv(features, 32) * 16

        dest = destination.reshape(records, 1)
        codes = destination.reshape(1, records) * points + column.reshape(1, records)
        codes = jnp.broadcast_to(jnp.pad(codes, ((0, 0), (0, LANES - records))), (lon_devices, LANES))
        codes = lax.all_to_all(codes, "lon", split_axis=0, concat_axis=0, tiled=True)

        found = gather_state(codes, state_field, records, capacity)
        found = found.reshape(lon_devices, capacity, found.shape[-1])
        found = lax.all_to_all(found, "lon", split_axis=0, concat_axis=0, tiled=True)
        found = found.reshape(lon_devices * capacity, found.shape[-1])

        products = departures(
            dest,
            valid_count.reshape(records, 1),
            found,
            observed.reshape(records, channels),
            inverse_var.reshape(records, channels),
            jnp.swapaxes(jacobian.reshape(records, variables, levels, channels), 1, 2).reshape(-1, channels),
            capacity,
            lon_devices,
            tall,
        )
        products = lax.all_to_all(products, "lon", split_axis=0, concat_axis=0, tiled=True)

        listed = 3 * lon_devices * capacity
        wide = pl.cdiv(features, LANES) * LANES
        plan = pl.pallas_call(
            functools.partial(plan_kernel, records, points, reach),
            out_shape=(
                jax.ShapeDtypeStruct((listed, span), BF16),
                jax.ShapeDtypeStruct((1, listed + LANES), jnp.int32),
            ),
            scratch_shapes=[pltpu.VMEM((span, LANES), jnp.int32), pltpu.VMEM((span, LANES), F32)],
            compiler_params=pltpu.CompilerParams(vmem_limit_bytes=16 * 1024 * 1024),
            cost_estimate=pl.CostEstimate(flops=8 * span * span, bytes_accessed=span * listed * 2, transcendentals=0),
            name="plan_points",
        )
        same, info = plan(codes)
        down = [(i, i + 1) for i in range(lat_devices - 1)]
        up = [(i + 1, i) for i in range(lat_devices - 1)]
        info_above, info_below = lax.ppermute(info, "lat", down), lax.ppermute(info, "lat", up)

        impact = pl.pallas_call(
            functools.partial(impact_kernel, records),
            out_shape=jax.ShapeDtypeStruct((tall, 2 * listed), BF16),
            scratch_shapes=[pltpu.VMEM((2, tall, span), BF16)],
            compiler_params=pltpu.CompilerParams(vmem_limit_bytes=16 * 1024 * 1024),
            name="impact_columns",
        )(products, same)
        above, below = lax.ppermute(impact, "lat", down), lax.ppermute(impact, "lat", up)

        mixing = jnp.stack(
            [
                jnp.pad(vertical[v], ((0, 0), (v * levels, wide - (v + 1) * levels)))
                for v in range(variables)
            ],
            axis=1,
        ).reshape(features, wide)
        mixing = jnp.pad(mixing, ((0, 2 * tall - features), (0, 0))).reshape(2, tall, wide)
        lon_flat = jnp.pad(lon_taps.reshape(features, -1).T[::-1], ((0, 0), (0, wide - features)))
        taps = lon_flat.shape[0]
        lon_table = jnp.concatenate([jnp.pad(lon_flat, ((b, 16 - taps - b), (0, 0))) for b in range(8)])
        lat_flat = jnp.pad(lat_taps.reshape(features, -1).T, ((0, 0), (0, wide - features)))

        height = 8
        blocks = rows // height
        pitch = LANES + 16

        def filtered(lists, steps, block_of, before, name):
            held = [pl.BlockSpec(memory_space=pltpu.SMEM), pl.BlockSpec(memory_space=pltpu.VMEM)] * (len(lists) // 2)
            held += [pl.BlockSpec(memory_space=pltpu.VMEM)] * 3
            given = list(lists) + [mixing, lon_table, lat_flat]
            kernel = functools.partial(filter_kernel, block_of, reach, rows)
            if before is not None:
                given.append(before)
                held.append(pl.BlockSpec(memory_space=pl.ANY))
                at = len(lists) + 3
                inner = kernel
                kernel = lambda *refs: inner(*refs[:at], *refs[at + 1 :])
            return pl.pallas_call(
                kernel,
                grid=(steps,),
                in_specs=held,
                out_specs=pl.BlockSpec((features, height, cols), lambda s: (0, block_of(s), 0)),
                out_shape=jax.ShapeDtypeStruct((features, rows, cols), F32),
                scratch_shapes=[
                    pltpu.VMEM((len(lists) // 2 * listed, wide), F32),
                    pltpu.VMEM(((height + 2 * reach) * pitch, wide), F32),
                    pltpu.VMEM((height, cols, LANES), F32),
                ],
                input_output_aliases={} if before is None else {len(given) - 1: 0},
                compiler_params=pltpu.CompilerParams(vmem_limit_bytes=24 * 1024 * 1024),
                cost_estimate=pl.CostEstimate(
                    flops=40 * features * rows * cols, bytes_accessed=features * rows * cols * 2, transcendentals=0
                ),
                name=name,
            )(*given)

        inner = filtered([info, impact], blocks - 2, lambda s: s + 1, None, "inner_rows")
        result = filtered(
            [info, impact, info_above, above, info_below, below],
            2,
            lambda s: s * (blocks - 1),
            inner,
            "outer_rows",
        )
        return result.reshape(variables, levels, rows, cols)

    placed = (
        P(None, None, "lat", "lon"),
        P("lat", "lon", None, None, None),
        P("lat", "lon", None),
        P("lat", "lon", None),
        P("lat", "lon"),
        P("lat", "lon", None),
        P("lat", "lon"),
        P(),
        P(),
        P(),
    )
    return jax.shard_map(
        body, mesh=mesh, in_specs=placed, out_specs=P(None, None, "lat", "lon"), check_vma=False
    )
```

```python
import functools

import jax
import jax.numpy as jnp
from jax import lax
from jax.experimental import pallas as pl
from jax.experimental.pallas import tpu as pltpu
from jax.sharding import PartitionSpec as P

LANES = 128
F32 = jnp.float32
BF16 = jnp.bfloat16
VMEM_LIMIT = 56 * 1024 * 1024


def lane_iota(shape):
    return lax.broadcasted_iota(jnp.int32, shape, 1)


def row_iota(shape):
    return lax.broadcasted_iota(jnp.int32, shape, 0)


def earlier_rows(size):
    return (lane_iota((size, size)) < row_iota((size, size))).astype(F32).astype(BF16)


def split_codes(codes_ref, records, points):
    flipped = jnp.transpose(codes_ref[...].astype(F32))[:records].astype(jnp.int32)
    tile = lax.div(flipped, points)
    return tile, flipped - tile * points


def lay_state_kernel(rows, levels, chunk, state_ref, out_ref, state, arrived):
    variables = state_ref.shape[0] // (rows * levels)
    half = rows // 2
    parts = []
    for first in range(0, levels, chunk):
        size = min(chunk, levels - first)
        for v in range(variables):
            start = (v * levels + first) * rows
            here = pl.ds(start, size * rows)
            copy = pltpu.make_async_copy(state_ref.at[here], state.at[here], arrived.at[len(parts)])
            copy.start()
            parts.append((v, first, size, start, copy))
    for v, first, size, start, copy in parts:
        copy.wait()
        for odd in range(2):
            some = state[pl.ds(start + odd, size * half, stride=2), :].astype(BF16)
            out_ref[first : first + size, v * half : (v + 1) * half, odd * LANES : (odd + 1) * LANES] = some.reshape(
                size, half, LANES
            )


def lay_state(state):
    variables, levels, rows, cols = state.shape
    chunk = 72
    return pl.pallas_call(
        functools.partial(lay_state_kernel, rows, levels, chunk),
        in_specs=[pl.BlockSpec(memory_space=pl.ANY)],
        out_shape=jax.ShapeDtypeStruct((levels, variables * rows // 2, 2 * cols), BF16),
        scratch_shapes=[
            pltpu.VMEM((variables * levels * rows, cols), F32),
            pltpu.SemaphoreType.DMA((variables * pl.cdiv(levels, chunk),)),
        ],
        compiler_params=pltpu.CompilerParams(vmem_limit_bytes=24 * 1024 * 1024),
        cost_estimate=pl.CostEstimate(flops=0, bytes_accessed=state.size * 6, transcendentals=0),
        name="lay_state",
    )(state.reshape(variables * levels * rows, cols))


def gather_kernel(records, capacity, rows, codes_ref, state_ref, out_ref, held):
    count = codes_ref.shape[0]
    slots = out_ref.shape[0]
    half = rows // 2
    features = state_ref.shape[0] // half
    me = lax.axis_index("lon")
    tile, column = split_codes(codes_ref, records, rows * LANES)
    mine = (tile == me).astype(F32)
    rank = jnp.dot(earlier_rows(records), mine.astype(BF16), preferred_element_type=F32)
    slot = lane_iota(mine.shape) * capacity + rank.astype(jnp.int32)
    slot = jnp.where(tile == me, slot, -1)
    place = jnp.zeros((records, slots), F32)
    for d in range(count):
        hit = slot[:, d : d + 1] == lane_iota((records, slots))
        place += jnp.where(hit, (column[:, d : d + 1] + 1).astype(F32), 0.0)
    place = jnp.sum(place, axis=0, keepdims=True).astype(jnp.int32) - 1
    row = lax.shift_right_arithmetic(place, LANES.bit_length() - 1)
    in_pair = jnp.where(place < 0, -1, jnp.bitwise_and(place, 2 * LANES - 1))
    pick = (row_iota((2 * LANES, slots)) == in_pair).astype(F32).astype(BF16)
    mask = (row_iota((half, slots)) == lax.shift_right_arithmetic(row, 1)).astype(F32)

    held[...] = jnp.zeros_like(held)
    chunk = 72
    for first in range(0, features, chunk):
        size = min(chunk, features - first)
        found = jnp.dot(
            state_ref[first * half : (first + size) * half, :], pick, preferred_element_type=F32
        )
        found = found.reshape(size, half, slots) * mask[None]
        held[first : first + size, :] = jnp.sum(found, axis=1)
    for t in range(out_ref.shape[1] // LANES):
        out_ref[:, t * LANES : (t + 1) * LANES] = jnp.transpose(
            held[t * LANES : (t + 1) * LANES, :]
        ).astype(BF16)


def gather_state(codes, laid, records, capacity, rows):
    features = laid.shape[0] * laid.shape[1] * 2 // rows
    wide = pl.cdiv(features, LANES) * LANES
    slots = codes.shape[0] * capacity
    vmem = pl.BlockSpec(memory_space=pltpu.VMEM)
    return pl.pallas_call(
        functools.partial(gather_kernel, records, capacity, rows),
        in_specs=[vmem, vmem],
        out_shape=jax.ShapeDtypeStruct((slots, wide), BF16),
        scratch_shapes=[pltpu.VMEM((wide, slots), F32)],
        compiler_params=pltpu.CompilerParams(vmem_limit_bytes=12 * 1024 * 1024),
        cost_estimate=pl.CostEstimate(flops=2 * laid.size * slots, bytes_accessed=laid.size * 2, transcendentals=0),
        name="gather_state",
    )(codes, laid.reshape(-1, laid.shape[2]))


def fetch_kernel(from_ref, after_ref, out_ref, arrived):
    copy = pltpu.make_async_copy(from_ref, out_ref, arrived)
    copy.start()
    copy.wait()


def fetch(array, after):
    anywhere = pl.BlockSpec(memory_space=pl.ANY)
    return pl.pallas_call(
        fetch_kernel,
        in_specs=[anywhere, anywhere],
        out_specs=pl.BlockSpec(memory_space=pltpu.VMEM),
        out_shape=jax.ShapeDtypeStruct(array.shape, array.dtype),
        scratch_shapes=[pltpu.SemaphoreType.DMA],
        compiler_params=pltpu.CompilerParams(vmem_limit_bytes=12 * 1024 * 1024),
        cost_estimate=pl.CostEstimate(flops=0, bytes_accessed=array.size * 4, transcendentals=0),
        name="fetch_jacobian",
    )(array, after)


def to_column(row):
    size = row.shape[1]
    wide = jnp.broadcast_to(row, (size, size))
    return jnp.sum(jnp.where(row_iota(wide.shape) == lane_iota(wide.shape), wide, 0), axis=1, keepdims=True)


def departure_kernel(capacity, group, dest_ref, valid_ref, states_ref, obs_ref, inv_ref, jac_ref, out_ref, total):
    records = dest_ref.shape[1]
    slots = states_ref.shape[0]
    channels = jac_ref.shape[1]
    features = jac_ref.shape[0] // records
    part = group // 2
    span = part * features

    dest = to_column(dest_ref[...])
    named = (dest == lane_iota((records, LANES))).astype(F32)
    before = jnp.dot(earlier_rows(records), named.astype(BF16), preferred_element_type=F32)
    rank = jnp.sum(before * named, axis=1, keepdims=True).astype(jnp.int32)
    chosen = (dest * capacity + rank == lane_iota((records, slots))).astype(F32).astype(BF16)
    columns = jnp.dot(chosen, states_ref[...], preferred_element_type=F32)
    alive = lane_iota((records, channels)) < to_column(valid_ref[...])
    weight = jnp.where(alive, inv_ref[...].astype(F32), 0.0)

    tiles, skip = divmod(features, LANES)
    wide = columns.shape[1]
    reach = pl.cdiv(skip * (part - 1) + features, LANES)
    tall = total.shape[0]
    total[...] = jnp.zeros_like(total)
    row = row_iota((group, LANES))
    index = jnp.bitwise_and(row, part - 1)
    for g in range(records // group):
        first = g * group * features
        mine = columns[g * group : (g + 1) * group]
        if reach * LANES > wide:
            mine = jnp.concatenate([mine, jnp.zeros((group, reach * LANES - wide), F32)], axis=1)
        bit = 1
        while bit < part:
            moved = pltpu.roll(mine, skip * bit, 1)
            mine = jnp.where(jnp.bitwise_and(row_iota(mine.shape), bit) > 0, moved, mine)
            bit *= 2
        spread = []
        for t in range(pl.cdiv(span, LANES)):
            piece = jnp.zeros((group, LANES), F32)
            for r in range(part):
                at = t - tiles * r
                if 0 <= at < reach:
                    piece = jnp.where(index == r, mine[:, at * LANES : (at + 1) * LANES], piece)
            spread.append(piece.astype(BF16))
        spread = jnp.concatenate(spread, axis=1)[:, :span]
        pair = jnp.concatenate([jac_ref[first : first + span, :], jac_ref[first + span : first + 2 * span, :]], axis=1)
        both = jnp.dot(spread, pair, preferred_element_type=F32)
        model = jnp.where(row < part, both[:, :channels], both[:, channels:])
        own = slice(g * group, (g + 1) * group)
        misfit = weight[own] * (model - obs_ref[own, :].astype(F32))
        low = misfit.astype(BF16).astype(F32)
        for r in range(part):
            against = jnp.concatenate([jnp.where(row == r, low, 0.0), jnp.where(row == r + part, low, 0.0)], axis=1)
            start = first + r * features
            lead = start % 16
            size = pl.cdiv(features + lead, 16) * 16
            rows = [jac_ref[start - lead + h * span : start - lead + h * span + size, :] for h in range(2)]
            one = lax.dot_general(
                jnp.concatenate(rows, axis=1),
                against.astype(BF16),
                (((1,), (1,)), ((), ())),
                preferred_element_type=F32,
            )
            one = one[lead : lead + features]
            sums = one if r == 0 else sums + one
        total[0:features, g * group : (g + 1) * group] = sums
    half = tall // 2
    lane = lane_iota((half, LANES))
    low = jnp.where(lane < records, total[0:half, :], pltpu.roll(total[half:, :], records, 1)).astype(BF16)
    for t in range(out_ref.shape[0]):
        out_ref[t] = low


def departures(dest, valid, states, obs, inv, jac, capacity, devices, tall):
    records, channels = obs.shape
    vmem = pl.BlockSpec(memory_space=pltpu.VMEM)
    return pl.pallas_call(
        functools.partial(departure_kernel, capacity, 16),
        in_specs=[vmem] * 6,
        out_shape=jax.ShapeDtypeStruct((devices, tall, 2 * records), BF16),
        scratch_shapes=[pltpu.VMEM((2 * tall, 2 * records), F32)],
        compiler_params=pltpu.CompilerParams(vmem_limit_bytes=20 * 1024 * 1024),
        cost_estimate=pl.CostEstimate(
            flops=4 * jac.size, bytes_accessed=jac.size * 2, transcendentals=0
        ),
        name="departures",
    )(dest, valid, states, obs, inv, jac)


STRIDE = 256
NOWHERE = 1 << 20


def point_key(tile, column, count, reach):
    me = lax.axis_index("lon")
    right, left = lax.rem(me + 1, count), lax.rem(me + count - 1, count)
    row = lax.div(column, LANES)
    lon = column - row * LANES
    key = jnp.where(tile == me, lon + reach, NOWHERE)
    key = jnp.where((tile == right) & (lon < reach), lon + LANES + reach, key)
    key = jnp.where((tile == left) & (lon >= LANES - reach), lon - LANES + reach, key)
    return jnp.where(key == NOWHERE, NOWHERE, key + row * STRIDE)


def plan_kernel(records, points, reach, codes_ref, vertical_ref, lon_ref, lat_ref, after_ref, same_ref, info_ref, mixing_ref, table_ref, taps_ref, down, first):
    count = codes_ref.shape[0]
    span, listed = count * records, same_ref.shape[0]
    tile, column = split_codes(codes_ref, records, points)
    key = point_key(tile, column, count, reach)
    for d in range(count):
        down[d * records : (d + 1) * records, :] = jnp.broadcast_to(key[:, d : d + 1], (records, LANES))
    codes = codes_ref[...]
    tile = lax.div(codes, points)
    key = point_key(tile, codes - tile * points, count, reach)
    per = LANES // records
    across = []
    for t in range(span // LANES):
        lane = lane_iota((1, LANES))
        one = key[per * t : per * t + 1, :]
        for h in range(1, per):
            one = jnp.where(
                lane < h * records, one, pltpu.roll(key[per * t + h : per * t + h + 1, :], h * records, 1)
            )
        across.append(one)
    repeats = jnp.zeros((span, LANES), F32)
    for t, one in enumerate(across):
        before = lane_iota((span, LANES)) + t * LANES < row_iota((span, LANES))
        repeats += ((down[...] == one) & before).astype(F32)
    fresh = jnp.sum(repeats, axis=1, keepdims=True) == 0.0
    first[...] = (fresh & (down[...] < NOWHERE)).astype(F32)
    found = jnp.zeros((listed, LANES), jnp.int32)
    for t, one in enumerate(across):
        rank = jnp.sum(jnp.where(down[...] < one, first[...], 0.0), axis=0, keepdims=True)
        rank = jnp.where(one < NOWHERE, rank.astype(jnp.int32), -1)
        same = rank == row_iota((listed, LANES))
        same_ref[:, t * LANES : (t + 1) * LANES] = same.astype(F32).astype(BF16)
        found = jnp.maximum(found, jnp.where(same, one, 0))
    found = jnp.max(found, axis=1, keepdims=True).astype(F32)
    for b in range(listed // LANES):
        wide = jnp.broadcast_to(found[b * LANES : (b + 1) * LANES], (LANES, LANES))
        info_ref[0:1, b * LANES : (b + 1) * LANES] = jnp.transpose(wide)[0:1].astype(jnp.int32)
    starts = jnp.where(down[...] < lane_iota((span, LANES)) * STRIDE, first[...], 0.0)
    info_ref[0:1, listed:] = jnp.sum(starts, axis=0, keepdims=True).astype(jnp.int32)

    features, levels = vertical_ref.shape
    wide = mixing_ref.shape[2]
    tall = mixing_ref.shape[1]
    variables = features // levels
    mixing_ref[...] = jnp.zeros_like(mixing_ref)
    rows = jnp.concatenate([vertical_ref[...].astype(F32), jnp.zeros((features, wide - levels), F32)], axis=1)
    spread = rows
    for v in range(1, variables):
        spread = jnp.where(row_iota(rows.shape) % variables == v, pltpu.roll(rows, v * levels, 1), spread)
    mixing_ref[0] = spread[:tall].astype(BF16)
    mixing_ref[1, 0 : features - tall, :] = spread[tall:].astype(BF16)
    taps = lon_ref.shape[0]
    spare = jnp.zeros((taps, wide - features), F32)
    lon = jnp.concatenate([lon_ref[...], spare], axis=1)
    lon = jnp.concatenate([lon[k : k + 1] for k in reversed(range(taps))] + [jnp.zeros((16 - taps, wide), F32)], axis=0)
    for b in range(8):
        table_ref[16 * b : 16 * (b + 1), :] = pltpu.roll(lon, b, 0) if b else lon
    taps_ref[...] = jnp.concatenate([lat_ref[...], spare], axis=1)


def impact_kernel(records, products_ref, same_ref, near_ref, far_ref, out_ref, terms):
    count, tall, width = products_ref.shape
    listed = same_ref.shape[0]
    lane = lane_iota((tall, width))
    for pair in range(count // 2):
        one = products_ref[2 * pair].astype(F32)
        two = products_ref[2 * pair + 1].astype(F32)
        first = jnp.where(lane < records, one, pltpu.roll(two, records, 1))
        second = jnp.where(lane < records, pltpu.roll(one, records, 1), two)
        terms[0, :, pair * width : (pair + 1) * width] = first.astype(BF16)
        terms[1, :, pair * width : (pair + 1) * width] = second.astype(BF16)
    for h in range(2):
        out_ref[:, h * listed : (h + 1) * listed] = lax.dot_general(
            terms[h], same_ref[...], (((1,), (1,)), ((), ())), preferred_element_type=F32
        ).astype(BF16)


def filter_kernel(block_of, reach, rows, *refs):
    (*lists, vertical_ref, lon_ref, lat_ref, out_ref, mixed, along, mean) = refs
    lists = [(lists[n], lists[n + 1]) for n in range(0, len(lists) // 2 * 2, 2)]
    listed = lists[0][1].shape[1] // vertical_ref.shape[0]
    features = out_ref.shape[0]
    wide = vertical_ref.shape[2]
    height = out_ref.shape[1]
    window = height + 2 * reach
    pitch = along.shape[0] // window
    step = pl.program_id(0)
    base = block_of(step) * height - reach

    @pl.when(step == 0)
    def _():
        for n, (_, impact) in enumerate(lists):
            total = 0.0
            for v in range(vertical_ref.shape[0]):
                total += lax.dot_general(
                    impact[:, v * listed : (v + 1) * listed],
                    vertical_ref[v],
                    (((0,), (0,)), ((), ())),
                    preferred_element_type=F32,
                )
            mixed[n * listed : (n + 1) * listed, :] = total

    along[...] = jnp.zeros_like(along)
    for n, (info, _) in enumerate(lists):
        offset = -base
        if n:
            side = 1 - 2 * lax.rem(lax.axis_index("lat"), 2)
            offset += (rows if n == 1 else -rows) * side
        low = jnp.clip(-offset, 0, rows)
        high = jnp.clip(window - offset, 0, rows)

        def add(s, carry, info=info, n=n, offset=offset):
            key = info[0, s]
            row = lax.shift_right_logical(key, 8) + offset
            place = jnp.bitwise_and(key, STRIDE - 1)
            spot = jnp.bitwise_and(place, 7)
            at = pl.ds(pl.multiple_of(row * pitch + place - spot, 8), 16)
            taps = lon_ref[pl.ds(pl.multiple_of(spot * 16, 16), 16), :]
            along[at, :] += taps * mixed[pl.ds(n * listed + s, 1), :]
            return carry

        lax.fori_loop(info[0, listed + low], info[0, listed + high], add, 0)

    flat = out_ref.reshape(features * height, LANES)
    for t in range(wide // LANES):
        here = slice(t * LANES, (t + 1) * LANES)
        lat = [jnp.broadcast_to(lat_ref[k : k + 1, here], (8, LANES)) for k in range(2 * reach + 1)]

        @pl.loop(0, LANES // 8, unroll=LANES // 8)
        def _(j):
            sums = [None] * height
            for w in range(window):
                part = along[pl.ds(pl.multiple_of(w * pitch + 8 + j * 8, 8), 8), here]
                for row in range(max(0, w - 2 * reach), min(height, w + 1)):
                    term = lat[w - row] * part
                    sums[row] = term if sums[row] is None else sums[row] + term
            for row in range(height):
                mean[row, pl.ds(pl.multiple_of(j * 8, 8), 8), :] = sums[row]

        kept = min(LANES, features - t * LANES)
        for row in range(height):
            turned = jnp.transpose(mean[row])
            flat[pl.ds(t * LANES * height + row, kept, stride=height), :] = turned[0:kept]


def solution(mesh):
    lon_devices, lat_devices = mesh.shape["lon"], mesh.shape["lat"]

    def body(state_field, jacobian, observed, inverse_var, valid_count, destination, column, vertical, lon_taps, lat_taps):
        variables, levels, rows, cols = state_field.shape
        features = variables * levels
        records, channels = jacobian.shape[1], jacobian.shape[-1]
        capacity = max(2, 2 * records // lon_devices)
        reach = lon_taps.shape[-1] // 2
        points = rows * cols
        span = records * lon_devices
        tall = pl.cdiv(features, 32) * 16

        codes = destination.reshape(1, records) * points + column.reshape(1, records)
        codes = jnp.broadcast_to(jnp.pad(codes, ((0, 0), (0, LANES - records))), (lon_devices, LANES))
        codes = lax.all_to_all(codes, "lon", split_axis=0, concat_axis=0, tiled=True)
        laid = lay_state(state_field)

        found = gather_state(codes, laid, records, capacity, rows)
        found_in = lax.all_to_all(
            found.reshape(lon_devices, capacity, found.shape[-1]), "lon", split_axis=0, concat_axis=0, tiled=True
        )
        own = jnp.swapaxes(jacobian.reshape(records, variables, levels, channels), 1, 2).reshape(-1, channels)
        products = departures(
            destination.reshape(1, records),
            valid_count.reshape(1, records),
            found_in.reshape(lon_devices * capacity, found.shape[-1]),
            observed.reshape(records, channels),
            inverse_var.reshape(records, channels),
            fetch(own, found),
            capacity,
            lon_devices,
            tall,
        )
        products_in = lax.all_to_all(products, "lon", split_axis=0, concat_axis=0, tiled=True)

        listed = 3 * lon_devices * capacity
        wide = pl.cdiv(features, LANES) * LANES
        taps = lon_taps.shape[-1]
        vmem, anywhere = pl.BlockSpec(memory_space=pltpu.VMEM), pl.BlockSpec(memory_space=pl.ANY)
        same, info, mixing, lon_table, lat_flat = pl.pallas_call(
            functools.partial(plan_kernel, records, points, reach),
            in_specs=[vmem] * 4 + [anywhere],
            out_shape=(
                jax.ShapeDtypeStruct((listed, span), BF16),
                jax.ShapeDtypeStruct((1, listed + LANES), jnp.int32),
                jax.ShapeDtypeStruct((2, tall, wide), BF16),
                jax.ShapeDtypeStruct((8 * 16, wide), F32),
                jax.ShapeDtypeStruct((taps, wide), F32),
            ),
            scratch_shapes=[pltpu.VMEM((span, LANES), jnp.int32), pltpu.VMEM((span, LANES), F32)],
            compiler_params=pltpu.CompilerParams(vmem_limit_bytes=16 * 1024 * 1024),
            cost_estimate=pl.CostEstimate(flops=8 * span * span, bytes_accessed=span * listed * 2, transcendentals=0),
            name="plan_points",
        )(
            codes,
            jnp.swapaxes(vertical, 0, 1).reshape(features, levels),
            jnp.moveaxis(lon_taps, 2, 0).reshape(taps, features),
            jnp.moveaxis(lat_taps, 2, 0).reshape(taps, features),
            found,
        )
        pairs = [(i, i + 1) for i in range(0, lat_devices - 1, 2)]
        between = [(i, i + 1) for i in range(1, lat_devices - 1, 2)]
        swaps = [[(a, b) for a, b in some] + [(b, a) for a, b in some] for some in (pairs, between)]
        info_far = lax.ppermute(info, "lat", swaps[1])
        info_near = lax.ppermute(info, "lat", swaps[0])

        impact = pl.pallas_call(
            functools.partial(impact_kernel, records),
            in_specs=[vmem] * 2 + [anywhere] * 2,
            out_shape=jax.ShapeDtypeStruct((tall, 2 * listed), BF16),
            scratch_shapes=[pltpu.VMEM((2, tall, span), BF16)],
            compiler_params=pltpu.CompilerParams(vmem_limit_bytes=16 * 1024 * 1024),
            name="impact_columns",
        )(products_in, same, info_near, info_far)
        impact_far = lax.ppermute(impact, "lat", swaps[1])
        impact_near = lax.ppermute(impact, "lat", swaps[0])

        height = 8
        blocks = rows // height
        pitch = LANES + 16

        def filtered(lists, steps, block_of, before, name):
            held = [pl.BlockSpec(memory_space=pltpu.SMEM), pl.BlockSpec(memory_space=pltpu.VMEM)] * (len(lists) // 2)
            held += [pl.BlockSpec(memory_space=pltpu.VMEM)] * 3
            given = list(lists) + [mixing, lon_table, lat_flat]
            kernel = functools.partial(filter_kernel, block_of, reach, rows)
            if before is not None:
                given.append(before)
                held.append(pl.BlockSpec(memory_space=pl.ANY))
                at = len(lists) + 3
                inner = kernel
                kernel = lambda *refs: inner(*refs[:at], *refs[at + 1 :])
            return pl.pallas_call(
                kernel,
                grid=(steps,),
                in_specs=held,
                out_specs=pl.BlockSpec((features, height, cols), lambda s: (0, block_of(s), 0)),
                out_shape=jax.ShapeDtypeStruct((features, rows, cols), F32),
                scratch_shapes=[
                    pltpu.VMEM((len(lists) // 2 * listed, wide), F32),
                    pltpu.VMEM(((height + 2 * reach) * pitch, wide), F32),
                    pltpu.VMEM((height, cols, LANES), F32),
                ],
                input_output_aliases={} if before is None else {len(given) - 1: 0},
                compiler_params=pltpu.CompilerParams(vmem_limit_bytes=24 * 1024 * 1024),
                cost_estimate=pl.CostEstimate(
                    flops=40 * features * rows * cols, bytes_accessed=features * rows * cols * 2, transcendentals=0
                ),
                name=name,
            )(*given)

        inner = filtered([info, impact], blocks - 2, lambda s: s + 1, None, "inner_rows")
        result = filtered(
            [info, impact, info_near, impact_near, info_far, impact_far],
            2,
            lambda s: s * (blocks - 1),
            inner,
            "outer_rows",
        )
        return result.reshape(variables, levels, rows, cols)

    placed = (
        P(None, None, "lat", "lon"),
        P("lat", "lon", None, None, None),
        P("lat", "lon", None),
        P("lat", "lon", None),
        P("lat", "lon"),
        P("lat", "lon", None),
        P("lat", "lon"),
        P(),
        P(),
        P(),
    )
    return jax.shard_map(
        body, mesh=mesh, in_specs=placed, out_specs=P(None, None, "lat", "lon"), check_vma=False
    )
```

```python
import functools

import jax
import jax.numpy as jnp
from jax import lax
from jax.experimental import pallas as pl
from jax.experimental.pallas import tpu as pltpu
from jax.sharding import PartitionSpec as P

LANES = 128
F32 = jnp.float32
BF16 = jnp.bfloat16
STRIDE = 256
NOWHERE = 1 << 20
SOME = 4


def lane_iota(shape):
    return lax.broadcasted_iota(jnp.int32, shape, 1)


def row_iota(shape):
    return lax.broadcasted_iota(jnp.int32, shape, 0)


def earlier_rows(size):
    return (lane_iota((size, size)) < row_iota((size, size))).astype(F32).astype(BF16)


def read_codes(codes_ref):
    count, records = codes_ref.shape
    codes = jnp.bitwise_and(codes_ref[...], NOWHERE - 1)
    return jnp.concatenate([codes, jnp.zeros((count, LANES - records), jnp.int32)], axis=1)


def split_codes(codes_ref, records, points):
    flipped = jnp.transpose(read_codes(codes_ref).astype(F32))[:records].astype(jnp.int32)
    tile = lax.div(flipped, points)
    return tile, flipped - tile * points


def lay_state_kernel(rows, levels, chunk, state_ref, out_ref, state, arrived):
    variables = state_ref.shape[0] // (rows * levels)
    half = rows // 2
    parts = []
    for first in range(0, levels, chunk):
        size = min(chunk, levels - first)
        for v in range(variables):
            start = (v * levels + first) * rows
            here = pl.ds(start, size * rows)
            copy = pltpu.make_async_copy(state_ref.at[here], state.at[here], arrived.at[len(parts)])
            copy.start()
            parts.append((v, first, size, start, copy))
    for v, first, size, start, copy in parts:
        copy.wait()
        for odd in range(2):
            some = state[pl.ds(start + odd, size * half, stride=2), :].astype(BF16)
            out_ref[first : first + size, v * half : (v + 1) * half, odd * LANES : (odd + 1) * LANES] = some.reshape(
                size, half, LANES
            )


def lay_state(state):
    variables, levels, rows, cols = state.shape
    chunk = 72
    return pl.pallas_call(
        functools.partial(lay_state_kernel, rows, levels, chunk),
        in_specs=[pl.BlockSpec(memory_space=pl.ANY)],
        out_shape=jax.ShapeDtypeStruct((levels, variables * rows // 2, 2 * cols), BF16),
        scratch_shapes=[
            pltpu.VMEM((variables * levels * rows, cols), F32),
            pltpu.SemaphoreType.DMA((variables * pl.cdiv(levels, chunk),)),
        ],
        compiler_params=pltpu.CompilerParams(vmem_limit_bytes=24 * 1024 * 1024),
        cost_estimate=pl.CostEstimate(flops=0, bytes_accessed=state.size * 6, transcendentals=0),
        name="lay_state",
    )(state.reshape(variables * levels * rows, cols))


def gather_kernel(records, capacity, rows, codes_ref, state_ref, out_ref, held):
    count = codes_ref.shape[0]
    slots = out_ref.shape[0]
    half = rows // 2
    features = state_ref.shape[0] // half
    me = lax.axis_index("lon")
    tile, column = split_codes(codes_ref, records, rows * LANES)
    mine = (tile == me).astype(F32)
    rank = jnp.dot(earlier_rows(records), mine.astype(BF16), preferred_element_type=F32)
    slot = lane_iota(mine.shape) * capacity + rank.astype(jnp.int32)
    slot = jnp.where(tile == me, slot, -1)
    place = jnp.zeros((records, slots), F32)
    for d in range(count):
        hit = slot[:, d : d + 1] == lane_iota((records, slots))
        place += jnp.where(hit, (column[:, d : d + 1] + 1).astype(F32), 0.0)
    place = jnp.sum(place, axis=0, keepdims=True).astype(jnp.int32) - 1
    row = lax.shift_right_arithmetic(place, LANES.bit_length() - 1)
    in_pair = jnp.where(place < 0, -1, jnp.bitwise_and(place, 2 * LANES - 1))
    pick = (row_iota((2 * LANES, slots)) == in_pair).astype(F32).astype(BF16)
    mask = (row_iota((half, slots)) == lax.shift_right_arithmetic(row, 1)).astype(F32)

    held[...] = jnp.zeros_like(held)
    chunk = 72
    for first in range(0, features, chunk):
        size = min(chunk, features - first)
        found = jnp.dot(
            state_ref[first * half : (first + size) * half, :], pick, preferred_element_type=F32
        )
        found = found.reshape(size, half, slots) * mask[None]
        held[first : first + size, :] = jnp.sum(found, axis=1)
    for t in range(out_ref.shape[1] // LANES):
        out_ref[:, t * LANES : (t + 1) * LANES] = jnp.transpose(
            held[t * LANES : (t + 1) * LANES, :]
        ).astype(BF16)


def gather_state(codes, laid, records, capacity, rows):
    features = laid.shape[0] * laid.shape[1] * 2 // rows
    wide = pl.cdiv(features, LANES) * LANES
    slots = codes.shape[0] * capacity
    vmem = pl.BlockSpec(memory_space=pltpu.VMEM)
    return pl.pallas_call(
        functools.partial(gather_kernel, records, capacity, rows),
        in_specs=[vmem, vmem],
        out_shape=jax.ShapeDtypeStruct((slots, wide), BF16),
        scratch_shapes=[pltpu.VMEM((wide, slots), F32)],
        compiler_params=pltpu.CompilerParams(vmem_limit_bytes=12 * 1024 * 1024),
        cost_estimate=pl.CostEstimate(flops=2 * laid.size * slots, bytes_accessed=laid.size * 2, transcendentals=0),
        name="gather_state",
    )(codes, laid.reshape(-1, laid.shape[2]))


def to_column(row):
    size = row.shape[1]
    wide = jnp.broadcast_to(row, (size, size))
    return jnp.sum(jnp.where(row_iota(wide.shape) == lane_iota(wide.shape), wide, 0), axis=1, keepdims=True)


def fetch_kernel(from_ref, after_ref, out_ref, arrived):
    copy = pltpu.make_async_copy(from_ref.at[pl.ds(0, out_ref.shape[0])], out_ref, arrived)
    copy.start()
    copy.wait()


def fetch(array, after, rows):
    anywhere = pl.BlockSpec(memory_space=pl.ANY)
    return pl.pallas_call(
        fetch_kernel,
        in_specs=[anywhere, anywhere],
        out_specs=pl.BlockSpec(memory_space=pltpu.VMEM),
        out_shape=jax.ShapeDtypeStruct((rows, array.shape[1]), array.dtype),
        scratch_shapes=[pltpu.SemaphoreType.DMA],
        compiler_params=pltpu.CompilerParams(vmem_limit_bytes=12 * 1024 * 1024),
        cost_estimate=pl.CostEstimate(flops=0, bytes_accessed=rows * array.shape[1] * 4, transcendentals=0),
        name="fetch_jacobian",
    )(array, after)


def first_departures(capacity, group, features, dest_ref, valid_ref, states_ref, obs_ref, inv_ref, jac_ref, after_ref, total_ref, columns_ref, weight_ref):
    records = dest_ref.shape[1]
    slots = states_ref.shape[0]
    channels = jac_ref.shape[1]
    dest = to_column(dest_ref[...])
    named = (dest == lane_iota((records, LANES))).astype(F32)
    before = jnp.dot(earlier_rows(records), named.astype(BF16), preferred_element_type=F32)
    rank = jnp.sum(before * named, axis=1, keepdims=True).astype(jnp.int32)
    chosen = (dest * capacity + rank == lane_iota((records, slots))).astype(F32).astype(BF16)
    columns = jnp.dot(chosen, states_ref[...], preferred_element_type=F32)
    alive = lane_iota((records, channels)) < to_column(valid_ref[...])
    columns_ref[...] = columns
    weight_ref[...] = jnp.where(alive, inv_ref[...].astype(F32), 0.0)
    total_ref[...] = jnp.zeros_like(total_ref)
    product_groups(group, features, 0, columns_ref, weight_ref, obs_ref, jac_ref, total_ref)


def last_departures(group, features, done, columns_ref, weight_ref, obs_ref, jac_ref, before_ref, out_ref, total):
    records = obs_ref.shape[0]
    total[...] = before_ref[...]
    product_groups(group, features, done, columns_ref, weight_ref, obs_ref, jac_ref, total)
    half = total.shape[0] // 2
    lane = lane_iota((half, LANES))
    low = jnp.where(lane < records, total[0:half, :], pltpu.roll(total[half:, :], records, 1)).astype(BF16)
    for t in range(out_ref.shape[0]):
        out_ref[t] = low


def product_groups(group, features, done, columns_ref, weight_ref, obs_ref, jac_ref, total):
    channels = jac_ref.shape[1]
    part = group // 2
    span = part * features
    tiles, skip = divmod(features, LANES)
    wide = columns_ref.shape[1]
    reach = pl.cdiv(skip * (part - 1) + features, LANES)
    row = row_iota((group, LANES))
    index = jnp.bitwise_and(row, part - 1)
    for g in range(done, jac_ref.shape[0] // (group * features)):
        first = g * group * features
        mine = columns_ref[g * group : (g + 1) * group, :]
        if reach * LANES > wide:
            mine = jnp.concatenate([mine, jnp.zeros((group, reach * LANES - wide), F32)], axis=1)
        bit = 1
        while bit < part:
            moved = pltpu.roll(mine, skip * bit, 1)
            mine = jnp.where(jnp.bitwise_and(row_iota(mine.shape), bit) > 0, moved, mine)
            bit *= 2
        spread = []
        for t in range(pl.cdiv(span, LANES)):
            piece = jnp.zeros((group, LANES), F32)
            for r in range(part):
                at = t - tiles * r
                if 0 <= at < reach:
                    piece = jnp.where(index == r, mine[:, at * LANES : (at + 1) * LANES], piece)
            spread.append(piece.astype(BF16))
        spread = jnp.concatenate(spread, axis=1)[:, :span]
        pair = jnp.concatenate([jac_ref[first : first + span, :], jac_ref[first + span : first + 2 * span, :]], axis=1)
        both = jnp.dot(spread, pair, preferred_element_type=F32)
        model = jnp.where(row < part, both[:, :channels], both[:, channels:])
        own = slice(g * group, (g + 1) * group)
        misfit = weight_ref[own, :] * (model - obs_ref[own, :].astype(F32))
        low = misfit.astype(BF16).astype(F32)
        for r in range(part):
            against = jnp.concatenate([jnp.where(row == r, low, 0.0), jnp.where(row == r + part, low, 0.0)], axis=1)
            start = first + r * features
            lead = start % 16
            size = pl.cdiv(features + lead, 16) * 16
            rows = [jac_ref[start - lead + h * span : start - lead + h * span + size, :] for h in range(2)]
            one = lax.dot_general(
                jnp.concatenate(rows, axis=1),
                against.astype(BF16),
                (((1,), (1,)), ((), ())),
                preferred_element_type=F32,
            )
            one = one[lead : lead + features]
            sums = one if r == 0 else sums + one
        total[0:features, g * group : (g + 1) * group] = sums


def departures(dest, valid, states, obs, inv, jac, after, capacity, devices, tall):
    records, channels = obs.shape
    features = jac.shape[0] // records
    group = 16
    done = records // group // 2
    vmem, anywhere = pl.BlockSpec(memory_space=pltpu.VMEM), pl.BlockSpec(memory_space=pl.ANY)
    params = pltpu.CompilerParams(vmem_limit_bytes=16 * 1024 * 1024)
    cost = pl.CostEstimate(flops=3_000_000_000, bytes_accessed=jac.size, transcendentals=0)
    total, columns, weight = pl.pallas_call(
        functools.partial(first_departures, capacity, group, features),
        in_specs=[vmem] * 6 + [anywhere],
        out_shape=(
            jax.ShapeDtypeStruct((2 * tall, 2 * records), F32),
            jax.ShapeDtypeStruct((records, states.shape[1]), F32),
            jax.ShapeDtypeStruct((records, channels), F32),
        ),
        compiler_params=params,
        cost_estimate=cost,
        name="first_departures",
    )(dest, valid, states, obs, inv, fetch(jac, after, done * group * features), after)
    return pl.pallas_call(
        functools.partial(last_departures, group, features, done),
        in_specs=[vmem] * 5,
        out_shape=jax.ShapeDtypeStruct((devices, tall, 2 * records), BF16),
        scratch_shapes=[pltpu.VMEM((2 * tall, 2 * records), F32)],
        compiler_params=params,
        cost_estimate=cost,
        name="last_departures",
    )(columns, weight, obs, jac, total)


def point_key(tile, column, count, reach):
    me = lax.axis_index("lon")
    right, left = lax.rem(me + 1, count), lax.rem(me + count - 1, count)
    row = lax.div(column, LANES)
    lon = column - row * LANES
    key = jnp.where(tile == me, lon + reach, NOWHERE)
    key = jnp.where((tile == right) & (lon < reach), lon + LANES + reach, key)
    key = jnp.where((tile == left) & (lon >= LANES - reach), lon - LANES + reach, key)
    return jnp.where(key == NOWHERE, NOWHERE, key + row * STRIDE)


def plan_kernel(records, points, reach, codes_ref, vertical_ref, lon_ref, lat_ref, after_ref, same_ref, info_ref, mixing_ref, table_ref, taps_ref, down, first):
    count = codes_ref.shape[0]
    span, listed = count * records, same_ref.shape[0]
    tile, column = split_codes(codes_ref, records, points)
    key = point_key(tile, column, count, reach)
    for d in range(count):
        down[d * records : (d + 1) * records, :] = jnp.broadcast_to(key[:, d : d + 1], (records, LANES))
    codes = read_codes(codes_ref)
    tile = lax.div(codes, points)
    key = point_key(tile, codes - tile * points, count, reach)
    per = LANES // records
    across = []
    for t in range(span // LANES):
        lane = lane_iota((1, LANES))
        one = key[per * t : per * t + 1, :]
        for h in range(1, per):
            one = jnp.where(
                lane < h * records, one, pltpu.roll(key[per * t + h : per * t + h + 1, :], h * records, 1)
            )
        across.append(one)
    repeats = jnp.zeros((span, LANES), F32)
    for t, one in enumerate(across):
        before = lane_iota((span, LANES)) + t * LANES < row_iota((span, LANES))
        repeats += ((down[...] == one) & before).astype(F32)
    fresh = jnp.sum(repeats, axis=1, keepdims=True) == 0.0
    first[...] = (fresh & (down[...] < NOWHERE)).astype(F32)
    found = jnp.zeros((listed, LANES), jnp.int32)
    for t, one in enumerate(across):
        rank = jnp.sum(jnp.where(down[...] < one, first[...], 0.0), axis=0, keepdims=True)
        rank = jnp.where(one < NOWHERE, rank.astype(jnp.int32), -1)
        same = rank == row_iota((listed, LANES))
        same_ref[:, t * LANES : (t + 1) * LANES] = same.astype(F32).astype(BF16)
        found = jnp.maximum(found, jnp.where(same, one, 0))
    found = jnp.max(found, axis=1, keepdims=True).astype(F32)
    for b in range(listed // LANES):
        wide = jnp.broadcast_to(found[b * LANES : (b + 1) * LANES], (LANES, LANES))
        info_ref[0:1, b * LANES : (b + 1) * LANES] = jnp.transpose(wide)[0:1].astype(jnp.int32)
    starts = jnp.where(down[...] < lane_iota((span, LANES)) * STRIDE, first[...], 0.0)
    info_ref[0:1, listed:] = jnp.sum(starts, axis=0, keepdims=True).astype(jnp.int32)

    features, levels = vertical_ref.shape
    wide = mixing_ref.shape[2]
    tall = mixing_ref.shape[1]
    variables = features // levels
    mixing_ref[...] = jnp.zeros_like(mixing_ref)
    rows = jnp.concatenate([vertical_ref[...].astype(F32), jnp.zeros((features, wide - levels), F32)], axis=1)
    spread = rows
    for v in range(1, variables):
        spread = jnp.where(row_iota(rows.shape) % variables == v, pltpu.roll(rows, v * levels, 1), spread)
    mixing_ref[0] = spread[:tall].astype(BF16)
    mixing_ref[1, 0 : features - tall, :] = spread[tall:].astype(BF16)
    taps = lon_ref.shape[0]
    spare = jnp.zeros((taps, wide - features), F32)
    lon = jnp.concatenate([lon_ref[...], spare], axis=1)
    lon = jnp.concatenate([lon[k : k + 1] for k in reversed(range(taps))] + [jnp.zeros((16 - taps, wide), F32)], axis=0)
    for b in range(8):
        table_ref[16 * b : 16 * (b + 1), :] = pltpu.roll(lon, b, 0) if b else lon
    taps_ref[...] = jnp.concatenate([lat_ref[...], spare], axis=1)


def impact_kernel(records, products_ref, same_ref, near_ref, far_ref, out_ref, terms):
    count, tall, width = products_ref.shape
    listed = same_ref.shape[0]
    lane = lane_iota((tall, width))
    for pair in range(count // 2):
        one = products_ref[2 * pair].astype(F32)
        two = products_ref[2 * pair + 1].astype(F32)
        first = jnp.where(lane < records, one, pltpu.roll(two, records, 1))
        second = jnp.where(lane < records, pltpu.roll(one, records, 1), two)
        terms[0, :, pair * width : (pair + 1) * width] = first.astype(BF16)
        terms[1, :, pair * width : (pair + 1) * width] = second.astype(BF16)
    for h in range(2):
        out_ref[:, h * listed : (h + 1) * listed] = lax.dot_general(
            terms[h], same_ref[...], (((1,), (1,)), ((), ())), preferred_element_type=F32
        ).astype(BF16)


def filter_kernel(block_of, reach, rows, *refs):
    (*lists, vertical_ref, lon_ref, lat_ref, out_ref, mixed, along, mean, ready, sent) = refs
    lists = [(lists[n], lists[n + 1]) for n in range(0, len(lists) // 2 * 2, 2)]
    listed = lists[0][1].shape[1] // vertical_ref.shape[0]
    features = out_ref.shape[0]
    wide = vertical_ref.shape[2]
    height = ready.shape[2]
    window = height + 2 * reach
    pitch = along.shape[0] // window
    step = pl.program_id(0)
    base = block_of(step) * height - reach

    @pl.when(step == 0)
    def _():
        along[...] = jnp.zeros_like(along)
        for n, (info, impact) in enumerate(lists):
            for part in range(0, listed, LANES):

                @pl.when(info[0, listed + rows] > part)
                def _(n=n, impact=impact, part=part):
                    total = 0.0
                    for h in range(vertical_ref.shape[0]):
                        total += lax.dot_general(
                            impact[:, h * listed + part : h * listed + part + LANES],
                            vertical_ref[h],
                            (((0,), (0,)), ((), ())),
                            preferred_element_type=F32,
                        )
                    mixed[n * listed + part : n * listed + part + LANES, :] = total

    for n, (info, _) in enumerate(lists):
        offset = -base
        if n:
            side = 1 - 2 * lax.rem(lax.axis_index("lat"), 2)
            offset += (rows if n == 1 else -rows) * side
        low = jnp.clip(-offset, 0, rows)
        high = jnp.clip(window - offset, 0, rows)

        start, stop = info[0, listed + low], info[0, listed + high]

        def add_some(i, carry, info=info, n=n, offset=offset, start=start, stop=stop):
            pieces = []
            for u in range(SOME):
                here = start + i * SOME + u
                live = here < stop
                here = jnp.where(live, here, start)
                key = info[0, here]
                row = lax.shift_right_logical(key, 8) + offset
                place = jnp.bitwise_and(key, STRIDE - 1)
                spot = jnp.bitwise_and(place, 7)
                at = pl.ds(pl.multiple_of(row * pitch + place - spot, 8), 16)
                taps = lon_ref[pl.ds(pl.multiple_of(spot * 16, 16), 16), :]
                column = mixed[pl.ds(n * listed + here, 1), :] * jnp.where(live, 1.0, 0.0)
                pieces.append((at, taps * column))
            for at, piece in pieces:
                along[at, :] += piece
            return carry

        lax.fori_loop(0, lax.div(stop - start + SOME - 1, SOME), add_some, 0)

    flat = ready.reshape(ready.shape[0] * features * height, LANES)

    def leave(at, t):
        here = pl.ds(t * LANES, min(LANES, features - t * LANES))
        there = pl.ds(pl.multiple_of(block_of(at) * height, height), height)
        return pltpu.make_async_copy(ready.at[at, here], out_ref.at[here, there], sent.at[at, t])

    for t in range(wide // LANES):
        here = slice(t * LANES, (t + 1) * LANES)
        lat = [jnp.broadcast_to(lat_ref[k : k + 1, here], (8, LANES)) for k in range(2 * reach + 1)]

        for j in range(LANES // 8):
            sums = [None] * height
            for w in range(window):
                spot = pl.ds(w * pitch + 8 + j * 8, 8)
                part = along[spot, here]
                along[spot, here] = jnp.zeros_like(part)
                for row in range(max(0, w - 2 * reach), min(height, w + 1)):
                    term = lat[w - row] * part
                    sums[row] = term if sums[row] is None else sums[row] + term
            for row in range(height):
                mean[t % 2, row, j * 8 : (j + 1) * 8, :] = sums[row]

        kept = min(LANES, features - t * LANES)
        for row in range(height):
            turned = jnp.transpose(mean[t % 2, row])
            flat[pl.ds((step * features + t * LANES) * height + row, kept, stride=height), :] = turned[0:kept]
        leave(step, t).start()

    @pl.when(step == ready.shape[0] - 1)
    def _():
        for at in range(ready.shape[0]):
            for t in range(wide // LANES):
                leave(at, t).wait()


def solution(mesh):
    lon_devices, lat_devices = mesh.shape["lon"], mesh.shape["lat"]

    def body(state_field, jacobian, observed, inverse_var, valid_count, destination, column, vertical, lon_taps, lat_taps):
        variables, levels, rows, cols = state_field.shape
        features = variables * levels
        records, channels = jacobian.shape[1], jacobian.shape[-1]
        capacity = max(2, 2 * records // lon_devices)
        reach = lon_taps.shape[-1] // 2
        points = rows * cols
        span = records * lon_devices
        tall = pl.cdiv(features, 32) * 16

        codes = destination.reshape(1, 1, records) * points + column.reshape(1, 1, records)
        codes = codes + lax.broadcasted_iota(jnp.int32, (lon_devices, 1, records), 0) * NOWHERE
        codes = lax.all_to_all(codes, "lon", split_axis=0, concat_axis=0, tiled=True)
        codes = codes.reshape(lon_devices, records)
        laid = lay_state(state_field)

        found = gather_state(codes, laid, records, capacity, rows)
        found_in = lax.all_to_all(
            found.reshape(lon_devices, capacity, found.shape[-1]), "lon", split_axis=0, concat_axis=0, tiled=True
        )
        listed = 3 * lon_devices * capacity
        wide = pl.cdiv(features, LANES) * LANES
        taps = lon_taps.shape[-1]
        vmem, anywhere = pl.BlockSpec(memory_space=pltpu.VMEM), pl.BlockSpec(memory_space=pl.ANY)
        same, info, mixing, lon_table, lat_flat = pl.pallas_call(
            functools.partial(plan_kernel, records, points, reach),
            in_specs=[vmem] * 4 + [anywhere],
            out_shape=(
                jax.ShapeDtypeStruct((listed, span), BF16),
                jax.ShapeDtypeStruct((1, listed + LANES), jnp.int32),
                jax.ShapeDtypeStruct((2, tall, wide), BF16),
                jax.ShapeDtypeStruct((8 * 16, wide), F32),
                jax.ShapeDtypeStruct((taps, wide), F32),
            ),
            scratch_shapes=[pltpu.VMEM((span, LANES), jnp.int32), pltpu.VMEM((span, LANES), F32)],
            compiler_params=pltpu.CompilerParams(vmem_limit_bytes=16 * 1024 * 1024),
            cost_estimate=pl.CostEstimate(flops=8 * span * span, bytes_accessed=span * listed * 2, transcendentals=0),
            name="plan_points",
        )(
            codes,
            jnp.swapaxes(vertical, 0, 1).reshape(features, levels),
            jnp.moveaxis(lon_taps, 2, 0).reshape(taps, features),
            jnp.moveaxis(lat_taps, 2, 0).reshape(taps, features),
            found,
        )
        own = jnp.swapaxes(jacobian.reshape(records, variables, levels, channels), 1, 2).reshape(-1, channels)
        products = departures(
            destination.reshape(1, records),
            valid_count.reshape(1, records),
            found_in.reshape(lon_devices * capacity, found.shape[-1]),
            observed.reshape(records, channels),
            inverse_var.reshape(records, channels),
            own,
            info,
            capacity,
            lon_devices,
            tall,
        )
        products_in = lax.all_to_all(products, "lon", split_axis=0, concat_axis=0, tiled=True)

        pairs = [(i, i + 1) for i in range(0, lat_devices - 1, 2)]
        between = [(i, i + 1) for i in range(1, lat_devices - 1, 2)]
        swaps = [[(a, b) for a, b in some] + [(b, a) for a, b in some] for some in (pairs, between)]
        info_near = lax.ppermute(info, "lat", swaps[0])
        info_far = lax.ppermute(info, "lat", swaps[1])

        impact = pl.pallas_call(
            functools.partial(impact_kernel, records),
            in_specs=[vmem] * 2 + [anywhere] * 2,
            out_shape=jax.ShapeDtypeStruct((tall, 2 * listed), BF16),
            scratch_shapes=[pltpu.VMEM((2, tall, span), BF16)],
            compiler_params=pltpu.CompilerParams(vmem_limit_bytes=16 * 1024 * 1024),
            name="impact_columns",
        )(products_in, same, info_near, info_far)
        impact_near = lax.ppermute(impact, "lat", swaps[0])
        impact_far = lax.ppermute(impact, "lat", swaps[1])

        height = 8
        blocks = rows // height
        pitch = LANES + 16

        def filtered(lists, steps, block_of, before, name):
            held = [pl.BlockSpec(memory_space=pltpu.SMEM), pl.BlockSpec(memory_space=pltpu.VMEM)] * (len(lists) // 2)
            held += [pl.BlockSpec(memory_space=pltpu.VMEM)] * 3
            given = list(lists) + [mixing, lon_table, lat_flat]
            kernel = functools.partial(filter_kernel, block_of, reach, rows)
            if before is not None:
                given.append(before)
                held.append(pl.BlockSpec(memory_space=pl.ANY))
                at = len(lists) + 3
                inner = kernel
                kernel = lambda *refs: inner(*refs[:at], *refs[at + 1 :])
            return pl.pallas_call(
                kernel,
                grid=(steps,),
                in_specs=held,
                out_specs=pl.BlockSpec(memory_space=pl.ANY),
                out_shape=jax.ShapeDtypeStruct((features, rows, cols), F32),
                scratch_shapes=[
                    pltpu.VMEM((len(lists) // 2 * listed, wide), F32),
                    pltpu.VMEM(((height + 2 * reach) * pitch, wide), F32),
                    pltpu.VMEM((2, height, cols, LANES), F32),
                    pltpu.VMEM((steps, features, height, cols), F32),
                    pltpu.SemaphoreType.DMA((steps, wide // LANES)),
                ],
                input_output_aliases={} if before is None else {len(given) - 1: 0},
                compiler_params=pltpu.CompilerParams(vmem_limit_bytes=24 * 1024 * 1024),
                cost_estimate=pl.CostEstimate(
                    flops=40 * features * rows * cols, bytes_accessed=features * rows * cols * 2, transcendentals=0
                ),
                name=name,
            )(*given)

        inner = filtered([info, impact], blocks - 2, lambda s: s + 1, None, "inner_rows")
        result = filtered(
            [info, impact, info_near, impact_near, info_far, impact_far],
            2,
            lambda s: s * (blocks - 1),
            inner,
            "outer_rows",
        )
        return result.reshape(variables, levels, rows, cols)

    placed = (
        P(None, None, "lat", "lon"),
        P("lat", "lon", None, None, None),
        P("lat", "lon", None),
        P("lat", "lon", None),
        P("lat", "lon"),
        P("lat", "lon", None),
        P("lat", "lon"),
        P(),
        P(),
        P(),
    )
    return jax.shard_map(
        body, mesh=mesh, in_specs=placed, out_specs=P(None, None, "lat", "lon"), check_vma=False
    )
```

```python
import functools

import jax
import jax.numpy as jnp
from jax import lax
from jax.experimental import pallas as pl
from jax.experimental.pallas import tpu as pltpu
from jax.sharding import PartitionSpec as P

LANES = 128
F32 = jnp.float32
BF16 = jnp.bfloat16
STRIDE = 256
NOWHERE = 1 << 20
SOME = 4


def lane_iota(shape):
    return lax.broadcasted_iota(jnp.int32, shape, 1)


def row_iota(shape):
    return lax.broadcasted_iota(jnp.int32, shape, 0)


def earlier_rows(size):
    return (lane_iota((size, size)) < row_iota((size, size))).astype(F32).astype(BF16)


def read_codes(codes_ref):
    count, records = codes_ref.shape
    codes = jnp.bitwise_and(codes_ref[...], NOWHERE - 1)
    return jnp.concatenate([codes, jnp.zeros((count, LANES - records), jnp.int32)], axis=1)


def split_codes(codes_ref, records, points):
    flipped = jnp.transpose(read_codes(codes_ref).astype(F32))[:records].astype(jnp.int32)
    tile = lax.div(flipped, points)
    return tile, flipped - tile * points


def lay_state_kernel(rows, levels, chunk, state_ref, out_ref, state, arrived):
    variables = state_ref.shape[0] // (rows * levels)
    half = rows // 2
    parts = []
    for first in range(0, levels, chunk):
        size = min(chunk, levels - first)
        for v in range(variables):
            start = (v * levels + first) * rows
            here = pl.ds(start, size * rows)
            copy = pltpu.make_async_copy(state_ref.at[here], state.at[here], arrived.at[len(parts)])
            copy.start()
            parts.append((v, first, size, start, copy))
    for v, first, size, start, copy in parts:
        copy.wait()
        for odd in range(2):
            some = state[pl.ds(start + odd, size * half, stride=2), :].astype(BF16)
            out_ref[first : first + size, v * half : (v + 1) * half, odd * LANES : (odd + 1) * LANES] = some.reshape(
                size, half, LANES
            )


def lay_state(state):
    variables, levels, rows, cols = state.shape
    chunk = 72
    return pl.pallas_call(
        functools.partial(lay_state_kernel, rows, levels, chunk),
        in_specs=[pl.BlockSpec(memory_space=pl.ANY)],
        out_shape=jax.ShapeDtypeStruct((levels, variables * rows // 2, 2 * cols), BF16),
        scratch_shapes=[
            pltpu.VMEM((variables * levels * rows, cols), F32),
            pltpu.SemaphoreType.DMA((variables * pl.cdiv(levels, chunk),)),
        ],
        compiler_params=pltpu.CompilerParams(vmem_limit_bytes=24 * 1024 * 1024),
        cost_estimate=pl.CostEstimate(flops=0, bytes_accessed=state.size * 6, transcendentals=0),
        name="lay_state",
    )(state.reshape(variables * levels * rows, cols))


def gather_kernel(records, capacity, rows, codes_ref, state_ref, out_ref, held):
    count = codes_ref.shape[0]
    slots = out_ref.shape[0]
    half = rows // 2
    features = state_ref.shape[0] // half
    me = lax.axis_index("lon")
    tile, column = split_codes(codes_ref, records, rows * LANES)
    mine = (tile == me).astype(F32)
    rank = jnp.dot(earlier_rows(records), mine.astype(BF16), preferred_element_type=F32)
    slot = lane_iota(mine.shape) * capacity + rank.astype(jnp.int32)
    slot = jnp.where(tile == me, slot, -1)
    place = jnp.zeros((records, slots), F32)
    for d in range(count):
        hit = slot[:, d : d + 1] == lane_iota((records, slots))
        place += jnp.where(hit, (column[:, d : d + 1] + 1).astype(F32), 0.0)
    place = jnp.sum(place, axis=0, keepdims=True).astype(jnp.int32) - 1
    row = lax.shift_right_arithmetic(place, LANES.bit_length() - 1)
    in_pair = jnp.where(place < 0, -1, jnp.bitwise_and(place, 2 * LANES - 1))
    pick = (row_iota((2 * LANES, slots)) == in_pair).astype(F32).astype(BF16)
    mask = (row_iota((half, slots)) == lax.shift_right_arithmetic(row, 1)).astype(F32)

    held[...] = jnp.zeros_like(held)
    chunk = 72
    for first in range(0, features, chunk):
        size = min(chunk, features - first)
        found = jnp.dot(
            state_ref[first * half : (first + size) * half, :], pick, preferred_element_type=F32
        )
        found = found.reshape(size, half, slots) * mask[None]
        held[first : first + size, :] = jnp.sum(found, axis=1)
    for t in range(out_ref.shape[1] // LANES):
        out_ref[:, t * LANES : (t + 1) * LANES] = jnp.transpose(
            held[t * LANES : (t + 1) * LANES, :]
        ).astype(BF16)


def gather_state(codes, laid, records, capacity, rows):
    features = laid.shape[0] * laid.shape[1] * 2 // rows
    wide = pl.cdiv(features, LANES) * LANES
    slots = codes.shape[0] * capacity
    vmem = pl.BlockSpec(memory_space=pltpu.VMEM)
    return pl.pallas_call(
        functools.partial(gather_kernel, records, capacity, rows),
        in_specs=[vmem, vmem],
        out_shape=jax.ShapeDtypeStruct((slots, wide), BF16),
        scratch_shapes=[pltpu.VMEM((wide, slots), F32)],
        compiler_params=pltpu.CompilerParams(vmem_limit_bytes=12 * 1024 * 1024),
        cost_estimate=pl.CostEstimate(flops=2 * laid.size * slots, bytes_accessed=laid.size * 2, transcendentals=0),
        name="gather_state",
    )(codes, laid.reshape(-1, laid.shape[2]))


def to_column(row):
    size = row.shape[1]
    wide = jnp.broadcast_to(row, (size, size))
    return jnp.sum(jnp.where(row_iota(wide.shape) == lane_iota(wide.shape), wide, 0), axis=1, keepdims=True)


def fetch_kernel(from_ref, after_ref, out_ref, arrived):
    copy = pltpu.make_async_copy(from_ref.at[pl.ds(0, out_ref.shape[0])], out_ref, arrived)
    copy.start()
    copy.wait()


def fetch(array, after, rows):
    anywhere = pl.BlockSpec(memory_space=pl.ANY)
    return pl.pallas_call(
        fetch_kernel,
        in_specs=[anywhere, anywhere],
        out_specs=pl.BlockSpec(memory_space=pltpu.VMEM),
        out_shape=jax.ShapeDtypeStruct((rows, array.shape[1]), array.dtype),
        scratch_shapes=[pltpu.SemaphoreType.DMA],
        compiler_params=pltpu.CompilerParams(vmem_limit_bytes=12 * 1024 * 1024),
        cost_estimate=pl.CostEstimate(flops=0, bytes_accessed=rows * array.shape[1] * 4, transcendentals=0),
        name="fetch_jacobian",
    )(array, after)


def first_departures(group, features, chosen_ref, states_ref, weight_ref, obs_ref, jac_ref, after_ref, total_ref, columns_ref):
    columns_ref[...] = jnp.dot(chosen_ref[...], states_ref[...], preferred_element_type=F32)
    total_ref[...] = jnp.zeros_like(total_ref)
    product_groups(group, features, 0, columns_ref, weight_ref, obs_ref, jac_ref, total_ref)


def last_departures(group, features, done, columns_ref, weight_ref, obs_ref, jac_ref, before_ref, out_ref, total):
    records = obs_ref.shape[0]
    total[...] = before_ref[...]
    product_groups(group, features, done, columns_ref, weight_ref, obs_ref, jac_ref, total)
    half = total.shape[0] // 2
    lane = lane_iota((half, LANES))
    low = jnp.where(lane < records, total[0:half, :], pltpu.roll(total[half:, :], records, 1)).astype(BF16)
    for t in range(out_ref.shape[0]):
        out_ref[t] = low


def product_groups(group, features, done, columns_ref, weight_ref, obs_ref, jac_ref, total):
    channels = jac_ref.shape[1]
    part = group // 2
    span = part * features
    tiles, skip = divmod(features, LANES)
    wide = columns_ref.shape[1]
    reach = pl.cdiv(skip * (part - 1) + features, LANES)
    row = row_iota((group, LANES))
    index = jnp.bitwise_and(row, part - 1)
    lows = {}
    for g in range(done, jac_ref.shape[0] // (group * features)):
        first = g * group * features
        mine = columns_ref[g * group : (g + 1) * group, :]
        if reach * LANES > wide:
            mine = jnp.concatenate([mine, jnp.zeros((group, reach * LANES - wide), F32)], axis=1)
        bit = 1
        while bit < part:
            moved = pltpu.roll(mine, skip * bit, 1)
            mine = jnp.where(jnp.bitwise_and(row_iota(mine.shape), bit) > 0, moved, mine)
            bit *= 2
        spread = []
        for t in range(pl.cdiv(span, LANES)):
            piece = jnp.zeros((group, LANES), F32)
            for r in range(part):
                at = t - tiles * r
                if 0 <= at < reach:
                    piece = jnp.where(index == r, mine[:, at * LANES : (at + 1) * LANES], piece)
            spread.append(piece.astype(BF16))
        spread = jnp.concatenate(spread, axis=1)[:, :span]
        pair = jnp.concatenate([jac_ref[first : first + span, :], jac_ref[first + span : first + 2 * span, :]], axis=1)
        both = jnp.dot(spread, pair, preferred_element_type=F32)
        model = jnp.where(row < part, both[:, :channels], both[:, channels:])
        own = slice(g * group, (g + 1) * group)
        misfit = weight_ref[own, :] * (model - obs_ref[own, :].astype(F32))
        lows[g] = misfit.astype(BF16).astype(F32)
    for g, low in lows.items():
        first = g * group * features
        for r in range(part):
            against = jnp.concatenate([jnp.where(row == r, low, 0.0), jnp.where(row == r + part, low, 0.0)], axis=1)
            start = first + r * features
            lead = start % 16
            size = pl.cdiv(features + lead, 16) * 16
            rows = [jac_ref[start - lead + h * span : start - lead + h * span + size, :] for h in range(2)]
            one = lax.dot_general(
                jnp.concatenate(rows, axis=1),
                against.astype(BF16),
                (((1,), (1,)), ((), ())),
                preferred_element_type=F32,
            )
            one = one[lead : lead + features]
            sums = one if r == 0 else sums + one
        total[0:features, g * group : (g + 1) * group] = sums


def departures(chosen, states, weight, obs, jac, after, devices, tall):
    records, channels = obs.shape
    features = jac.shape[0] // records
    group = 16
    done = records // group // 2
    vmem, anywhere = pl.BlockSpec(memory_space=pltpu.VMEM), pl.BlockSpec(memory_space=pl.ANY)
    params = pltpu.CompilerParams(vmem_limit_bytes=16 * 1024 * 1024)
    cost = pl.CostEstimate(flops=3_000_000_000, bytes_accessed=jac.size, transcendentals=0)
    total, columns = pl.pallas_call(
        functools.partial(first_departures, group, features),
        in_specs=[vmem] * 5 + [anywhere],
        out_shape=(
            jax.ShapeDtypeStruct((2 * tall, 2 * records), F32),
            jax.ShapeDtypeStruct((records, states.shape[1]), F32),
        ),
        compiler_params=params,
        cost_estimate=cost,
        name="first_departures",
    )(chosen, states, weight, obs, fetch(jac, after, done * group * features), after)
    return pl.pallas_call(
        functools.partial(last_departures, group, features, done),
        in_specs=[vmem] * 5,
        out_shape=jax.ShapeDtypeStruct((devices, tall, 2 * records), BF16),
        scratch_shapes=[pltpu.VMEM((2 * tall, 2 * records), F32)],
        compiler_params=params,
        cost_estimate=cost,
        name="last_departures",
    )(columns, weight, obs, jac, total)


def point_key(tile, column, count, reach):
    me = lax.axis_index("lon")
    right, left = lax.rem(me + 1, count), lax.rem(me + count - 1, count)
    row = lax.div(column, LANES)
    lon = column - row * LANES
    key = jnp.where(tile == me, lon + reach, NOWHERE)
    key = jnp.where((tile == right) & (lon < reach), lon + LANES + reach, key)
    key = jnp.where((tile == left) & (lon >= LANES - reach), lon - LANES + reach, key)
    return jnp.where(key == NOWHERE, NOWHERE, key + row * STRIDE)


def plan_kernel(records, points, reach, capacity, codes_ref, dest_ref, valid_ref, inv_ref, vertical_ref, lon_ref, lat_ref, after_ref, chosen_ref, weight_ref, same_ref, info_ref, mixing_ref, table_ref, taps_ref, down, first):
    count = codes_ref.shape[0]
    span, listed = count * records, same_ref.shape[0]
    tile, column = split_codes(codes_ref, records, points)
    key = point_key(tile, column, count, reach)
    for d in range(count):
        down[d * records : (d + 1) * records, :] = jnp.broadcast_to(key[:, d : d + 1], (records, LANES))
    codes = read_codes(codes_ref)
    tile = lax.div(codes, points)
    key = point_key(tile, codes - tile * points, count, reach)
    per = LANES // records
    across = []
    for t in range(span // LANES):
        lane = lane_iota((1, LANES))
        one = key[per * t : per * t + 1, :]
        for h in range(1, per):
            one = jnp.where(
                lane < h * records, one, pltpu.roll(key[per * t + h : per * t + h + 1, :], h * records, 1)
            )
        across.append(one)
    repeats = jnp.zeros((span, LANES), F32)
    for t, one in enumerate(across):
        before = lane_iota((span, LANES)) + t * LANES < row_iota((span, LANES))
        repeats += ((down[...] == one) & before).astype(F32)
    fresh = jnp.sum(repeats, axis=1, keepdims=True) == 0.0
    first[...] = (fresh & (down[...] < NOWHERE)).astype(F32)
    found = jnp.zeros((listed, LANES), jnp.int32)
    for t, one in enumerate(across):
        rank = jnp.sum(jnp.where(down[...] < one, first[...], 0.0), axis=0, keepdims=True)
        rank = jnp.where(one < NOWHERE, rank.astype(jnp.int32), -1)
        same = rank == row_iota((listed, LANES))
        same_ref[:, t * LANES : (t + 1) * LANES] = same.astype(F32).astype(BF16)
        found = jnp.maximum(found, jnp.where(same, one, 0))
    found = jnp.max(found, axis=1, keepdims=True).astype(F32)
    for b in range(listed // LANES):
        wide = jnp.broadcast_to(found[b * LANES : (b + 1) * LANES], (LANES, LANES))
        info_ref[0:1, b * LANES : (b + 1) * LANES] = jnp.transpose(wide)[0:1].astype(jnp.int32)
    starts = jnp.where(down[...] < lane_iota((span, LANES)) * STRIDE, first[...], 0.0)
    info_ref[0:1, listed:] = jnp.sum(starts, axis=0, keepdims=True).astype(jnp.int32)

    dest = to_column(dest_ref[...])
    named = (dest == lane_iota((records, LANES))).astype(F32)
    before = jnp.dot(earlier_rows(records), named.astype(BF16), preferred_element_type=F32)
    rank = jnp.sum(before * named, axis=1, keepdims=True).astype(jnp.int32)
    chosen_ref[...] = (dest * capacity + rank == lane_iota(chosen_ref.shape)).astype(F32).astype(BF16)
    alive = lane_iota(weight_ref.shape) < to_column(valid_ref[...])
    weight_ref[...] = jnp.where(alive, inv_ref[...].astype(F32), 0.0)

    features, levels = vertical_ref.shape
    wide = mixing_ref.shape[2]
    tall = mixing_ref.shape[1]
    variables = features // levels
    mixing_ref[...] = jnp.zeros_like(mixing_ref)
    rows = jnp.concatenate([vertical_ref[...].astype(F32), jnp.zeros((features, wide - levels), F32)], axis=1)
    spread = rows
    for v in range(1, variables):
        spread = jnp.where(row_iota(rows.shape) % variables == v, pltpu.roll(rows, v * levels, 1), spread)
    mixing_ref[0] = spread[:tall].astype(BF16)
    mixing_ref[1, 0 : features - tall, :] = spread[tall:].astype(BF16)
    taps = lon_ref.shape[0]
    spare = jnp.zeros((taps, wide - features), F32)
    lon = jnp.concatenate([lon_ref[...], spare], axis=1)
    lon = jnp.concatenate([lon[k : k + 1] for k in reversed(range(taps))] + [jnp.zeros((16 - taps, wide), F32)], axis=0)
    for b in range(8):
        table_ref[16 * b : 16 * (b + 1), :] = pltpu.roll(lon, b, 0) if b else lon
    taps_ref[...] = jnp.concatenate([lat_ref[...], spare], axis=1)


def impact_kernel(records, products_ref, same_ref, near_ref, far_ref, out_ref, terms):
    count, tall, width = products_ref.shape
    listed = same_ref.shape[0]
    lane = lane_iota((tall, width))
    for pair in range(count // 2):
        one = products_ref[2 * pair].astype(F32)
        two = products_ref[2 * pair + 1].astype(F32)
        first = jnp.where(lane < records, one, pltpu.roll(two, records, 1))
        second = jnp.where(lane < records, pltpu.roll(one, records, 1), two)
        terms[0, :, pair * width : (pair + 1) * width] = first.astype(BF16)
        terms[1, :, pair * width : (pair + 1) * width] = second.astype(BF16)
    for h in range(2):
        out_ref[:, h * listed : (h + 1) * listed] = lax.dot_general(
            terms[h], same_ref[...], (((1,), (1,)), ((), ())), preferred_element_type=F32
        ).astype(BF16)


def filter_kernel(block_of, reach, rows, *refs):
    (*lists, vertical_ref, lon_ref, lat_ref, out_ref, mixed, along, mean, ready, sent) = refs
    lists = [(lists[n], lists[n + 1]) for n in range(0, len(lists) // 2 * 2, 2)]
    listed = lists[0][1].shape[1] // vertical_ref.shape[0]
    features = out_ref.shape[0]
    wide = vertical_ref.shape[2]
    height = ready.shape[2]
    window = height + 2 * reach
    pitch = along.shape[0] // window
    step = pl.program_id(0)
    base = block_of(step) * height - reach

    @pl.when(step == 0)
    def _():
        along[...] = jnp.zeros_like(along)
        for n, (info, impact) in enumerate(lists):
            for part in range(0, listed, LANES):

                @pl.when(info[0, listed + rows] > part)
                def _(n=n, impact=impact, part=part):
                    total = 0.0
                    for h in range(vertical_ref.shape[0]):
                        total += lax.dot_general(
                            impact[:, h * listed + part : h * listed + part + LANES],
                            vertical_ref[h],
                            (((0,), (0,)), ((), ())),
                            preferred_element_type=F32,
                        )
                    mixed[n * listed + part : n * listed + part + LANES, :] = total

    for n, (info, _) in enumerate(lists):
        offset = -base
        if n:
            side = 1 - 2 * lax.rem(lax.axis_index("lat"), 2)
            offset += (rows if n == 1 else -rows) * side
        low = jnp.clip(-offset, 0, rows)
        high = jnp.clip(window - offset, 0, rows)

        start, stop = info[0, listed + low], info[0, listed + high]

        def add_some(i, carry, info=info, n=n, offset=offset, start=start, stop=stop):
            pieces = []
            for u in range(SOME):
                here = start + i * SOME + u
                live = here < stop
                here = jnp.where(live, here, start)
                key = info[0, here]
                row = lax.shift_right_logical(key, 8) + offset
                place = jnp.bitwise_and(key, STRIDE - 1)
                spot = jnp.bitwise_and(place, 7)
                at = pl.ds(pl.multiple_of(row * pitch + place - spot, 8), 16)
                taps = lon_ref[pl.ds(pl.multiple_of(spot * 16, 16), 16), :]
                column = mixed[pl.ds(n * listed + here, 1), :] * jnp.where(live, 1.0, 0.0)
                pieces.append((at, taps * column))
            for at, piece in pieces:
                along[at, :] += piece
            return carry

        lax.fori_loop(0, lax.div(stop - start + SOME - 1, SOME), add_some, 0)

    flat = ready.reshape(ready.shape[0] * features * height, LANES)

    def leave(at, t):
        here = pl.ds(t * LANES, min(LANES, features - t * LANES))
        there = pl.ds(pl.multiple_of(block_of(at) * height, height), height)
        return pltpu.make_async_copy(ready.at[at, here], out_ref.at[here, there], sent.at[at, t])

    for t in range(wide // LANES):
        here = slice(t * LANES, (t + 1) * LANES)
        lat = [jnp.broadcast_to(lat_ref[k : k + 1, here], (8, LANES)) for k in range(2 * reach + 1)]

        for j in range(LANES // 8):
            sums = [None] * height
            for w in range(window):
                spot = pl.ds(w * pitch + 8 + j * 8, 8)
                part = along[spot, here]
                along[spot, here] = jnp.zeros_like(part)
                for row in range(max(0, w - 2 * reach), min(height, w + 1)):
                    term = lat[w - row] * part
                    sums[row] = term if sums[row] is None else sums[row] + term
            for row in range(height):
                mean[t % 2, row, j * 8 : (j + 1) * 8, :] = sums[row]

        kept = min(LANES, features - t * LANES)
        for row in range(height):
            turned = jnp.transpose(mean[t % 2, row])
            flat[pl.ds((step * features + t * LANES) * height + row, kept, stride=height), :] = turned[0:kept]
        leave(step, t).start()

    @pl.when(step == ready.shape[0] - 1)
    def _():
        for at in range(ready.shape[0]):
            for t in range(wide // LANES):
                leave(at, t).wait()


def solution(mesh):
    lon_devices, lat_devices = mesh.shape["lon"], mesh.shape["lat"]

    def body(state_field, jacobian, observed, inverse_var, valid_count, destination, column, vertical, lon_taps, lat_taps):
        variables, levels, rows, cols = state_field.shape
        features = variables * levels
        records, channels = jacobian.shape[1], jacobian.shape[-1]
        capacity = max(2, 2 * records // lon_devices)
        reach = lon_taps.shape[-1] // 2
        points = rows * cols
        span = records * lon_devices
        tall = pl.cdiv(features, 32) * 16

        told = (lon_devices, 1, records)
        codes = lax.broadcasted_iota(jnp.int32, told, 0) * (NOWHERE // points)
        codes = (codes + jnp.broadcast_to(destination.reshape(1, 1, records), told)) * points
        codes = codes + jnp.broadcast_to(column.reshape(1, 1, records), told)
        codes = lax.all_to_all(codes, "lon", split_axis=0, concat_axis=0, tiled=True)
        codes = codes.reshape(lon_devices, records)
        laid = lay_state(state_field)

        found = gather_state(codes, laid, records, capacity, rows)
        found_in = lax.all_to_all(
            found.reshape(lon_devices, capacity, found.shape[-1]), "lon", split_axis=0, concat_axis=0, tiled=True
        )
        listed = 3 * lon_devices * capacity
        wide = pl.cdiv(features, LANES) * LANES
        taps = lon_taps.shape[-1]
        vmem, anywhere = pl.BlockSpec(memory_space=pltpu.VMEM), pl.BlockSpec(memory_space=pl.ANY)
        chosen, weight, same, info, mixing, lon_table, lat_flat = pl.pallas_call(
            functools.partial(plan_kernel, records, points, reach, capacity),
            in_specs=[vmem] * 7 + [anywhere],
            out_shape=(
                jax.ShapeDtypeStruct((records, lon_devices * capacity), BF16),
                jax.ShapeDtypeStruct((records, channels), F32),
                jax.ShapeDtypeStruct((listed, span), BF16),
                jax.ShapeDtypeStruct((1, listed + LANES), jnp.int32),
                jax.ShapeDtypeStruct((2, tall, wide), BF16),
                jax.ShapeDtypeStruct((8 * 16, wide), F32),
                jax.ShapeDtypeStruct((taps, wide), F32),
            ),
            scratch_shapes=[pltpu.VMEM((span, LANES), jnp.int32), pltpu.VMEM((span, LANES), F32)],
            compiler_params=pltpu.CompilerParams(vmem_limit_bytes=16 * 1024 * 1024),
            cost_estimate=pl.CostEstimate(flops=8 * span * span, bytes_accessed=span * listed * 2, transcendentals=0),
            name="plan_points",
        )(
            codes,
            destination.reshape(1, records),
            valid_count.reshape(1, records),
            inverse_var.reshape(records, channels),
            jnp.swapaxes(vertical, 0, 1).reshape(features, levels),
            jnp.moveaxis(lon_taps, 2, 0).reshape(taps, features),
            jnp.moveaxis(lat_taps, 2, 0).reshape(taps, features),
            found,
        )
        own = jnp.swapaxes(jacobian.reshape(records, variables, levels, channels), 1, 2).reshape(-1, channels)
        products = departures(
            chosen,
            found_in.reshape(lon_devices * capacity, found.shape[-1]),
            weight,
            observed.reshape(records, channels),
            own,
            info,
            lon_devices,
            tall,
        )
        products_in = lax.all_to_all(products, "lon", split_axis=0, concat_axis=0, tiled=True)

        pairs = [(i, i + 1) for i in range(0, lat_devices - 1, 2)]
        between = [(i, i + 1) for i in range(1, lat_devices - 1, 2)]
        swaps = [[(a, b) for a, b in some] + [(b, a) for a, b in some] for some in (pairs, between)]
        info_near = lax.ppermute(info, "lat", swaps[0])
        info_far = lax.ppermute(info, "lat", swaps[1])

        impact = pl.pallas_call(
            functools.partial(impact_kernel, records),
            in_specs=[vmem] * 2 + [anywhere] * 2,
            out_shape=jax.ShapeDtypeStruct((tall, 2 * listed), BF16),
            scratch_shapes=[pltpu.VMEM((2, tall, span), BF16)],
            compiler_params=pltpu.CompilerParams(vmem_limit_bytes=16 * 1024 * 1024),
            name="impact_columns",
        )(products_in, same, info_near, info_far)
        impact_near = lax.ppermute(impact, "lat", swaps[0])
        impact_far = lax.ppermute(impact, "lat", swaps[1])

        height = 8
        blocks = rows // height
        pitch = LANES + 16

        def filtered(lists, steps, block_of, before, name):
            held = [pl.BlockSpec(memory_space=pltpu.SMEM), pl.BlockSpec(memory_space=pltpu.VMEM)] * (len(lists) // 2)
            held += [pl.BlockSpec(memory_space=pltpu.VMEM)] * 3
            given = list(lists) + [mixing, lon_table, lat_flat]
            kernel = functools.partial(filter_kernel, block_of, reach, rows)
            if before is not None:
                given.append(before)
                held.append(pl.BlockSpec(memory_space=pl.ANY))
                at = len(lists) + 3
                inner = kernel
                kernel = lambda *refs: inner(*refs[:at], *refs[at + 1 :])
            return pl.pallas_call(
                kernel,
                grid=(steps,),
                in_specs=held,
                out_specs=pl.BlockSpec(memory_space=pl.ANY),
                out_shape=jax.ShapeDtypeStruct((features, rows, cols), F32),
                scratch_shapes=[
                    pltpu.VMEM((len(lists) // 2 * listed, wide), F32),
                    pltpu.VMEM(((height + 2 * reach) * pitch, wide), F32),
                    pltpu.VMEM((2, height, cols, LANES), F32),
                    pltpu.VMEM((steps, features, height, cols), F32),
                    pltpu.SemaphoreType.DMA((steps, wide // LANES)),
                ],
                input_output_aliases={} if before is None else {len(given) - 1: 0},
                compiler_params=pltpu.CompilerParams(vmem_limit_bytes=24 * 1024 * 1024),
                cost_estimate=pl.CostEstimate(
                    flops=40 * features * rows * cols, bytes_accessed=features * rows * cols * 2, transcendentals=0
                ),
                name=name,
            )(*given)

        inner = filtered([info, impact], blocks - 2, lambda s: s + 1, None, "inner_rows")
        result = filtered(
            [info, impact, info_near, impact_near, info_far, impact_far],
            2,
            lambda s: s * (blocks - 1),
            inner,
            "outer_rows",
        )
        return result.reshape(variables, levels, rows, cols)

    placed = (
        P(None, None, "lat", "lon"),
        P("lat", "lon", None, None, None),
        P("lat", "lon", None),
        P("lat", "lon", None),
        P("lat", "lon"),
        P("lat", "lon", None),
        P("lat", "lon"),
        P(),
        P(),
        P(),
    )
    return jax.shard_map(
        body, mesh=mesh, in_specs=placed, out_specs=P(None, None, "lat", "lon"), check_vma=False
    )
```

```python
import functools

import jax
import jax.numpy as jnp
from jax import lax
from jax.experimental import pallas as pl
from jax.experimental.pallas import tpu as pltpu
from jax.sharding import PartitionSpec as P

LANES = 128
F32 = jnp.float32
BF16 = jnp.bfloat16
STRIDE = 256
NOWHERE = 1 << 20
SOME = 4


def lane_iota(shape):
    return lax.broadcasted_iota(jnp.int32, shape, 1)


def row_iota(shape):
    return lax.broadcasted_iota(jnp.int32, shape, 0)


def earlier_rows(size):
    return (lane_iota((size, size)) < row_iota((size, size))).astype(F32).astype(BF16)


def read_codes(codes_ref):
    count, records = codes_ref.shape
    codes = jnp.bitwise_and(codes_ref[...], NOWHERE - 1)
    return jnp.concatenate([codes, jnp.zeros((count, LANES - records), jnp.int32)], axis=1)


def split_codes(codes_ref, records, points):
    flipped = jnp.transpose(read_codes(codes_ref).astype(F32))[:records].astype(jnp.int32)
    tile = lax.div(flipped, points)
    return tile, flipped - tile * points


def lay_state_kernel(rows, levels, chunk, state_ref, out_ref, state, arrived):
    variables = state_ref.shape[0] // (rows * levels)
    half = rows // 2
    parts = []
    for first in range(0, levels, chunk):
        size = min(chunk, levels - first)
        for v in range(variables):
            start = (v * levels + first) * rows
            here = pl.ds(start, size * rows)
            copy = pltpu.make_async_copy(state_ref.at[here], state.at[here], arrived.at[len(parts)])
            copy.start()
            parts.append((v, first, size, start, copy))
    for v, first, size, start, copy in parts:
        copy.wait()
        for odd in range(2):
            some = state[pl.ds(start + odd, size * half, stride=2), :].astype(BF16)
            out_ref[first : first + size, v * half : (v + 1) * half, odd * LANES : (odd + 1) * LANES] = some.reshape(
                size, half, LANES
            )


def lay_state(state):
    variables, levels, rows, cols = state.shape
    chunk = 72
    return pl.pallas_call(
        functools.partial(lay_state_kernel, rows, levels, chunk),
        in_specs=[pl.BlockSpec(memory_space=pl.ANY)],
        out_shape=jax.ShapeDtypeStruct((levels, variables * rows // 2, 2 * cols), BF16),
        scratch_shapes=[
            pltpu.VMEM((variables * levels * rows, cols), F32),
            pltpu.SemaphoreType.DMA((variables * pl.cdiv(levels, chunk),)),
        ],
        compiler_params=pltpu.CompilerParams(vmem_limit_bytes=24 * 1024 * 1024),
        cost_estimate=pl.CostEstimate(flops=0, bytes_accessed=state.size * 6, transcendentals=0),
        name="lay_state",
    )(state.reshape(variables * levels * rows, cols))


def gather_kernel(records, capacity, rows, codes_ref, state_ref, out_ref, held):
    count = codes_ref.shape[0]
    slots = out_ref.shape[0]
    half = rows // 2
    features = state_ref.shape[0] // half
    me = lax.axis_index("lon")
    tile, column = split_codes(codes_ref, records, rows * LANES)
    mine = (tile == me).astype(F32)
    rank = jnp.dot(earlier_rows(records), mine.astype(BF16), preferred_element_type=F32)
    slot = lane_iota(mine.shape) * capacity + rank.astype(jnp.int32)
    slot = jnp.where(tile == me, slot, -1)
    place = jnp.zeros((records, slots), F32)
    for d in range(count):
        hit = slot[:, d : d + 1] == lane_iota((records, slots))
        place += jnp.where(hit, (column[:, d : d + 1] + 1).astype(F32), 0.0)
    place = jnp.sum(place, axis=0, keepdims=True).astype(jnp.int32) - 1
    row = lax.shift_right_arithmetic(place, LANES.bit_length() - 1)
    in_pair = jnp.where(place < 0, -1, jnp.bitwise_and(place, 2 * LANES - 1))
    pick = (row_iota((2 * LANES, slots)) == in_pair).astype(F32).astype(BF16)
    mask = (row_iota((half, slots)) == lax.shift_right_arithmetic(row, 1)).astype(F32)

    held[...] = jnp.zeros_like(held)
    chunk = 72
    for first in range(0, features, chunk):
        size = min(chunk, features - first)
        found = jnp.dot(
            state_ref[first * half : (first + size) * half, :], pick, preferred_element_type=F32
        )
        found = found.reshape(size, half, slots) * mask[None]
        held[first : first + size, :] = jnp.sum(found, axis=1)
    for t in range(out_ref.shape[1] // LANES):
        out_ref[:, t * LANES : (t + 1) * LANES] = jnp.transpose(
            held[t * LANES : (t + 1) * LANES, :]
        ).astype(BF16)


def gather_state(codes, laid, records, capacity, rows):
    features = laid.shape[0] * laid.shape[1] * 2 // rows
    wide = pl.cdiv(features, LANES) * LANES
    slots = codes.shape[0] * capacity
    vmem = pl.BlockSpec(memory_space=pltpu.VMEM)
    return pl.pallas_call(
        functools.partial(gather_kernel, records, capacity, rows),
        in_specs=[vmem, vmem],
        out_shape=jax.ShapeDtypeStruct((slots, wide), BF16),
        scratch_shapes=[pltpu.VMEM((wide, slots), F32)],
        compiler_params=pltpu.CompilerParams(vmem_limit_bytes=12 * 1024 * 1024),
        cost_estimate=pl.CostEstimate(flops=2 * laid.size * slots, bytes_accessed=laid.size * 2, transcendentals=0),
        name="gather_state",
    )(codes, laid.reshape(-1, laid.shape[2]))


def to_column(row):
    size = row.shape[1]
    wide = jnp.broadcast_to(row, (size, size))
    return jnp.sum(jnp.where(row_iota(wide.shape) == lane_iota(wide.shape), wide, 0), axis=1, keepdims=True)


def fetch_kernel(from_ref, after_ref, out_ref, arrived):
    copy = pltpu.make_async_copy(from_ref.at[pl.ds(0, out_ref.shape[0])], out_ref, arrived)
    copy.start()
    copy.wait()


def fetch(array, after, rows):
    anywhere = pl.BlockSpec(memory_space=pl.ANY)
    return pl.pallas_call(
        fetch_kernel,
        in_specs=[anywhere, anywhere],
        out_specs=pl.BlockSpec(memory_space=pltpu.VMEM),
        out_shape=jax.ShapeDtypeStruct((rows, array.shape[1]), array.dtype),
        scratch_shapes=[pltpu.SemaphoreType.DMA],
        compiler_params=pltpu.CompilerParams(vmem_limit_bytes=12 * 1024 * 1024),
        cost_estimate=pl.CostEstimate(flops=0, bytes_accessed=rows * array.shape[1] * 4, transcendentals=0),
        name="fetch_jacobian",
    )(array, after)


def first_departures(group, features, chosen_ref, states_ref, weight_ref, obs_ref, jac_ref, after_ref, total_ref, columns_ref):
    columns_ref[...] = jnp.dot(chosen_ref[...], states_ref[...], preferred_element_type=F32)
    total_ref[...] = jnp.zeros_like(total_ref)
    product_groups(group, features, 0, columns_ref, weight_ref, obs_ref, jac_ref, total_ref)


def last_departures(group, features, done, columns_ref, weight_ref, obs_ref, jac_ref, before_ref, out_ref, total):
    records = obs_ref.shape[0]
    total[...] = before_ref[...]
    product_groups(group, features, done, columns_ref, weight_ref, obs_ref, jac_ref, total)
    half = total.shape[0] // 2
    lane = lane_iota((half, LANES))
    low = jnp.where(lane < records, total[0:half, :], pltpu.roll(total[half:, :], records, 1)).astype(BF16)
    for t in range(out_ref.shape[0]):
        out_ref[t] = low


def product_groups(group, features, done, columns_ref, weight_ref, obs_ref, jac_ref, total):
    channels = jac_ref.shape[1]
    part = group // 2
    span = part * features
    tiles, skip = divmod(features, LANES)
    wide = columns_ref.shape[1]
    reach = pl.cdiv(skip * (part - 1) + features, LANES)
    row = row_iota((group, LANES))
    index = jnp.bitwise_and(row, part - 1)
    lows = {}
    for g in range(done, jac_ref.shape[0] // (group * features)):
        first = g * group * features
        mine = columns_ref[g * group : (g + 1) * group, :]
        if reach * LANES > wide:
            mine = jnp.concatenate([mine, jnp.zeros((group, reach * LANES - wide), F32)], axis=1)
        bit = 1
        while bit < part:
            moved = pltpu.roll(mine, skip * bit, 1)
            mine = jnp.where(jnp.bitwise_and(row_iota(mine.shape), bit) > 0, moved, mine)
            bit *= 2
        spread = []
        for t in range(pl.cdiv(span, LANES)):
            piece = jnp.zeros((group, LANES), F32)
            for r in range(part):
                at = t - tiles * r
                if 0 <= at < reach:
                    piece = jnp.where(index == r, mine[:, at * LANES : (at + 1) * LANES], piece)
            spread.append(piece.astype(BF16))
        spread = jnp.concatenate(spread, axis=1)[:, :span]
        pair = jnp.concatenate([jac_ref[first : first + span, :], jac_ref[first + span : first + 2 * span, :]], axis=1)
        both = jnp.dot(spread, pair, preferred_element_type=F32)
        model = jnp.where(row < part, both[:, :channels], both[:, channels:])
        own = slice(g * group, (g + 1) * group)
        misfit = weight_ref[own, :] * (model - obs_ref[own, :].astype(F32))
        lows[g] = misfit.astype(BF16).astype(F32)
    for g, low in lows.items():
        first = g * group * features
        for r in range(part):
            against = jnp.concatenate([jnp.where(row == r, low, 0.0), jnp.where(row == r + part, low, 0.0)], axis=1)
            start = first + r * features
            lead = start % 16
            size = pl.cdiv(features + lead, 16) * 16
            rows = [jac_ref[start - lead + h * span : start - lead + h * span + size, :] for h in range(2)]
            one = lax.dot_general(
                jnp.concatenate(rows, axis=1),
                against.astype(BF16),
                (((1,), (1,)), ((), ())),
                preferred_element_type=F32,
            )
            one = one[lead : lead + features]
            sums = one if r == 0 else sums + one
        total[0:features, g * group : (g + 1) * group] = sums


def departures(chosen, states, weight, obs, jac, after, devices, tall):
    records, channels = obs.shape
    features = jac.shape[0] // records
    group = 16
    done = records // group // 2
    vmem, anywhere = pl.BlockSpec(memory_space=pltpu.VMEM), pl.BlockSpec(memory_space=pl.ANY)
    params = pltpu.CompilerParams(vmem_limit_bytes=16 * 1024 * 1024)
    cost = pl.CostEstimate(flops=3_000_000_000, bytes_accessed=jac.size, transcendentals=0)
    total, columns = pl.pallas_call(
        functools.partial(first_departures, group, features),
        in_specs=[vmem] * 5 + [anywhere],
        out_shape=(
            jax.ShapeDtypeStruct((2 * tall, 2 * records), F32),
            jax.ShapeDtypeStruct((records, states.shape[1]), F32),
        ),
        compiler_params=params,
        cost_estimate=cost,
        name="first_departures",
    )(chosen, states, weight, obs, fetch(jac, after, done * group * features), after)
    return pl.pallas_call(
        functools.partial(last_departures, group, features, done),
        in_specs=[vmem] * 5,
        out_shape=jax.ShapeDtypeStruct((devices, tall, 2 * records), BF16),
        scratch_shapes=[pltpu.VMEM((2 * tall, 2 * records), F32)],
        compiler_params=params,
        cost_estimate=cost,
        name="last_departures",
    )(columns, weight, obs, jac, total)


def point_key(tile, column, count, reach):
    me = lax.axis_index("lon")
    right, left = lax.rem(me + 1, count), lax.rem(me + count - 1, count)
    row = lax.div(column, LANES)
    lon = column - row * LANES
    key = jnp.where(tile == me, lon + reach, NOWHERE)
    key = jnp.where((tile == right) & (lon < reach), lon + LANES + reach, key)
    key = jnp.where((tile == left) & (lon >= LANES - reach), lon - LANES + reach, key)
    return jnp.where(key == NOWHERE, NOWHERE, key + row * STRIDE)


def twice(array, features):
    left = features % LANES
    lane = lane_iota(array.shape)
    return jnp.where((lane >= features) & (lane < features + left), pltpu.roll(array, left, 1), array)


def plan_kernel(records, points, reach, capacity, codes_ref, dest_ref, valid_ref, inv_ref, vertical_ref, lon_ref, lat_ref, after_ref, chosen_ref, weight_ref, same_ref, info_ref, mixing_ref, table_ref, taps_ref, down, first):
    count = codes_ref.shape[0]
    span, listed = count * records, same_ref.shape[0]
    tile, column = split_codes(codes_ref, records, points)
    key = point_key(tile, column, count, reach)
    for d in range(count):
        down[d * records : (d + 1) * records, :] = jnp.broadcast_to(key[:, d : d + 1], (records, LANES))
    codes = read_codes(codes_ref)
    tile = lax.div(codes, points)
    key = point_key(tile, codes - tile * points, count, reach)
    per = LANES // records
    across = []
    for t in range(span // LANES):
        lane = lane_iota((1, LANES))
        one = key[per * t : per * t + 1, :]
        for h in range(1, per):
            one = jnp.where(
                lane < h * records, one, pltpu.roll(key[per * t + h : per * t + h + 1, :], h * records, 1)
            )
        across.append(one)
    repeats = jnp.zeros((span, LANES), F32)
    for t, one in enumerate(across):
        before = lane_iota((span, LANES)) + t * LANES < row_iota((span, LANES))
        repeats += ((down[...] == one) & before).astype(F32)
    fresh = jnp.sum(repeats, axis=1, keepdims=True) == 0.0
    first[...] = (fresh & (down[...] < NOWHERE)).astype(F32)
    found = jnp.zeros((listed, LANES), jnp.int32)
    for t, one in enumerate(across):
        rank = jnp.sum(jnp.where(down[...] < one, first[...], 0.0), axis=0, keepdims=True)
        rank = jnp.where(one < NOWHERE, rank.astype(jnp.int32), -1)
        same = rank == row_iota((listed, LANES))
        same_ref[:, t * LANES : (t + 1) * LANES] = same.astype(F32).astype(BF16)
        found = jnp.maximum(found, jnp.where(same, one, 0))
    found = jnp.max(found, axis=1, keepdims=True).astype(F32)
    for b in range(listed // LANES):
        wide = jnp.broadcast_to(found[b * LANES : (b + 1) * LANES], (LANES, LANES))
        info_ref[0:1, b * LANES : (b + 1) * LANES] = jnp.transpose(wide)[0:1].astype(jnp.int32)
    starts = jnp.where(down[...] < lane_iota((span, LANES)) * STRIDE, first[...], 0.0)
    info_ref[0:1, listed:] = jnp.sum(starts, axis=0, keepdims=True).astype(jnp.int32)

    dest = to_column(dest_ref[...])
    named = (dest == lane_iota((records, LANES))).astype(F32)
    before = jnp.dot(earlier_rows(records), named.astype(BF16), preferred_element_type=F32)
    rank = jnp.sum(before * named, axis=1, keepdims=True).astype(jnp.int32)
    chosen_ref[...] = (dest * capacity + rank == lane_iota(chosen_ref.shape)).astype(F32).astype(BF16)
    alive = lane_iota(weight_ref.shape) < to_column(valid_ref[...])
    weight_ref[...] = jnp.where(alive, inv_ref[...].astype(F32), 0.0)

    features, levels = vertical_ref.shape
    wide = mixing_ref.shape[2]
    tall = mixing_ref.shape[1]
    variables = features // levels
    mixing_ref[...] = jnp.zeros_like(mixing_ref)
    rows = jnp.concatenate([vertical_ref[...].astype(F32), jnp.zeros((features, wide - levels), F32)], axis=1)
    spread = rows
    for v in range(1, variables):
        spread = jnp.where(row_iota(rows.shape) % variables == v, pltpu.roll(rows, v * levels, 1), spread)
    spread = twice(spread, features)
    mixing_ref[0] = spread[:tall].astype(BF16)
    mixing_ref[1, 0 : features - tall, :] = spread[tall:].astype(BF16)
    taps = lon_ref.shape[0]
    spare = jnp.zeros((taps, wide - features), F32)
    lon = twice(jnp.concatenate([lon_ref[...], spare], axis=1), features)
    lon = jnp.concatenate([lon[k : k + 1] for k in reversed(range(taps))] + [jnp.zeros((16 - taps, wide), F32)], axis=0)
    for b in range(8):
        table_ref[16 * b : 16 * (b + 1), :] = pltpu.roll(lon, b, 0) if b else lon
    taps_ref[...] = twice(jnp.concatenate([lat_ref[...], spare], axis=1), features)


def impact_kernel(records, products_ref, same_ref, near_ref, far_ref, out_ref, terms):
    count, tall, width = products_ref.shape
    listed = same_ref.shape[0]
    lane = lane_iota((tall, width))
    for pair in range(count // 2):
        one = products_ref[2 * pair].astype(F32)
        two = products_ref[2 * pair + 1].astype(F32)
        first = jnp.where(lane < records, one, pltpu.roll(two, records, 1))
        second = jnp.where(lane < records, pltpu.roll(one, records, 1), two)
        terms[0, :, pair * width : (pair + 1) * width] = first.astype(BF16)
        terms[1, :, pair * width : (pair + 1) * width] = second.astype(BF16)
    for h in range(2):
        out_ref[:, h * listed : (h + 1) * listed] = lax.dot_general(
            terms[h], same_ref[...], (((1,), (1,)), ((), ())), preferred_element_type=F32
        ).astype(BF16)


def filter_kernel(block_of, reach, rows, steps, inner, *refs):
    if inner:
        (*lists, vertical_ref, lon_ref, lat_ref, ready, mixed, along, mean) = refs
    else:
        (*lists, vertical_ref, lon_ref, lat_ref, inner_ref, out_ref, mixed, along, mean, ready, sent) = refs
    lists = [(lists[n], lists[n + 1]) for n in range(0, len(lists) // 2 * 2, 2)]
    listed = lists[0][1].shape[1] // vertical_ref.shape[0]
    features = ready.shape[0]
    wide = vertical_ref.shape[2]
    height = ready.shape[1] // steps
    window = height + 2 * reach
    pitch = along.shape[0] // window
    step = pl.program_id(0)
    base = block_of(step) * height - reach

    def leave_inner():
        there = pl.ds(height, inner_ref.shape[1])
        return pltpu.make_async_copy(inner_ref, out_ref.at[:, there], sent.at[steps, 0])

    @pl.when(step == 0)
    def _():
        if not inner:
            leave_inner().start()
        along[...] = jnp.zeros_like(along)
        for n, (info, impact) in enumerate(lists):
            for part in range(0, listed, LANES):

                @pl.when(info[0, listed + rows] > part)
                def _(n=n, impact=impact, part=part):
                    total = 0.0
                    for h in range(vertical_ref.shape[0]):
                        total += lax.dot_general(
                            impact[:, h * listed + part : h * listed + part + LANES],
                            vertical_ref[h],
                            (((0,), (0,)), ((), ())),
                            preferred_element_type=F32,
                        )
                    mixed[n * listed + part : n * listed + part + LANES, :] = total

    full, left = divmod(features, LANES)
    lane = lane_iota((1, wide)) - full * LANES
    mine = (lane < 0) | ((lane >= step * left) & (lane < (step + 1) * left))
    mine = jnp.where(mine, 1.0, 0.0)
    for n, (info, _) in enumerate(lists):
        offset = -base
        if n:
            side = 1 - 2 * lax.rem(lax.axis_index("lat"), 2)
            offset += (rows if n == 1 else -rows) * side
        low = jnp.clip(-offset, 0, rows)
        high = jnp.clip(window - offset, 0, rows)

        start, stop = info[0, listed + low], info[0, listed + high]

        def add_some(i, carry, info=info, n=n, offset=offset, start=start, stop=stop):
            pieces = []
            for u in range(SOME):
                here = start + i * SOME + u
                live = here < stop
                here = jnp.where(live, here, start)
                key = info[0, here]
                row = lax.shift_right_logical(key, 8) + offset
                place = jnp.bitwise_and(key, STRIDE - 1)
                spot = jnp.bitwise_and(place, 7)
                at = pl.ds(pl.multiple_of(row * pitch + place - spot, 8), 16)
                taps = lon_ref[pl.ds(pl.multiple_of(spot * 16, 16), 16), :]
                column = mixed[pl.ds(n * listed + here, 1), :] * jnp.where(live, mine, 0.0)
                pieces.append((at, taps * column))
            for at, piece in pieces:
                along[at, :] += piece
            return carry

        lax.fori_loop(0, lax.div(stop - start + SOME - 1, SOME), add_some, 0)

    tall = steps * height
    flat = ready.reshape(features * tall, LANES)

    def leave(at, t):
        here = pl.ds(t * LANES, min(LANES, features - t * LANES))
        mine = pl.ds(pl.multiple_of(at * height, height), height)
        there = pl.ds(pl.multiple_of(block_of(at) * height, height), height)
        return pltpu.make_async_copy(ready.at[here, mine], out_ref.at[here, there], sent.at[at, t])

    def smooth(t, again):
        here = slice(t * LANES, (t + 1) * LANES)
        lat = [jnp.broadcast_to(lat_ref[k : k + 1, here], (8, LANES)) for k in range(2 * reach + 1)]
        for j in range(LANES // 8):
            sums = [None] * height
            for w in range(window):
                spot = pl.ds(w * pitch + 8 + j * 8, 8)
                part = along[spot, here]
                if again:
                    along[spot, here] = jnp.zeros_like(part)
                for row in range(max(0, w - 2 * reach), min(height, w + 1)):
                    term = lat[w - row] * part
                    sums[row] = term if sums[row] is None else sums[row] + term
            for row in range(height):
                mean[t % 2, row, j * 8 : (j + 1) * 8, :] = sums[row]

    for t in range(full):
        smooth(t, True)
        for row in range(height):
            flat[pl.ds(t * LANES * tall + step * height + row, LANES, stride=tall), :] = jnp.transpose(
                mean[t % 2, row]
            )
        if not inner:
            leave(step, t).start()

    @pl.when(step == steps - 1)
    def _():
        smooth(full, False)
        for row in range(height):
            turned = jnp.transpose(mean[full % 2, row])
            for at in range(steps):
                flat[pl.ds(full * LANES * tall + at * height + row, left, stride=tall), :] = turned[
                    at * left : (at + 1) * left
                ]
        if not inner:
            for at in range(steps):
                leave(at, full).start()
            for at in range(steps):
                for t in range(full + 1):
                    leave(at, t).wait()
            leave_inner().wait()


def solution(mesh):
    lon_devices, lat_devices = mesh.shape["lon"], mesh.shape["lat"]

    def body(state_field, jacobian, observed, inverse_var, valid_count, destination, column, vertical, lon_taps, lat_taps):
        variables, levels, rows, cols = state_field.shape
        features = variables * levels
        records, channels = jacobian.shape[1], jacobian.shape[-1]
        capacity = max(2, 2 * records // lon_devices)
        reach = lon_taps.shape[-1] // 2
        points = rows * cols
        span = records * lon_devices
        tall = pl.cdiv(features, 32) * 16

        told = (lon_devices, 1, records)
        codes = lax.broadcasted_iota(jnp.int32, told, 0) * (NOWHERE // points)
        codes = (codes + jnp.broadcast_to(destination.reshape(1, 1, records), told)) * points
        codes = codes + jnp.broadcast_to(column.reshape(1, 1, records), told)
        codes = lax.all_to_all(codes, "lon", split_axis=0, concat_axis=0, tiled=True)
        codes = codes.reshape(lon_devices, records)
        laid = lay_state(state_field)

        found = gather_state(codes, laid, records, capacity, rows)
        found_in = lax.all_to_all(
            found.reshape(lon_devices, capacity, found.shape[-1]), "lon", split_axis=0, concat_axis=0, tiled=True
        )
        listed = 3 * lon_devices * capacity
        wide = pl.cdiv(features, LANES) * LANES
        taps = lon_taps.shape[-1]
        vmem, anywhere = pl.BlockSpec(memory_space=pltpu.VMEM), pl.BlockSpec(memory_space=pl.ANY)
        chosen, weight, same, info, mixing, lon_table, lat_flat = pl.pallas_call(
            functools.partial(plan_kernel, records, points, reach, capacity),
            in_specs=[vmem] * 7 + [anywhere],
            out_shape=(
                jax.ShapeDtypeStruct((records, lon_devices * capacity), BF16),
                jax.ShapeDtypeStruct((records, channels), F32),
                jax.ShapeDtypeStruct((listed, span), BF16),
                jax.ShapeDtypeStruct((1, listed + LANES), jnp.int32),
                jax.ShapeDtypeStruct((2, tall, wide), BF16),
                jax.ShapeDtypeStruct((8 * 16, wide), F32),
                jax.ShapeDtypeStruct((taps, wide), F32),
            ),
            scratch_shapes=[pltpu.VMEM((span, LANES), jnp.int32), pltpu.VMEM((span, LANES), F32)],
            compiler_params=pltpu.CompilerParams(vmem_limit_bytes=16 * 1024 * 1024),
            cost_estimate=pl.CostEstimate(flops=8 * span * span, bytes_accessed=span * listed * 2, transcendentals=0),
            name="plan_points",
        )(
            codes,
            destination.reshape(1, records),
            valid_count.reshape(1, records),
            inverse_var.reshape(records, channels),
            jnp.swapaxes(vertical, 0, 1).reshape(features, levels),
            jnp.moveaxis(lon_taps, 2, 0).reshape(taps, features),
            jnp.moveaxis(lat_taps, 2, 0).reshape(taps, features),
            found,
        )
        own = jnp.swapaxes(jacobian.reshape(records, variables, levels, channels), 1, 2).reshape(-1, channels)
        products = departures(
            chosen,
            found_in.reshape(lon_devices * capacity, found.shape[-1]),
            weight,
            observed.reshape(records, channels),
            own,
            info,
            lon_devices,
            tall,
        )
        products_in = lax.all_to_all(products, "lon", split_axis=0, concat_axis=0, tiled=True)

        pairs = [(i, i + 1) for i in range(0, lat_devices - 1, 2)]
        between = [(i, i + 1) for i in range(1, lat_devices - 1, 2)]
        swaps = [[(a, b) for a, b in some] + [(b, a) for a, b in some] for some in (pairs, between)]
        info_near = lax.ppermute(info, "lat", swaps[0])
        info_far = lax.ppermute(info, "lat", swaps[1])

        impact = pl.pallas_call(
            functools.partial(impact_kernel, records),
            in_specs=[vmem] * 2 + [anywhere] * 2,
            out_shape=jax.ShapeDtypeStruct((tall, 2 * listed), BF16),
            scratch_shapes=[pltpu.VMEM((2, tall, span), BF16)],
            compiler_params=pltpu.CompilerParams(vmem_limit_bytes=16 * 1024 * 1024),
            name="impact_columns",
        )(products_in, same, info_near, info_far)
        impact_near = lax.ppermute(impact, "lat", swaps[0])
        impact_far = lax.ppermute(impact, "lat", swaps[1])

        height = 8
        blocks = rows // height
        pitch = LANES + 16

        def filtered(lists, steps, block_of, before, name):
            held = [pl.BlockSpec(memory_space=pltpu.SMEM), vmem] * (len(lists) // 2) + [vmem] * 3
            given = list(lists) + [mixing, lon_table, lat_flat]
            scratch = [
                pltpu.VMEM((len(lists) // 2 * listed, wide), F32),
                pltpu.VMEM(((height + 2 * reach) * pitch, wide), F32),
                pltpu.VMEM((2, height, cols, LANES), F32),
            ]
            own_rows = (features, steps * height, cols)
            if before is not None:
                given.append(before)
                held.append(vmem)
                scratch += [pltpu.VMEM(own_rows, F32), pltpu.SemaphoreType.DMA((steps + 1, wide // LANES))]
            return pl.pallas_call(
                functools.partial(filter_kernel, block_of, reach, rows, steps, before is None),
                grid=(steps,),
                in_specs=held,
                out_specs=vmem if before is None else anywhere,
                out_shape=jax.ShapeDtypeStruct(own_rows if before is None else (features, rows, cols), F32),
                scratch_shapes=scratch,
                compiler_params=pltpu.CompilerParams(vmem_limit_bytes=24 * 1024 * 1024),
                cost_estimate=pl.CostEstimate(
                    flops=40 * features * rows * cols, bytes_accessed=features * rows * cols * 2, transcendentals=0
                ),
                name=name,
            )(*given)

        inner = filtered([info, impact], blocks - 2, lambda s: s + 1, None, "inner_rows")
        result = filtered(
            [info, impact, info_near, impact_near, info_far, impact_far],
            2,
            lambda s: s * (blocks - 1),
            inner,
            "outer_rows",
        )
        return result.reshape(variables, levels, rows, cols)

    placed = (
        P(None, None, "lat", "lon"),
        P("lat", "lon", None, None, None),
        P("lat", "lon", None),
        P("lat", "lon", None),
        P("lat", "lon"),
        P("lat", "lon", None),
        P("lat", "lon"),
        P(),
        P(),
        P(),
    )
    return jax.shard_map(
        body, mesh=mesh, in_specs=placed, out_specs=P(None, None, "lat", "lon"), check_vma=False
    )
```

```python
import functools

import jax
import jax.numpy as jnp
from jax import lax
from jax.experimental import pallas as pl
from jax.experimental.pallas import tpu as pltpu
from jax.sharding import PartitionSpec as P

LANES = 128
F32 = jnp.float32
BF16 = jnp.bfloat16
STRIDE = 256
NOWHERE = 1 << 20
SOME = 4


def lane_iota(shape):
    return lax.broadcasted_iota(jnp.int32, shape, 1)


def row_iota(shape):
    return lax.broadcasted_iota(jnp.int32, shape, 0)


def earlier_rows(size):
    return (lane_iota((size, size)) < row_iota((size, size))).astype(F32).astype(BF16)


def read_codes(codes_ref):
    count, records = codes_ref.shape
    codes = jnp.bitwise_and(codes_ref[...], NOWHERE - 1)
    return jnp.concatenate([codes, jnp.zeros((count, LANES - records), jnp.int32)], axis=1)


def split_codes(codes_ref, records, points):
    flipped = jnp.transpose(read_codes(codes_ref).astype(F32))[:records].astype(jnp.int32)
    tile = lax.div(flipped, points)
    return tile, flipped - tile * points


def lay_state_kernel(rows, levels, chunk, state_ref, out_ref, state, arrived):
    variables = state_ref.shape[0] // (rows * levels)
    half = rows // 2
    parts = []
    for first in range(0, levels, chunk):
        size = min(chunk, levels - first)
        for v in range(variables):
            start = (v * levels + first) * rows
            here = pl.ds(start, size * rows)
            copy = pltpu.make_async_copy(state_ref.at[here], state.at[here], arrived.at[len(parts)])
            copy.start()
            parts.append((v, first, size, start, copy))
    for v, first, size, start, copy in parts:
        copy.wait()
        for odd in range(2):
            some = state[pl.ds(start + odd, size * half, stride=2), :].astype(BF16)
            out_ref[first : first + size, v * half : (v + 1) * half, odd * LANES : (odd + 1) * LANES] = some.reshape(
                size, half, LANES
            )


def lay_state(state):
    variables, levels, rows, cols = state.shape
    chunk = 72
    return pl.pallas_call(
        functools.partial(lay_state_kernel, rows, levels, chunk),
        in_specs=[pl.BlockSpec(memory_space=pl.ANY)],
        out_shape=jax.ShapeDtypeStruct((levels, variables * rows // 2, 2 * cols), BF16),
        scratch_shapes=[
            pltpu.VMEM((variables * levels * rows, cols), F32),
            pltpu.SemaphoreType.DMA((variables * pl.cdiv(levels, chunk),)),
        ],
        compiler_params=pltpu.CompilerParams(vmem_limit_bytes=24 * 1024 * 1024),
        cost_estimate=pl.CostEstimate(flops=0, bytes_accessed=state.size * 6, transcendentals=0),
        name="lay_state",
    )(state.reshape(variables * levels * rows, cols))


def gather_kernel(records, capacity, rows, codes_ref, state_ref, out_ref, held):
    count = codes_ref.shape[0]
    slots = out_ref.shape[0]
    half = rows // 2
    features = state_ref.shape[0] // half
    me = lax.axis_index("lon")
    tile, column = split_codes(codes_ref, records, rows * LANES)
    mine = (tile == me).astype(F32)
    rank = jnp.dot(earlier_rows(records), mine.astype(BF16), preferred_element_type=F32)
    slot = lane_iota(mine.shape) * capacity + rank.astype(jnp.int32)
    slot = jnp.where(tile == me, slot, -1)
    place = jnp.zeros((records, slots), F32)
    for d in range(count):
        hit = slot[:, d : d + 1] == lane_iota((records, slots))
        place += jnp.where(hit, (column[:, d : d + 1] + 1).astype(F32), 0.0)
    place = jnp.sum(place, axis=0, keepdims=True).astype(jnp.int32) - 1
    row = lax.shift_right_arithmetic(place, LANES.bit_length() - 1)
    in_pair = jnp.where(place < 0, -1, jnp.bitwise_and(place, 2 * LANES - 1))
    pick = (row_iota((2 * LANES, slots)) == in_pair).astype(F32).astype(BF16)
    mask = (row_iota((half, slots)) == lax.shift_right_arithmetic(row, 1)).astype(F32)

    held[...] = jnp.zeros_like(held)
    chunk = 72
    for first in range(0, features, chunk):
        size = min(chunk, features - first)
        found = jnp.dot(
            state_ref[first * half : (first + size) * half, :], pick, preferred_element_type=F32
        )
        found = found.reshape(size, half, slots) * mask[None]
        held[first : first + size, :] = jnp.sum(found, axis=1)
    for t in range(out_ref.shape[1] // LANES):
        out_ref[:, t * LANES : (t + 1) * LANES] = jnp.transpose(
            held[t * LANES : (t + 1) * LANES, :]
        ).astype(BF16)


def gather_state(codes, laid, records, capacity, rows):
    features = laid.shape[0] * laid.shape[1] * 2 // rows
    wide = pl.cdiv(features, LANES) * LANES
    slots = codes.shape[0] * capacity
    vmem = pl.BlockSpec(memory_space=pltpu.VMEM)
    return pl.pallas_call(
        functools.partial(gather_kernel, records, capacity, rows),
        in_specs=[vmem, vmem],
        out_shape=jax.ShapeDtypeStruct((slots, wide), BF16),
        scratch_shapes=[pltpu.VMEM((wide, slots), F32)],
        compiler_params=pltpu.CompilerParams(vmem_limit_bytes=12 * 1024 * 1024),
        cost_estimate=pl.CostEstimate(flops=2 * laid.size * slots, bytes_accessed=laid.size * 2, transcendentals=0),
        name="gather_state",
    )(codes, laid.reshape(-1, laid.shape[2]))


def to_column(row):
    size = row.shape[1]
    wide = jnp.broadcast_to(row, (size, size))
    return jnp.sum(jnp.where(row_iota(wide.shape) == lane_iota(wide.shape), wide, 0), axis=1, keepdims=True)


def fetch_kernel(from_ref, after_ref, out_ref, arrived):
    copy = pltpu.make_async_copy(from_ref.at[pl.ds(0, out_ref.shape[0])], out_ref, arrived)
    copy.start()
    copy.wait()


def fetch(array, after, rows):
    anywhere = pl.BlockSpec(memory_space=pl.ANY)
    return pl.pallas_call(
        fetch_kernel,
        in_specs=[anywhere, anywhere],
        out_specs=pl.BlockSpec(memory_space=pltpu.VMEM),
        out_shape=jax.ShapeDtypeStruct((rows, array.shape[1]), array.dtype),
        scratch_shapes=[pltpu.SemaphoreType.DMA],
        compiler_params=pltpu.CompilerParams(vmem_limit_bytes=12 * 1024 * 1024),
        cost_estimate=pl.CostEstimate(flops=0, bytes_accessed=rows * array.shape[1] * 4, transcendentals=0),
        name="fetch_jacobian",
    )(array, after)


def first_departures(group, features, chosen_ref, states_ref, weight_ref, obs_ref, jac_ref, after_ref, total_ref, columns_ref):
    columns_ref[...] = jnp.dot(chosen_ref[...], states_ref[...], preferred_element_type=F32)
    total_ref[...] = jnp.zeros_like(total_ref)
    product_groups(group, features, 0, columns_ref, weight_ref, obs_ref, jac_ref, total_ref)


def last_departures(group, features, done, columns_ref, weight_ref, obs_ref, jac_ref, before_ref, out_ref, total):
    records = obs_ref.shape[0]
    total[...] = before_ref[...]
    product_groups(group, features, done, columns_ref, weight_ref, obs_ref, jac_ref, total)
    half = total.shape[0] // 2
    lane = lane_iota((half, LANES))
    low = jnp.where(lane < records, total[0:half, :], pltpu.roll(total[half:, :], records, 1)).astype(BF16)
    for t in range(out_ref.shape[0]):
        out_ref[t] = low


def product_groups(group, features, done, columns_ref, weight_ref, obs_ref, jac_ref, total):
    channels = jac_ref.shape[1]
    part = group // 2
    span = part * features
    tiles, skip = divmod(features, LANES)
    wide = columns_ref.shape[1]
    reach = pl.cdiv(skip * (part - 1) + features, LANES)
    row = row_iota((group, LANES))
    index = jnp.bitwise_and(row, part - 1)
    lows = {}
    for g in range(done, jac_ref.shape[0] // (group * features)):
        first = g * group * features
        mine = columns_ref[g * group : (g + 1) * group, :]
        if reach * LANES > wide:
            mine = jnp.concatenate([mine, jnp.zeros((group, reach * LANES - wide), F32)], axis=1)
        bit = 1
        while bit < part:
            moved = pltpu.roll(mine, skip * bit, 1)
            mine = jnp.where(jnp.bitwise_and(row_iota(mine.shape), bit) > 0, moved, mine)
            bit *= 2
        spread = []
        for t in range(pl.cdiv(span, LANES)):
            piece = jnp.zeros((group, LANES), F32)
            for r in range(part):
                at = t - tiles * r
                if 0 <= at < reach:
                    piece = jnp.where(index == r, mine[:, at * LANES : (at + 1) * LANES], piece)
            spread.append(piece.astype(BF16))
        spread = jnp.concatenate(spread, axis=1)[:, :span]
        pair = jnp.concatenate([jac_ref[first : first + span, :], jac_ref[first + span : first + 2 * span, :]], axis=1)
        both = jnp.dot(spread, pair, preferred_element_type=F32)
        model = jnp.where(row < part, both[:, :channels], both[:, channels:])
        own = slice(g * group, (g + 1) * group)
        misfit = weight_ref[own, :] * (model - obs_ref[own, :].astype(F32))
        lows[g] = misfit.astype(BF16).astype(F32)
    for g, low in lows.items():
        first = g * group * features
        for r in range(part):
            against = jnp.concatenate([jnp.where(row == r, low, 0.0), jnp.where(row == r + part, low, 0.0)], axis=1)
            start = first + r * features
            lead = start % 16
            size = pl.cdiv(features + lead, 16) * 16
            rows = [jac_ref[start - lead + h * span : start - lead + h * span + size, :] for h in range(2)]
            one = lax.dot_general(
                jnp.concatenate(rows, axis=1),
                against.astype(BF16),
                (((1,), (1,)), ((), ())),
                preferred_element_type=F32,
            )
            one = one[lead : lead + features]
            sums = one if r == 0 else sums + one
        total[0:features, g * group : (g + 1) * group] = sums


def departures(chosen, states, weight, obs, jac, after, devices, tall):
    records, channels = obs.shape
    features = jac.shape[0] // records
    group = 16
    done = records // group // 2
    vmem, anywhere = pl.BlockSpec(memory_space=pltpu.VMEM), pl.BlockSpec(memory_space=pl.ANY)
    params = pltpu.CompilerParams(vmem_limit_bytes=16 * 1024 * 1024)
    cost = pl.CostEstimate(flops=3_000_000_000, bytes_accessed=jac.size, transcendentals=0)
    total, columns = pl.pallas_call(
        functools.partial(first_departures, group, features),
        in_specs=[vmem] * 5 + [anywhere],
        out_shape=(
            jax.ShapeDtypeStruct((2 * tall, 2 * records), F32),
            jax.ShapeDtypeStruct((records, states.shape[1]), F32),
        ),
        compiler_params=params,
        cost_estimate=cost,
        name="first_departures",
    )(chosen, states, weight, obs, fetch(jac, after, done * group * features), after)
    return pl.pallas_call(
        functools.partial(last_departures, group, features, done),
        in_specs=[vmem] * 5,
        out_shape=jax.ShapeDtypeStruct((devices, tall, 2 * records), BF16),
        scratch_shapes=[pltpu.VMEM((2 * tall, 2 * records), F32)],
        compiler_params=params,
        cost_estimate=cost,
        name="last_departures",
    )(columns, weight, obs, jac, total)


def point_key(tile, column, count, reach):
    me = lax.axis_index("lon")
    right, left = lax.rem(me + 1, count), lax.rem(me + count - 1, count)
    row = lax.div(column, LANES)
    lon = column - row * LANES
    key = jnp.where(tile == me, lon + reach, NOWHERE)
    key = jnp.where((tile == right) & (lon < reach), lon + LANES + reach, key)
    key = jnp.where((tile == left) & (lon >= LANES - reach), lon - LANES + reach, key)
    return jnp.where(key == NOWHERE, NOWHERE, key + row * STRIDE)


def twice(array, features):
    left = features % LANES
    lane = lane_iota(array.shape)
    return jnp.where((lane >= features) & (lane < features + left), pltpu.roll(array, left, 1), array)


def plan_kernel(records, points, reach, capacity, codes_ref, dest_ref, valid_ref, inv_ref, after_ref, chosen_ref, weight_ref, same_ref, info_ref, down, first):
    count = codes_ref.shape[0]
    span, listed = count * records, same_ref.shape[0]
    tile, column = split_codes(codes_ref, records, points)
    key = point_key(tile, column, count, reach)
    for d in range(count):
        down[d * records : (d + 1) * records, :] = jnp.broadcast_to(key[:, d : d + 1], (records, LANES))
    codes = read_codes(codes_ref)
    tile = lax.div(codes, points)
    key = point_key(tile, codes - tile * points, count, reach)
    per = LANES // records
    across = []
    for t in range(span // LANES):
        lane = lane_iota((1, LANES))
        one = key[per * t : per * t + 1, :]
        for h in range(1, per):
            one = jnp.where(
                lane < h * records, one, pltpu.roll(key[per * t + h : per * t + h + 1, :], h * records, 1)
            )
        across.append(one)
    repeats = jnp.zeros((span, LANES), F32)
    for t, one in enumerate(across):
        before = lane_iota((span, LANES)) + t * LANES < row_iota((span, LANES))
        repeats += ((down[...] == one) & before).astype(F32)
    fresh = jnp.sum(repeats, axis=1, keepdims=True) == 0.0
    first[...] = (fresh & (down[...] < NOWHERE)).astype(F32)
    found = jnp.zeros((listed, LANES), jnp.int32)
    for t, one in enumerate(across):
        rank = jnp.sum(jnp.where(down[...] < one, first[...], 0.0), axis=0, keepdims=True)
        rank = jnp.where(one < NOWHERE, rank.astype(jnp.int32), -1)
        same = rank == row_iota((listed, LANES))
        same_ref[:, t * LANES : (t + 1) * LANES] = same.astype(F32).astype(BF16)
        found = jnp.maximum(found, jnp.where(same, one, 0))
    found = jnp.max(found, axis=1, keepdims=True).astype(F32)
    for b in range(listed // LANES):
        wide = jnp.broadcast_to(found[b * LANES : (b + 1) * LANES], (LANES, LANES))
        info_ref[0:1, b * LANES : (b + 1) * LANES] = jnp.transpose(wide)[0:1].astype(jnp.int32)
    starts = jnp.where(down[...] < lane_iota((span, LANES)) * STRIDE, first[...], 0.0)
    info_ref[0:1, listed:] = jnp.sum(starts, axis=0, keepdims=True).astype(jnp.int32)

    dest = to_column(dest_ref[...])
    named = (dest == lane_iota((records, LANES))).astype(F32)
    before = jnp.dot(earlier_rows(records), named.astype(BF16), preferred_element_type=F32)
    rank = jnp.sum(before * named, axis=1, keepdims=True).astype(jnp.int32)
    chosen_ref[...] = (dest * capacity + rank == lane_iota(chosen_ref.shape)).astype(F32).astype(BF16)
    alive = lane_iota(weight_ref.shape) < to_column(valid_ref[...])
    weight_ref[...] = jnp.where(alive, inv_ref[...].astype(F32), 0.0)


def tables_kernel(vertical_ref, lon_ref, lat_ref, after_ref, mixing_ref, table_ref, taps_ref):
    features, levels = vertical_ref.shape
    wide = mixing_ref.shape[2]
    tall = mixing_ref.shape[1]
    variables = features // levels
    mixing_ref[...] = jnp.zeros_like(mixing_ref)
    rows = jnp.concatenate([vertical_ref[...].astype(F32), jnp.zeros((features, wide - levels), F32)], axis=1)
    spread = rows
    for v in range(1, variables):
        spread = jnp.where(row_iota(rows.shape) % variables == v, pltpu.roll(rows, v * levels, 1), spread)
    spread = twice(spread, features)
    mixing_ref[0] = spread[:tall].astype(BF16)
    mixing_ref[1, 0 : features - tall, :] = spread[tall:].astype(BF16)
    taps = lon_ref.shape[0]
    spare = jnp.zeros((taps, wide - features), F32)
    lon = twice(jnp.concatenate([lon_ref[...], spare], axis=1), features)
    lon = jnp.concatenate([lon[k : k + 1] for k in reversed(range(taps))] + [jnp.zeros((16 - taps, wide), F32)], axis=0)
    for b in range(8):
        table_ref[16 * b : 16 * (b + 1), :] = pltpu.roll(lon, b, 0) if b else lon
    taps_ref[...] = twice(jnp.concatenate([lat_ref[...], spare], axis=1), features)


def impact_kernel(records, products_ref, same_ref, near_ref, far_ref, tables_ref, out_ref, terms):
    count, tall, width = products_ref.shape
    listed = same_ref.shape[0]
    lane = lane_iota((tall, width))
    for pair in range(count // 2):
        one = products_ref[2 * pair].astype(F32)
        two = products_ref[2 * pair + 1].astype(F32)
        first = jnp.where(lane < records, one, pltpu.roll(two, records, 1))
        second = jnp.where(lane < records, pltpu.roll(one, records, 1), two)
        terms[0, :, pair * width : (pair + 1) * width] = first.astype(BF16)
        terms[1, :, pair * width : (pair + 1) * width] = second.astype(BF16)
    for h in range(2):
        out_ref[:, h * listed : (h + 1) * listed] = lax.dot_general(
            terms[h], same_ref[...], (((1,), (1,)), ((), ())), preferred_element_type=F32
        ).astype(BF16)


def filter_kernel(block_of, reach, rows, *refs):
    (*lists, vertical_ref, lon_ref, lat_ref, out_ref, mixed, along, mean, ready, sent) = refs
    lists = [(lists[n], lists[n + 1]) for n in range(0, len(lists) // 2 * 2, 2)]
    listed = lists[0][1].shape[1] // vertical_ref.shape[0]
    features = out_ref.shape[0]
    wide = vertical_ref.shape[2]
    height = ready.shape[2]
    window = height + 2 * reach
    pitch = along.shape[0] // window
    step = pl.program_id(0)
    base = block_of(step) * height - reach

    @pl.when(step == 0)
    def _():
        along[...] = jnp.zeros_like(along)
        for n, (info, impact) in enumerate(lists):
            for part in range(0, listed, LANES):

                @pl.when(info[0, listed + rows] > part)
                def _(n=n, impact=impact, part=part):
                    total = 0.0
                    for h in range(vertical_ref.shape[0]):
                        total += lax.dot_general(
                            impact[:, h * listed + part : h * listed + part + LANES],
                            vertical_ref[h],
                            (((0,), (0,)), ((), ())),
                            preferred_element_type=F32,
                        )
                    mixed[n * listed + part : n * listed + part + LANES, :] = total

    steps = ready.shape[0]
    full, left = divmod(features, LANES)
    lane = lane_iota((1, wide)) - full * LANES
    mine = (lane < 0) | ((lane >= step * left) & (lane < (step + 1) * left))
    mine = jnp.where(mine, 1.0, 0.0)
    for n, (info, _) in enumerate(lists):
        offset = -base
        if n:
            side = 1 - 2 * lax.rem(lax.axis_index("lat"), 2)
            offset += (rows if n == 2 else -rows) * side
        low = jnp.clip(-offset, 0, rows)
        high = jnp.clip(window - offset, 0, rows)

        start, stop = info[0, listed + low], info[0, listed + high]

        def add_some(i, carry, info=info, n=n, offset=offset, start=start, stop=stop):
            pieces = []
            for u in range(SOME):
                here = start + i * SOME + u
                live = here < stop
                here = jnp.where(live, here, start)
                key = info[0, here]
                row = lax.shift_right_logical(key, 8) + offset
                place = jnp.bitwise_and(key, STRIDE - 1)
                spot = jnp.bitwise_and(place, 7)
                at = pl.ds(pl.multiple_of(row * pitch + place - spot, 8), 16)
                taps = lon_ref[pl.ds(pl.multiple_of(spot * 16, 16), 16), :]
                column = mixed[pl.ds(n * listed + here, 1), :] * jnp.where(live, mine, 0.0)
                pieces.append((at, taps * column))
            for at, piece in pieces:
                along[at, :] += piece
            return carry

        lax.fori_loop(0, lax.div(stop - start + SOME - 1, SOME), add_some, 0)

    flat = ready.reshape(ready.shape[0] * features * height, LANES)

    def leave(at, t):
        here = pl.ds(t * LANES, min(LANES, features - t * LANES))
        there = pl.ds(pl.multiple_of(block_of(at) * height, height), height)
        return pltpu.make_async_copy(ready.at[at, here], out_ref.at[here, there], sent.at[at, t])

    def smooth(t, again):
        here = slice(t * LANES, (t + 1) * LANES)
        lat = [jnp.broadcast_to(lat_ref[k : k + 1, here], (8, LANES)) for k in range(2 * reach + 1)]
        for j in range(LANES // 8):
            sums = [None] * height
            for w in range(window):
                spot = pl.ds(w * pitch + 8 + j * 8, 8)
                part = along[spot, here]
                if again:
                    along[spot, here] = jnp.zeros_like(part)
                for row in range(max(0, w - 2 * reach), min(height, w + 1)):
                    term = lat[w - row] * part
                    sums[row] = term if sums[row] is None else sums[row] + term
            for row in range(height):
                mean[t % 2, row, j * 8 : (j + 1) * 8, :] = sums[row]

    for t in range(full):
        smooth(t, True)
        for row in range(height):
            flat[pl.ds((step * features + t * LANES) * height + row, LANES, stride=height), :] = jnp.transpose(
                mean[t % 2, row]
            )
        leave(step, t).start()

    @pl.when(step == steps - 1)
    def _():
        smooth(full, False)
        for row in range(height):
            turned = jnp.transpose(mean[full % 2, row])
            for at in range(steps):
                flat[pl.ds((at * features + full * LANES) * height + row, left, stride=height), :] = turned[
                    at * left : (at + 1) * left
                ]
        for at in range(steps):
            leave(at, full).start()
        for at in range(steps):
            for t in range(full + 1):
                leave(at, t).wait()


def solution(mesh):
    lon_devices, lat_devices = mesh.shape["lon"], mesh.shape["lat"]

    def body(state_field, jacobian, observed, inverse_var, valid_count, destination, column, vertical, lon_taps, lat_taps):
        variables, levels, rows, cols = state_field.shape
        features = variables * levels
        records, channels = jacobian.shape[1], jacobian.shape[-1]
        capacity = max(2, 2 * records // lon_devices)
        reach = lon_taps.shape[-1] // 2
        points = rows * cols
        span = records * lon_devices
        tall = pl.cdiv(features, 32) * 16

        told = (lon_devices, 1, records)
        codes = lax.broadcasted_iota(jnp.int32, told, 0) * (NOWHERE // points)
        codes = (codes + jnp.broadcast_to(destination.reshape(1, 1, records), told)) * points
        codes = codes + jnp.broadcast_to(column.reshape(1, 1, records), told)
        codes = lax.all_to_all(codes, "lon", split_axis=0, concat_axis=0, tiled=True)
        codes = codes.reshape(lon_devices, records)
        laid = lay_state(state_field)

        found = gather_state(codes, laid, records, capacity, rows)
        found_in = lax.all_to_all(
            found.reshape(lon_devices, capacity, found.shape[-1]), "lon", split_axis=0, concat_axis=0, tiled=True
        )
        listed = 3 * lon_devices * capacity
        wide = pl.cdiv(features, LANES) * LANES
        taps = lon_taps.shape[-1]
        vmem, anywhere = pl.BlockSpec(memory_space=pltpu.VMEM), pl.BlockSpec(memory_space=pl.ANY)
        chosen, weight, same, info = pl.pallas_call(
            functools.partial(plan_kernel, records, points, reach, capacity),
            in_specs=[vmem] * 4 + [anywhere],
            out_shape=(
                jax.ShapeDtypeStruct((records, lon_devices * capacity), BF16),
                jax.ShapeDtypeStruct((records, channels), F32),
                jax.ShapeDtypeStruct((listed, span), BF16),
                jax.ShapeDtypeStruct((1, listed + LANES), jnp.int32),
            ),
            scratch_shapes=[pltpu.VMEM((span, LANES), jnp.int32), pltpu.VMEM((span, LANES), F32)],
            compiler_params=pltpu.CompilerParams(vmem_limit_bytes=16 * 1024 * 1024),
            cost_estimate=pl.CostEstimate(flops=8 * span * span, bytes_accessed=span * listed * 2, transcendentals=0),
            name="plan_points",
        )(
            codes,
            destination.reshape(1, records),
            valid_count.reshape(1, records),
            inverse_var.reshape(records, channels),
            found,
        )
        own = jnp.swapaxes(jacobian.reshape(records, variables, levels, channels), 1, 2).reshape(-1, channels)
        products = departures(
            chosen,
            found_in.reshape(lon_devices * capacity, found.shape[-1]),
            weight,
            observed.reshape(records, channels),
            own,
            info,
            lon_devices,
            tall,
        )
        products_in = lax.all_to_all(products, "lon", split_axis=0, concat_axis=0, tiled=True)

        mixing, lon_table, lat_flat = pl.pallas_call(
            tables_kernel,
            in_specs=[vmem] * 3 + [anywhere],
            out_shape=(
                jax.ShapeDtypeStruct((2, tall, wide), BF16),
                jax.ShapeDtypeStruct((8 * 16, wide), F32),
                jax.ShapeDtypeStruct((taps, wide), F32),
            ),
            compiler_params=pltpu.CompilerParams(vmem_limit_bytes=16 * 1024 * 1024),
            cost_estimate=pl.CostEstimate(flops=0, bytes_accessed=4 * features * wide, transcendentals=0),
            name="tables",
        )(
            jnp.swapaxes(vertical, 0, 1).reshape(features, levels),
            jnp.moveaxis(lon_taps, 2, 0).reshape(taps, features),
            jnp.moveaxis(lat_taps, 2, 0).reshape(taps, features),
            products,
        )
        pairs = [(i, i + 1) for i in range(0, lat_devices - 1, 2)]
        between = [(i, i + 1) for i in range(1, lat_devices - 1, 2)]
        swaps = [[(a, b) for a, b in some] + [(b, a) for a, b in some] for some in (pairs, between)]
        info_near = lax.ppermute(info, "lat", swaps[0])
        info_far = lax.ppermute(info, "lat", swaps[1])

        impact = pl.pallas_call(
            functools.partial(impact_kernel, records),
            in_specs=[vmem] * 2 + [anywhere] * 3,
            out_shape=jax.ShapeDtypeStruct((tall, 2 * listed), BF16),
            scratch_shapes=[pltpu.VMEM((2, tall, span), BF16)],
            compiler_params=pltpu.CompilerParams(vmem_limit_bytes=16 * 1024 * 1024),
            name="impact_columns",
        )(products_in, same, info_near, info_far, mixing)
        impact_near = lax.ppermute(impact, "lat", swaps[0])
        impact_far = lax.ppermute(impact, "lat", swaps[1])

        height = 8
        blocks = rows // height
        pitch = LANES + 16

        def filtered(lists, steps, block_of, before, name):
            held = [pl.BlockSpec(memory_space=pltpu.SMEM), pl.BlockSpec(memory_space=pltpu.VMEM)] * (len(lists) // 2)
            held += [pl.BlockSpec(memory_space=pltpu.VMEM)] * 3
            given = list(lists) + [mixing, lon_table, lat_flat]
            kernel = functools.partial(filter_kernel, block_of, reach, rows)
            if before is not None:
                given.append(before)
                held.append(pl.BlockSpec(memory_space=pl.ANY))
                at = len(lists) + 3
                inner = kernel
                kernel = lambda *refs: inner(*refs[:at], *refs[at + 1 :])
            return pl.pallas_call(
                kernel,
                grid=(steps,),
                in_specs=held,
                out_specs=pl.BlockSpec(memory_space=pl.ANY),
                out_shape=jax.ShapeDtypeStruct((features, rows, cols), F32),
                scratch_shapes=[
                    pltpu.VMEM((len(lists) // 2 * listed, wide), F32),
                    pltpu.VMEM(((height + 2 * reach) * pitch, wide), F32),
                    pltpu.VMEM((2, height, cols, LANES), F32),
                    pltpu.VMEM((steps, features, height, cols), F32),
                    pltpu.SemaphoreType.DMA((steps, wide // LANES)),
                ],
                input_output_aliases={} if before is None else {len(given) - 1: 0},
                compiler_params=pltpu.CompilerParams(vmem_limit_bytes=24 * 1024 * 1024),
                cost_estimate=pl.CostEstimate(
                    flops=40 * features * rows * cols, bytes_accessed=features * rows * cols * 2, transcendentals=0
                ),
                name=name,
            )(*given)

        inner = filtered([info, impact], blocks - 2, lambda s: s + 1, None, "inner_rows")
        result = filtered(
            [info, impact, info_far, impact_far, info_near, impact_near],
            2,
            lambda s: s * (blocks - 1),
            inner,
            "outer_rows",
        )
        return result.reshape(variables, levels, rows, cols)

    placed = (
        P(None, None, "lat", "lon"),
        P("lat", "lon", None, None, None),
        P("lat", "lon", None),
        P("lat", "lon", None),
        P("lat", "lon"),
        P("lat", "lon", None),
        P("lat", "lon"),
        P(),
        P(),
        P(),
    )
    return jax.shard_map(
        body, mesh=mesh, in_specs=placed, out_specs=P(None, None, "lat", "lon"), check_vma=False
    )
```
